128 devices in a mesh: bx: 16 (over z, x), by: 8 (over y, core).
Axes of the slice: x: 4, y: 4, z: 4, core: 2. Of those that a mesh axis runs over, the one named last changes fastest.
Arguments:
- coefficients: float32 [2, 6, 1024, 6, 1024], P(None, None, 'bx', None, 'by'), may hold values from -0.4 to 0.4
- slowness: float32 [4, 96, 96], replicated, may hold values from 0.25 to 1
Outputs:
- transformed: float32 [2, 6, 1024, 6, 1024], P(None, None, 'bx', None, 'by')
The draws below stay inside these ranges and needn't reach their ends.
All inputs are finite; a program needn't handle non-finite values.
Results may differ from the reference program's by a relative error of at most 0.00095.
Values sent between devices are 32-bit elements; how exact they have to be, the bound alone decides.
A program may use at most 192 MiB of HBM per device.

```python
import math
import jax
import jax.numpy as jnp
import numpy as np
from jax import lax

N = 2048
CHEB = 6
LEVELS = 4
S1 = 1024
S2 = 1024
TABLE = 96


def steps_of(stream_key, shape, shards, low, high):
    loudness, own = 1.0, jax.random.fold_in(stream_key, 6)
    for axis_at, blocks in shards:
        steps = jnp.exp(jax.random.uniform(jax.random.fold_in(own, axis_at), (blocks,), jnp.float32, low / len(shards), high / len(shards)))
        loudness = loudness * jnp.repeat(steps, shape[axis_at] // blocks).reshape([-1 if axis == axis_at else 1 for axis in range(len(shape))])
    return loudness


def centred(key, shape, width, bound, shards=(), held_as=jnp.bfloat16):
    entries = width * jax.random.normal(key, shape, jnp.float32)
    if shards:
        entries = entries * steps_of(key, shape, shards, -0.22, 0.18)
    return jnp.clip(entries, -bound, bound).astype(held_as)


def setup_inputs(seed: int = 0) -> dict:
    arg_keys = jax.random.split(jax.random.key(seed), 3)
    return {
        "coefficients": centred(arg_keys[0], (2, CHEB, S1, CHEB, S2), 0.0625, 0.4, ((2, 16), (4, 8)), jnp.float32),
        "slowness": jnp.clip(jax.random.uniform(arg_keys[1], (LEVELS, TABLE, TABLE), jnp.float32, 0.25, 1.0), 0.25, 1.0),
    }


def cheb_points_of(order_count):
    return np.cos(np.pi * (2 * np.arange(order_count) + 1) / (2 * order_count))

def lagrange_table(order_count):
    cheb_points = cheb_points_of(order_count)
    weights = np.zeros((2, order_count, order_count))
    for quadrant in range(2):
        shifted = quadrant - 0.5 + cheb_points / 2
        for target in range(order_count):
            for source in range(order_count):
                product = 1.0
                for others in range(order_count):
                    if others != source:
                        product = product * (shifted[target] - cheb_points[others]) / (cheb_points[source] - cheb_points[others])
                weights[quadrant, target, source] = product
    return weights

def row_terms(row_ids, total_bits, level_index, grid_size, order_count):
    shift_bits = total_bits - level_index
    parent_box = row_ids >> shift_bits
    child_bit = row_ids >> shift_bits - 1 & 1
    source_box = jnp.zeros_like(row_ids)
    for offset in range(shift_bits):
        source_box = source_box + (row_ids >> shift_bits - 1 - offset & 1) * (1 << offset)
    box_width = grid_size * 2.0 ** level_index / 2.0 ** total_bits
    child_freq = (source_box.astype(jnp.float32) + 0.5) * box_width - grid_size / 2.0
    parent_freq = child_freq - (child_bit.astype(jnp.float32) - 0.5) * box_width
    cheb_points = jnp.asarray(cheb_points_of(order_count), jnp.float32)
    quadrants = jnp.arange(2, dtype=jnp.int32)
    target_box = 2 * parent_box[None, :] + quadrants[:, None]
    position = (target_box[:, None, :].astype(jnp.float32) + (1.0 + cheb_points)[None, :, None] / 2.0) / 2.0 ** (level_index + 1)
    lookup = order_count * target_box[:, None, :] + jnp.arange(order_count, dtype=jnp.int32)[None, :, None]
    return (position, child_freq, parent_freq, lookup)

def reference(coefficients, slowness):
    highest = lax.Precision.HIGHEST
    lagrange = jnp.asarray(lagrange_table(CHEB), jnp.float32)
    total_x = S1.bit_length() - 1
    total_y = S2.bit_length() - 1
    rows_x = jnp.arange(S1, dtype=jnp.int32)
    rows_y = jnp.arange(S2, dtype=jnp.int32)
    current = coefficients
    for level_index in range(LEVELS):
        table_now = slowness[level_index]
        pos_x, child_x, parent_x, look_x = row_terms(rows_x, total_x, level_index, N, CHEB)
        pos_y, child_y, parent_y, look_y = row_terms(rows_y, total_y, level_index, N, CHEB)
        step_x = child_x - parent_x
        step_y = child_y - parent_y
        magnitude = jnp.sqrt(child_x[:, None] ** 2 + child_y[None, :] ** 2) - jnp.sqrt(parent_x[:, None] ** 2 + parent_y[None, :] ** 2)
        high_part = 2 ** level_index
        low_x = S1 // (2 * high_part)
        low_y = S2 // (2 * high_part)
        pieces_x = []
        for quad_x in range(2):
            pieces_y = []
            for quad_y in range(2):
                interp = jnp.einsum('ts,zsaub->ztaub', lagrange[quad_x], current, precision=highest)
                interp = jnp.einsum('uv,ztavb->ztaub', lagrange[quad_y], interp, precision=highest)
                speed_vals = table_now[look_x[quad_x][:, :, None, None], look_y[quad_y][None, None, :, :]]
                angles = pos_x[quad_x][:, :, None, None] * step_x[None, :, None, None] + pos_y[quad_y][None, None, :, :] * step_y[None, None, None, :] + speed_vals * magnitude[None, :, None, :]
                angles = 2.0 * math.pi * angles
                cosine = jnp.cos(angles)
                sine_part = jnp.sin(angles)
                real_part = cosine * interp[0] - sine_part * interp[1]
                imag_part = cosine * interp[1] + sine_part * interp[0]
                summed = jnp.stack([real_part, imag_part])
                summed = summed.reshape(2, CHEB, high_part, 2, low_x, CHEB, high_part, 2, low_y).sum(axis=(3, 7))
                pieces_y.append(summed)
            pieces_x.append(jnp.stack(pieces_y, axis=6))
        current = jnp.stack(pieces_x, axis=3).reshape(2, CHEB, S1, CHEB, S2)
    return current
```

```python
import functools

import jax
import jax.numpy as jnp
import ml_dtypes
import numpy as np
from jax import lax
from jax.experimental import pallas as pl
from jax.experimental.pallas import tpu as pltpu
from jax.sharding import PartitionSpec as P

N = 2048
CHEB = 6
HALF = CHEB * CHEB
ROWS = 2 * HALF
TERMS = 4 * HALF
PAD = 80
LANES = 128
MESH = pl.DeviceIdType.MESH


def cheb_points():
    return np.cos(np.pi * (2 * np.arange(CHEB) + 1) / (2 * CHEB))


def lagrange_table():
    points = cheb_points()
    weights = np.zeros((2, CHEB, CHEB))
    for quadrant in range(2):
        shifted = quadrant - 0.5 + points / 2
        for target in range(CHEB):
            for source in range(CHEB):
                product = 1.0
                for other in range(CHEB):
                    if other != source:
                        product = (
                            product
                            * (shifted[target] - points[other])
                            / (points[source] - points[other])
                        )
                weights[quadrant, target, source] = product
    return weights


def turns_table():
    return np.arange(2)[:, None] + (1.0 + cheb_points())[None, :] / 2.0


def split16(values):
    high = values.astype(ml_dtypes.bfloat16)
    low = (values - high.astype(np.float64)).astype(ml_dtypes.bfloat16)
    return high, low


def mixing_tables():
    weights = lagrange_table()
    turns = turns_table()
    tables = []
    for c1, c2 in ((0, 0), (0, 1), (1, 0), (1, 1), (0, None), (1, None)):
        phase1 = np.exp(2j * np.pi * (c1 - 0.5) * turns)
        phase2 = np.exp(2j * np.pi * (0 if c2 is None else c2 - 0.5) * turns)
        w1 = weights * phase1[:, :, None]
        w2 = weights * phase2[:, :, None]
        full = np.einsum("qts,puv->qptusv", w1, w2).reshape(TERMS, HALF)
        real = np.block([[full.real, -full.imag], [full.imag, full.real]])
        high, low = split16(real)
        table = np.zeros((2 * TERMS, 3 * PAD), ml_dtypes.bfloat16)
        table[:, 0:ROWS] = high
        table[:, PAD : PAD + ROWS] = high
        table[:, 2 * PAD : 2 * PAD + ROWS] = low
        tables.append(table)
    return np.stack(tables)


def row_tables():
    q1, q2, t1, t2 = [
        axis.reshape(-1) for axis in np.meshgrid(*[np.arange(n) for n in (2, 2, CHEB, CHEB)], indexing="ij")
    ]
    rows = np.stack([CHEB * q1 + t1, CHEB * q2 + t2, turns_table()[q2, t2]])
    return np.broadcast_to(rows[:, :, None], (3, TERMS, LANES)).astype(np.float32)


def fit(function, degree):
    count = 200
    s = 0.125 * (1 + np.cos(np.pi * (2 * np.arange(count) + 1) / (2 * count)))
    series = np.polynomial.chebyshev.Chebyshev.fit(s, function(np.sqrt(s)), degree, domain=[0, 0.25])
    return [float(c) for c in series.convert(kind=np.polynomial.Polynomial).coef]


SIN = fit(lambda r: np.sin(2 * np.pi * r) / r, 5)
COS = fit(lambda r: np.cos(2 * np.pi * r), 5)


def horner(coefficients, s):
    value = s * coefficients[-1] + coefficients[-2]
    for coefficient in coefficients[-3::-1]:
        value = value * s + coefficient
    return value


def unit(turns):
    r = turns - jnp.round(turns)
    s = r * r
    return horner(COS, s), horner(SIN, s) * r


def operand(block):
    block = jnp.concatenate([block, jnp.zeros((PAD - ROWS, block.shape[1]), jnp.float32)], axis=0)
    high = block.astype(jnp.bfloat16)
    low = (block - high.astype(jnp.float32)).astype(jnp.bfloat16)
    return jnp.concatenate([high, low, high], axis=0)


def reverse6(value):
    total = 0
    for bit in range(6):
        total = total + lax.rem(lax.div(value, 1 << bit), 2) * (1 << (5 - bit))
    return total


def kernel(
    coef_ref, slow_ref, mix_ref, rows_ref, out_ref,
    sbuf, xin, s0, z1, zr, s2, obuf, orecv, vtab, lane_ref, m_ref, y_ref, acc_ref,
    in_send, in_recv, sib_send, sib_recv, out_send, out_recv,
):
    bx, by = lax.axis_index("bx"), lax.axis_index("by")
    my_z, my_x = lax.div(bx, 4), lax.rem(bx, 4)
    my_y, core = lax.div(by, 2), lax.rem(by, 2)
    chip = bx * 4 + my_y
    low1 = reverse6(chip) * 16

    for ell in range(64):
        for tile in range(9):
            sbuf[ell, 8 * tile : 8 * tile + 8, :] = coef_ref[pl.ds(tile * 512 + ell, 8, stride=64), :]

    local_in = pltpu.make_async_copy(sbuf.at[chip], xin.at[0, my_z, my_y], in_recv.at[0])
    local_in.start()

    def send_in(step, carry):
        hop_x = lax.div(step, 16)
        dx = hop_x + lax.div(hop_x, 2) * (1 - 2 * lax.rem(hop_x, 2))
        dz, dy = lax.div(lax.rem(step, 16), 4), lax.rem(step, 4)
        to_x, to_z, to_y = lax.rem(my_x + dx, 4), lax.rem(my_z + dz, 4), lax.rem(my_y + dy, 4)
        pltpu.make_async_remote_copy(
            src_ref=sbuf.at[to_z * 16 + to_x * 4 + to_y],
            dst_ref=xin.at[dx, my_z, my_y],
            send_sem=in_send,
            recv_sem=in_recv.at[dx],
            device_id=(to_z * 4 + to_x, to_y * 2 + core),
            device_id_type=MESH,
        ).start()
        return carry

    lax.fori_loop(1, 64, send_in, 0)

    lane = lax.broadcasted_iota(jnp.int32, (TERMS, 96), 1).astype(jnp.float32)
    row_i = rows_ref[0, :, 0:96]
    row_j = rows_ref[1, :, 0:96]

    def spread(level, a1):
        pick = jnp.where(row_i + (12 * a1).astype(jnp.float32) == lane, 1.0, 0.0)
        return jnp.dot(pick, slow_ref[level], precision=lax.Precision.HIGHEST, preferred_element_type=jnp.float32)

    def place(slot, spreaded, a2):
        picked = jnp.where(row_j + (12 * a2).astype(jnp.float32) == lane, spreaded, 0.0)
        column = jnp.sum(picked, axis=1, keepdims=True)
        vtab[slot] = jnp.broadcast_to(column, (TERMS, LANES))

    zero = jnp.int32(0)
    place(0, spread(0, zero), zero)

    def fill1(a1, carry):
        table = spread(1, a1)
        for a2 in range(2):
            place(1 + 2 * a1 + a2, table, jnp.int32(a2))
        return carry

    lax.fori_loop(0, 2, fill1, 0)

    def fill2(z, carry):
        table = spread(2, z)
        for y1 in range(2):
            place(5 + 2 * z + y1, table, 2 * y1 + core)
        return carry

    lax.fori_loop(0, 4, fill2, 0)

    def fill3(a1, carry):
        table = spread(3, a1)
        for y1 in range(2):
            for c in range(2):
                place(13 + 4 * a1 + 2 * y1 + c, table, 2 * (2 * y1 + core) + c)
        return carry

    lax.fori_loop(0, 8, fill3, 0)

    lanes = lax.broadcasted_iota(jnp.int32, (8, LANES), 1)
    bit3 = lanes // 64
    lane_ref[...] = bit3 * 8 + reverse6(lanes % 64) * 16

    def magnitude(level, r1, c1, r2, c2):
        width = 2.0 ** (level + 1)
        k = (lax.div(r1, 1 << level).astype(jnp.float32) + 0.5) * width - N / 2
        step = (c1.astype(jnp.float32) - 0.5) * width
        k0 = k - step
        k2 = (lax.shift_right_logical(r2, jnp.full(r2.shape, level, jnp.int32)).astype(jnp.float32) + 0.5) * width - N / 2
        step2 = (c2.astype(jnp.float32) - 0.5) * width
        k20 = k2 - step2
        above = step * (k + k0) + step2 * (k2 + k20)
        return above / (jnp.sqrt(k * k + k2 * k2) + jnp.sqrt(k0 * k0 + k20 * k20))

    def combine(count, slots, shift):
        def tile(i, carry):
            at = pl.ds(pl.multiple_of(8 * i, 8), 8)
            at_im = pl.ds(pl.multiple_of(8 * i + TERMS, 8), 8)
            for side in range(2):
                cols = pl.ds(side * LANES, LANES)
                v = vtab[slots[side], at, :]
                total_re = total_im = None
                for c in range(count):
                    turns = v * m_ref[c, side]
                    if shift is not None:
                        turns = turns + rows_ref[2, at, :] * shift
                    co, si = unit(turns)
                    y_re, y_im = y_ref[c, at, cols], y_ref[c, at_im, cols]
                    re = co * y_re - si * y_im
                    im = co * y_im + si * y_re
                    total_re = re if total_re is None else total_re + re
                    total_im = im if total_im is None else total_im + im
                acc_ref[at, cols] = total_re
                acc_ref[at_im, cols] = total_im
            return carry

        lax.fori_loop(0, TERMS // 8, tile, 0)

    def fold(side, q1, q2, put):
        cols = pl.ds(side * LANES, LANES)
        base = q1 * ROWS + q2 * HALF
        put(pl.ds(0, HALF), acc_ref[base : base + HALF, cols])
        put(pl.ds(HALF, HALF), acc_ref[TERMS + base : TERMS + base + HALF, cols])

    one = jnp.int32(1)

    def chunk(step, carry):
        dx = step + lax.div(step, 2) * (1 - 2 * lax.rem(step, 2))
        x = lax.rem(my_x - dx + 4, 4)
        x1, x0 = lax.div(x, 2), lax.rem(x, 2)
        high1 = low1 + 4 * x1 + 8 * x0
        pltpu.make_async_copy(xin.at[dx], xin.at[dx], in_recv.at[dx]).wait()

        def level0(z0, carry):
            for c1 in range(2):
                for c2 in range(2):
                    child = 2 * c1 + c2
                    blocks = []
                    for y0 in range(2):
                        blocks.append(xin[dx, 2 * c1 + z0, 2 * c2 + y0])
                        r1 = high1 + c1 + 2 * z0
                        r2 = lane_ref[...] + (c2 + 2 * y0 + 4 * core)
                        m_ref[child, y0] = magnitude(0, r1, c1 * one, r2, c2 * one)
                    y_ref[child] = jnp.dot(
                        mix_ref[child], operand(jnp.concatenate(blocks, axis=1)), preferred_element_type=jnp.float32
                    )
            combine(4, (0, 0), None)
            for y0 in range(2):
                for q1 in range(2):
                    for q2 in range(2):

                        def put(rows, values, q1=q1, q2=q2, y0=y0):
                            s0[2 * q1 + z0, 2 * q2 + y0, rows, :] = values

                        fold(y0, q1, q2, put)
            return carry

        lax.fori_loop(0, 2, level0, 0)

        def level1(a1, carry):
            for c1 in range(2):
                for c2 in range(2):
                    child = 2 * c1 + c2
                    blocks = []
                    for a2 in range(2):
                        blocks.append(s0[2 * a1 + c1, 2 * a2 + c2])
                        r1 = high1 + 2 * c1
                        r2 = lane_ref[...] + (2 * c2 + 4 * core)
                        m_ref[child, a2] = magnitude(1, r1, c1 * one, r2, c2 * one)
                    y_ref[child] = jnp.dot(
                        mix_ref[child], operand(jnp.concatenate(blocks, axis=1)), preferred_element_type=jnp.float32
                    )
            combine(4, (1 + 2 * a1, 2 + 2 * a1), None)
            for a2 in range(2):
                for q1 in range(2):
                    for q2 in range(2):

                        def put(rows, values, q1=q1, q2=q2, a2=a2):
                            z1[x, q2, 2 * a1 + q1, a2, rows, :] = values

                        fold(a2, q1, q2, put)
            return carry

        lax.fori_loop(0, 2, level1, 0)
        pltpu.make_async_remote_copy(
            src_ref=z1.at[x, 1 - core],
            dst_ref=zr.at[x],
            send_sem=sib_send.at[dx],
            recv_sem=sib_recv.at[dx],
            device_id=(bx, my_y * 2 + 1 - core),
            device_id_type=MESH,
        ).start()
        return carry

    lax.fori_loop(0, 4, chunk, 0)

    def sibling(dx, carry):
        pltpu.make_async_copy(zr.at[0], zr.at[0], sib_recv.at[dx]).wait()
        pltpu.make_async_copy(zr.at[0], zr.at[0], sib_send.at[dx]).wait()
        return carry

    lax.fori_loop(0, 4, sibling, 0)

    def target(step, carry):
        z = lax.rem(my_z + lax.div(step, 2) + 2, 4)
        y1 = lax.rem(lax.div(my_y, 2) + lax.rem(step, 2), 2)
        y = 2 * y1 + core
        for c1 in range(2):
            for other in range(2):
                child = 2 * c1 + other
                c2 = core + other * (1 - 2 * core)
                blocks = []
                for x0 in range(2):
                    x = 2 * c1 + x0
                    blocks.append(zr[x, z, y1] if other else z1[x, core, z, y1])
                    r1 = low1 + 4 * c1 + 8 * x0
                    r2 = lane_ref[...] + 4 * c2
                    m_ref[child, x0] = magnitude(2, r1, c1 * one, r2, c2)
                y_ref[child] = jnp.dot(
                    mix_ref[2 * c1 + c2], operand(jnp.concatenate(blocks, axis=1)), preferred_element_type=jnp.float32
                )
        slot = 5 + 2 * z + y1
        combine(4, (slot, slot), None)
        for x0 in range(2):
            for q1 in range(2):
                for q2 in range(2):

                    def put(rows, values, q1=q1, q2=q2, x0=x0):
                        s2[q1, q2, x0, rows, :] = values

                    fold(x0, q1, q2, put)

        def level3(x1, carry):
            for c1 in range(2):
                blocks = []
                for c in range(2):
                    blocks.append(s2[x1, c, c1])
                    r1 = low1 + 8 * c1
                    m_ref[c1, c] = magnitude(3, r1, c1 * one, lane_ref[...], bit3)
                y_ref[c1] = jnp.dot(
                    mix_ref[4 + c1], operand(jnp.concatenate(blocks, axis=1)), preferred_element_type=jnp.float32
                )
            slot = 13 + 4 * (2 * z + x1) + 2 * y1
            combine(2, (slot, slot + 1), bit3.astype(jnp.float32) - 0.5)
            left = lax.broadcasted_iota(jnp.int32, (HALF, LANES), 1) < 64
            for c in range(2):
                cols = pl.ds(c * LANES, LANES)
                for q1 in range(2):
                    for part in range(2):
                        base = part * TERMS + q1 * ROWS
                        first = acc_ref[base : base + HALF, cols]
                        second = acc_ref[base + HALF : base + ROWS, cols]
                        kept = jnp.where(left, first, second)
                        moved = jnp.where(left, second, first)
                        obuf[2 * step + x1, q1, c, HALF * part : HALF * part + HALF, :] = kept + pltpu.roll(moved, 64, 1)
            for q1 in range(2):
                for c in range(2):
                    to_bx = z * 4 + 2 * x1 + q1
                    to_by = 2 * y + c
                    src = obuf.at[2 * step + x1, q1, c]
                    dst = orecv.at[chip]
                    here = jnp.logical_and(to_bx == bx, to_by == by)

                    @pl.when(here)
                    def _(src=src, dst=dst):
                        pltpu.make_async_copy(src, dst, out_recv).start()

                    @pl.when(jnp.logical_not(here))
                    def _(src=src, dst=dst, to_bx=to_bx, to_by=to_by):
                        pltpu.make_async_remote_copy(
                            src_ref=src, dst_ref=dst, send_sem=out_send, recv_sem=out_recv,
                            device_id=(to_bx, to_by), device_id_type=MESH,
                        ).start()

            return carry

        lax.fori_loop(0, 2, level3, 0)
        return carry

    lax.fori_loop(0, 8, target, 0)

    pltpu.make_async_copy(sbuf.at[pl.ds(0, 63)], sbuf.at[pl.ds(0, 63)], in_send).wait()
    kept_here = lax.rem(my_y, 2) == core

    @pl.when(kept_here)
    def _():
        pltpu.make_async_copy(orecv.at[pl.ds(0, 63)], orecv.at[pl.ds(0, 63)], out_send).wait()

    @pl.when(jnp.logical_not(kept_here))
    def _():
        pltpu.make_async_copy(orecv, orecv, out_send).wait()

    pltpu.make_async_copy(orecv, orecv, out_recv).wait()
    for ell in range(64):
        for tile in range(9):
            out_ref[pl.ds(tile * 512 + ell, 8, stride=64), :] = orecv[ell, 8 * tile : 8 * tile + 8, :]


def shards(coefficients, slowness):
    rows = jnp.transpose(coefficients, (0, 1, 3, 2, 4)).reshape(ROWS * 64, LANES)
    block = (ROWS, LANES)
    scratch = [
        pltpu.VMEM((64,) + block, jnp.float32),
        pltpu.VMEM((4, 4, 4) + block, jnp.float32),
        pltpu.VMEM((4, 4) + block, jnp.float32),
        pltpu.VMEM((4, 2, 4, 2) + block, jnp.float32),
        pltpu.VMEM((4, 4, 2) + block, jnp.float32),
        pltpu.VMEM((2, 2, 2) + block, jnp.float32),
        pltpu.VMEM((16, 2, 2) + block, jnp.float32),
        pltpu.VMEM((64,) + block, jnp.float32),
        pltpu.VMEM((45, TERMS, LANES), jnp.float32),
        pltpu.VMEM((8, LANES), jnp.int32),
        pltpu.VMEM((4, 2, 8, LANES), jnp.float32),
        pltpu.VMEM((4, 2 * TERMS, 2 * LANES), jnp.float32),
        pltpu.VMEM((2 * TERMS, 2 * LANES), jnp.float32),
        pltpu.SemaphoreType.DMA,
        pltpu.SemaphoreType.DMA((4,)),
        pltpu.SemaphoreType.DMA((4,)),
        pltpu.SemaphoreType.DMA((4,)),
        pltpu.SemaphoreType.DMA,
        pltpu.SemaphoreType.DMA,
    ]
    vmem = pl.BlockSpec(memory_space=pltpu.VMEM)
    out = pl.pallas_call(
        kernel,
        out_shape=jax.ShapeDtypeStruct((ROWS * 64, LANES), jnp.float32),
        in_specs=[vmem] * 4,
        out_specs=vmem,
        scratch_shapes=scratch,
        compiler_params=pltpu.CompilerParams(has_side_effects=True, vmem_limit_bytes=50 << 20),
    )(rows, slowness, jnp.asarray(mixing_tables()), jnp.asarray(row_tables()))
    return jnp.transpose(out.reshape(2, CHEB, CHEB, 64, LANES), (0, 1, 3, 2, 4))


def solution(mesh):
    placed = (P(None, None, "bx", None, "by"), P())
    return jax.shard_map(
        shards,
        mesh=mesh,
        in_specs=placed,
        out_specs=P(None, None, "bx", None, "by"),
        check_vma=False,
    )
```

```python
import functools

import jax
import jax.numpy as jnp
import ml_dtypes
import numpy as np
from jax import lax
from jax.experimental import pallas as pl
from jax.experimental.pallas import tpu as pltpu
from jax.sharding import PartitionSpec as P

N = 2048
CHEB = 6
HALF = CHEB * CHEB
ROWS = 2 * HALF
TERMS = 4 * HALF
PAD = 80
LANES = 128
MESH = pl.DeviceIdType.MESH


def cheb_points():
    return np.cos(np.pi * (2 * np.arange(CHEB) + 1) / (2 * CHEB))


def lagrange_table():
    points = cheb_points()
    weights = np.zeros((2, CHEB, CHEB))
    for quadrant in range(2):
        shifted = quadrant - 0.5 + points / 2
        for target in range(CHEB):
            for source in range(CHEB):
                product = 1.0
                for other in range(CHEB):
                    if other != source:
                        product = (
                            product
                            * (shifted[target] - points[other])
                            / (points[source] - points[other])
                        )
                weights[quadrant, target, source] = product
    return weights


def turns_table():
    return np.arange(2)[:, None] + (1.0 + cheb_points())[None, :] / 2.0


def split16(values):
    high = values.astype(ml_dtypes.bfloat16)
    low = (values - high.astype(np.float64)).astype(ml_dtypes.bfloat16)
    return high, low


def mixing_tables():
    weights = lagrange_table()
    turns = turns_table()
    tables = []
    for parts in ((0, HALF), (0, 40), (4, 44)):
        for c1, c2 in ((0, 0), (0, 1), (1, 0), (1, 1)):
            w1 = weights * np.exp(2j * np.pi * (c1 - 0.5) * turns)[:, :, None]
            w2 = weights * np.exp(2j * np.pi * (c2 - 0.5) * turns)[:, :, None]
            full = np.einsum("qts,puv->qptusv", w1, w2).reshape(TERMS, HALF)
            real = np.zeros((2 * TERMS, PAD))
            real[:, parts[0] : parts[0] + HALF] = np.concatenate([full.real, full.imag])
            real[:, parts[1] : parts[1] + HALF] = np.concatenate([-full.imag, full.real])
            high, low = split16(real)
            tables.append(np.concatenate([high, high, low], axis=1))
    return np.stack(tables)


def row_tables():
    q1, q2, t1, t2 = [
        axis.reshape(-1) for axis in np.meshgrid(*[np.arange(n) for n in (2, 2, CHEB, CHEB)], indexing="ij")
    ]
    rows = np.stack([CHEB * q1 + t1, CHEB * q2 + t2])
    return np.broadcast_to(rows[:, :, None], (2, TERMS, LANES)).astype(np.float32)


def fit(function, degree):
    count = 200
    s = 0.125 * (1 + np.cos(np.pi * (2 * np.arange(count) + 1) / (2 * count)))
    series = np.polynomial.chebyshev.Chebyshev.fit(s, function(np.sqrt(s)), degree, domain=[0, 0.25])
    return [float(c) for c in series.convert(kind=np.polynomial.Polynomial).coef]


SIN = fit(lambda r: np.sin(2 * np.pi * r) / r, 5)
COS = fit(lambda r: np.cos(2 * np.pi * r), 5)


def horner(coefficients, s):
    value = s * coefficients[-1] + coefficients[-2]
    for coefficient in coefficients[-3::-1]:
        value = value * s + coefficient
    return value


def unit(turns):
    r = turns - jnp.round(turns)
    s = r * r
    return horner(COS, s), horner(SIN, s) * r


def operand(block):
    if block.shape[0] < PAD:
        block = jnp.concatenate([block, jnp.zeros((PAD - block.shape[0], block.shape[1]), jnp.float32)], axis=0)
    high = block.astype(jnp.bfloat16)
    low = (block - high.astype(jnp.float32)).astype(jnp.bfloat16)
    return jnp.concatenate([high, low, high], axis=0)


def reverse6(value):
    total = 0
    for bit in range(6):
        total = total + lax.rem(lax.div(value, 1 << bit), 2) * (1 << (5 - bit))
    return total


def kernel(
    coef_hbm, slow_hbm, mix_hbm, rows_hbm, out_ref,
    coef_ref, slow_ref, mix_ref, rows_ref,
    sbuf, xin, s0, z1, zr, s2, obuf, orecv, vtab, e_tab, y_a, y_b, acc_a, acc_b,
    load, in_send, in_recv, sib_send, sib_recv, out_send, out_recv,
):
    bx, by = lax.axis_index("bx"), lax.axis_index("by")
    my_z, my_x = lax.div(bx, 4), lax.rem(bx, 4)
    my_y, core = lax.div(by, 2), lax.rem(by, 2)
    my_x0 = lax.rem(my_x, 2)
    chip = bx * 4 + my_y
    low1 = reverse6(chip) * 16

    loads = [
        pltpu.make_async_copy(src, dst, load.at[i])
        for i, (src, dst) in enumerate(
            ((coef_hbm, coef_ref), (slow_hbm, slow_ref), (rows_hbm, rows_ref), (mix_hbm, mix_ref))
        )
    ]
    for copy in loads:
        copy.start()
    loads[0].wait()

    def send_in(step, carry):
        part, inner = lax.div(step, 16), lax.rem(step, 16)
        pz, py = lax.div(part, 2), lax.rem(lax.rem(part, 2) + core, 2)
        other = lax.div(inner, 4)
        dx = lax.rem(lax.rem(inner, 4) + other, 4)
        dz, dy = 2 * lax.div(other, 2) + pz, 2 * lax.rem(other, 2) + py
        sign = 1 - 2 * core
        dx, dz, dy = [lax.rem(4 + sign * d, 4) for d in (dx, dz, dy)]
        to_x, to_z, to_y = lax.rem(my_x + dx, 4), lax.rem(my_z + dz, 4), lax.rem(my_y + dy, 4)
        to_bx, to_by = to_z * 4 + to_x, to_y * 2 + my_x0
        ell = to_z * 16 + to_x * 4 + to_y
        for tile in range(9):
            sbuf[ell, 8 * tile : 8 * tile + 8, :] = coef_ref[pl.ds(tile * 512 + ell, 8, stride=64), :]
        src = sbuf.at[ell]
        dst = xin.at[lax.div(dx, 2), core, my_z, my_y]
        here = jnp.logical_and(to_bx == bx, to_by == by)

        @pl.when(here)
        def _():
            pltpu.make_async_copy(src, dst, in_recv.at[part]).start()

        @pl.when(jnp.logical_not(here))
        def _():
            pltpu.make_async_remote_copy(
                src_ref=src, dst_ref=dst, send_sem=in_send, recv_sem=in_recv.at[part],
                device_id=(to_bx, to_by), device_id_type=MESH,
            ).start()

        return carry

    lax.fori_loop(0, 64, send_in, 0)

    loads[1].wait()
    loads[2].wait()
    lane = lax.broadcasted_iota(jnp.int32, (TERMS, 96), 1).astype(jnp.float32)
    row_i = rows_ref[0, :, 0:96]
    row_j = rows_ref[1, :, 0:96]

    def spread(level, a1):
        pick = jnp.where(row_i + (12 * a1).astype(jnp.float32) == lane, 1.0, 0.0)
        return jnp.dot(pick, slow_ref[level], precision=lax.Precision.HIGHEST, preferred_element_type=jnp.float32)

    def column(table, a2):
        picked = jnp.where(row_j + (12 * a2).astype(jnp.float32) == lane, table, 0.0)
        return jnp.broadcast_to(jnp.sum(picked, axis=1, keepdims=True), (TERMS, LANES))

    zero, one = jnp.int32(0), jnp.int32(1)
    vtab[0] = column(spread(0, zero), zero)

    def fill1(a1, carry):
        table = spread(1, a1)
        for a2 in range(2):
            vtab[1 + 2 * a1 + a2] = column(table, a2 * one)
        return carry

    lax.fori_loop(0, 2, fill1, 0)

    def fill2(z, carry):
        table = spread(2, z)
        for a2 in range(2):
            vtab[5 + 2 * z + a2] = column(table, 2 * a2 + core)
        return carry

    lax.fori_loop(0, 4, fill2, 0)
    left_rows = lax.broadcasted_iota(jnp.int32, (TERMS, LANES), 1) < 64

    def fill3(a1, carry):
        table = spread(3, a1)
        for a2 in range(2):
            box = 2 * (2 * a2 + core)
            vtab[13 + 2 * a1 + a2] = jnp.where(left_rows, column(table, box), column(table, box + 1))
        return carry

    lax.fori_loop(0, 8, fill3, 0)

    lanes = lax.broadcasted_iota(jnp.int32, (8, LANES), 1)
    low2 = reverse6(lax.rem(lanes, 64)) * 16
    lane2 = lax.div(lanes, 64) * 8 + low2
    back = 127 - lanes
    back_half = lax.div(lanes, 64) * 64 + 63 - lax.rem(lanes, 64)

    def permute(block, index):
        rows = [
            jnp.take_along_axis(block[8 * i : 8 * i + 8], index, axis=1, mode="promise_in_bounds")
            for i in range(block.shape[0] // 8)
        ]
        return jnp.concatenate(rows, axis=0)

    def magnitude(level, r1, c1, r2, c2):
        width = 2.0 ** (level + 1)
        k = (lax.div(r1, 1 << level).astype(jnp.float32) + 0.5) * width - N / 2
        step = (c1 - 0.5) * width
        k0 = k - step
        k2 = (lax.div(r2, jnp.full(r2.shape, 1 << level, jnp.int32)).astype(jnp.float32) + 0.5) * width - N / 2
        step2 = (c2 - 0.5) * width
        k20 = k2 - step2
        above = step * (k + k0) + step2 * (k2 + k20)
        return above / (jnp.sqrt(k * k + k2 * k2) + jnp.sqrt(k0 * k0 + k20 * k20))

    def interpolate(y_ref, child, table, blocks):
        y_ref[child] = jnp.dot(
            mix_ref[table], operand(jnp.concatenate(blocks, axis=1)), preferred_element_type=jnp.float32
        )

    def tiles(body):
        def tile(i, carry):
            body(i, pl.ds(pl.multiple_of(8 * i, 8), 8), pl.ds(pl.multiple_of(8 * i + TERMS, 8), 8))
            return carry

        lax.fori_loop(0, TERMS // 8, tile, 0, unroll=True)

    def added(total, co, si, y_ref, child, at, at_im, side):
        cols = pl.ds(side * LANES, LANES)
        y_re, y_im = y_ref[child, at, cols], y_ref[child, at_im, cols]
        re, im = co * y_re - si * y_im, co * y_im + si * y_re
        return (re, im) if total is None else (total[0] + re, total[1] + im)

    def exponentials(entry, slots, sizes):
        def tile(i, carry):
            at = pl.ds(pl.multiple_of(8 * i, 8), 8)
            for j in range(4):
                co, si = unit(vtab[slots[j], at, :] * sizes[j])
                e_tab[entry, j, 0, at, :] = co
                e_tab[entry, j, 1, at, :] = si
            return carry

        lax.fori_loop(0, TERMS // 8, tile, 0, unroll=3)

    def combine_cores(y_ref, dst, entry):
        def body(i, at, at_im):
            totals = [None, None]
            for c1 in range(2):
                for c2 in range(2):
                    co, si = e_tab[entry, 2 * c1 + c2, 0, at, :], e_tab[entry, 2 * c1 + c2, 1, at, :]
                    totals[0] = added(totals[0], co, si, y_ref, 2 * c1 + c2, at, at_im, 0)
                    totals[1] = added(totals[1], co, si, y_ref, 2 * c1 + 1 - c2, at, at_im, 1)
            for side in range(2):
                put(dst[side], i, totals[side])

        tiles(body)

    def combine_mirrored(y_ref, dst, entry, index):
        def body(i, at, at_im):
            for side in range(2):
                totals = [None, None]
                for c1 in range(2):
                    co, si = e_tab[entry, 2 * c1 + side, 0, at, :], e_tab[entry, 2 * c1 + side, 1, at, :]
                    for c2 in range(2):
                        totals[c2] = added(totals[c2], co, si, y_ref, 2 * c1 + c2, at, at_im, side)
                put(dst[side], i, [totals[0][part] + permute(totals[1][part], index) for part in range(2)])

        tiles(body)

    def put(dst, i, total):
        rows = pl.ds(pl.multiple_of(8 * lax.rem(i, 9), 8), 8)
        for part in range(2):
            dst[2 * part + lax.div(i, 9), rows, :] = total[part]

    def window(src, q1, q2):
        rows = pl.ds(pl.multiple_of(32 * q2, 8), 40)
        return jnp.concatenate([src[q1, rows, :], src[2 + q1, rows, :]], axis=0)

    pairs = ((0, y_a, acc_a), (1, y_b, acc_b))

    def x_of(slot):
        dx = 2 * slot + lax.rem(my_x + core, 2)
        x = lax.rem(my_x - dx + 4, 4)
        return lax.div(x, 2), low1 + 4 * lax.div(x, 2) + 8 * core

    def group_of(part):
        return lax.rem(my_z + lax.div(part, 2), 2), lax.rem(my_y + lax.rem(part, 2), 2)

    def box_of(step):
        return lax.rem(lax.div(my_z, 2) + 1 + lax.div(step, 2), 2), lax.rem(lax.div(my_y, 2) + step, 2)

    children = [(c1, c2) for c1 in range(2) for c2 in range(2)]

    def phases0(part, carry):
        z0, y0 = group_of(part)
        for slot in range(2):
            r1 = x_of(slot)[1] + 2 * z0
            sizes = [magnitude(0, r1 + c1, c1, lane2 + (c2 + 2 * y0), c2) for c1, c2 in children]
            exponentials(2 * part + slot, (0,) * 4, sizes)
        return carry

    def phases1(step, carry):
        a1, a2 = box_of(step)
        for slot in range(2):
            r1 = x_of(slot)[1]
            sizes = [magnitude(1, r1 + 2 * c1, c1, lane2 + 2 * c2, c2) for c1, c2 in children]
            exponentials(8 + 2 * step + slot, (1 + 2 * a1 + a2,) * 4, sizes)
        return carry

    def phases2(step, carry):
        a1, a2 = box_of(step)
        sizes = [
            magnitude(2, low1 + 4 * c1 + 8 * x0, c1, lane2, 0) for c1 in range(2) for x0 in (core, 1 - core)
        ]
        for z0 in range(2):
            exponentials(16 + 2 * step + z0, (5 + 2 * (2 * a1 + z0) + a2,) * 4, sizes)
        return carry

    def phases3(step, carry):
        a1, a2 = box_of(step)
        sizes = [magnitude(3, low1 + 8 * c1, c1, low2, 0) for c1 in range(2) for side in range(2)]
        for z0 in range(2):
            slot = 13 + 4 * (2 * a1 + z0) + a2
            exponentials(24 + 2 * step + z0, (slot, slot + 2, slot, slot + 2), sizes)
        return carry

    def level0(part, carry):
        pltpu.make_async_copy(xin.at[0, 0], xin.at[0, 0], in_recv.at[part]).wait()
        z0, y0 = group_of(part)
        for slot, y_ref, _ in pairs:
            for c1, c2 in children:
                z = 2 * c1 + z0
                first = xin[slot, 0, z, 2 * c2 + y0]
                second = permute(xin[slot, 1, z, 2 * c2 + 1 - y0], back)
                interpolate(y_ref, 2 * c1 + c2, 2 * c1 + c2, [first, second])
        for slot, y_ref, _ in pairs:
            combine_cores(y_ref, (s0.at[slot, z0, y0, 0], s0.at[slot, z0, 1 - y0, 1]), 2 * part + slot)
        for number, later in ((0, phases1), (1, phases2), (2, phases3)):

            @pl.when(part == number)
            def _(later=later):
                lax.fori_loop(0, 4, later, 0)

        return carry

    lax.fori_loop(0, 4, phases0, 0)
    loads[3].wait()
    lax.fori_loop(0, 4, level0, 0)

    def level1(step):
        a1, a2 = box_of(step)
        for slot, y_ref, _ in pairs:
            for c1, c2 in children:
                blocks = [window(s0.at[slot, c1, c2, side], a1, a2) for side in range(2)]
                interpolate(y_ref, 2 * c1 + c2, 4 + 4 * a2 + 2 * c1 + c2, blocks)
        for slot, y_ref, _ in pairs:
            x1 = x_of(slot)[0]
            combine_cores(y_ref, (z1.at[step, x1, 0], z1.at[step, x1, 1]), 8 + 2 * step + slot)
        pltpu.make_async_remote_copy(
            src_ref=z1.at[step, :, :, :, pl.ds(pl.multiple_of(32 * (1 - core), 8), 40), :],
            dst_ref=zr.at[step],
            send_sem=sib_send.at[step],
            recv_sem=sib_recv.at[step],
            device_id=(bx, my_y * 2 + 1 - core),
            device_id_type=MESH,
        ).start()

    left = lax.broadcasted_iota(jnp.int32, (PAD, LANES), 1) < 64
    left_half = lax.broadcasted_iota(jnp.int32, (HALF, LANES), 1) < 64

    def level23(step):
        a1, a2 = box_of(step)
        y = 2 * a2 + core
        pltpu.make_async_copy(zr.at[0], zr.at[0], sib_recv.at[step]).wait()
        for z0, y_ref, _ in pairs:
            for c1, c2 in children:
                other = zr.at[step, c1, c2]
                blocks = [
                    window(z1.at[step, c1, c2], z0, core),
                    jnp.concatenate([other[z0], other[2 + z0]], axis=0),
                ]
                interpolate(y_ref, 2 * c1 + c2, 4 + 4 * core + 2 * c1 + c2, blocks)
        for z0, y_ref, _ in pairs:
            combine_mirrored(y_ref, (s2.at[z0, 0], s2.at[z0, 1]), 16 + 2 * step + z0, back)
        for z0, y_ref, _ in pairs:
            for c1 in range(2):
                src = s2.at[z0, lax.rem(c1 + core, 2)]
                near, far = [], []
                for x1 in range(2):
                    first = window(src, x1, 0)
                    second = window(src, x1, 1)
                    second = jnp.concatenate([second[4:40], second[36:40], second[44:80], second[76:80]], axis=0)
                    near.append(jnp.where(left, first, pltpu.roll(second, 64, 1)))
                    far.append(jnp.where(left, permute(first, back), permute(second, back_half)))
                interpolate(y_ref, 2 * c1, 4 + 2 * c1, near)
                interpolate(y_ref, 2 * c1 + 1, 4 + 2 * c1 + 1, far)
        for z0, y_ref, acc_ref in pairs:
            z = 2 * a1 + z0
            combine_mirrored(y_ref, (acc_ref.at[0], acc_ref.at[1]), 24 + 2 * step + z0, back_half)
            for x1 in range(2):
                for q1 in range(2):
                    for part in range(2):
                        upper = acc_ref[x1, 2 * part + q1, 0:HALF, :]
                        lower = acc_ref[x1, 2 * part + q1, HALF:ROWS, :]
                        rows = pl.ds(HALF * part, HALF)
                        obuf[step, z0, x1, q1, 0, rows, :] = jnp.where(left_half, upper, pltpu.roll(lower, 64, 1))
                        obuf[step, z0, x1, q1, 1, rows, :] = jnp.where(left_half, pltpu.roll(upper, 64, 1), lower)

            def send_out(target, carry, z=z, z0=z0):
                x1, q1, c = lax.div(target, 4), lax.rem(lax.div(target, 2), 2), lax.rem(target, 2)
                to_bx, to_by = z * 4 + 2 * x1 + q1, 2 * y + c
                src, dst = obuf.at[step, z0, x1, q1, c], orecv.at[chip]
                here = jnp.logical_and(to_bx == bx, to_by == by)

                @pl.when(here)
                def _():
                    pltpu.make_async_copy(src, dst, out_recv.at[step]).start()

                @pl.when(jnp.logical_not(here))
                def _():
                    pltpu.make_async_remote_copy(
                        src_ref=src, dst_ref=dst, send_sem=out_send, recv_sem=out_recv.at[step],
                        device_id=(to_bx, to_by), device_id_type=MESH,
                    ).start()

                return carry

            lax.fori_loop(0, 8, send_out, 0)

    def both(step, carry):
        @pl.when(step < 4)
        def _():
            level1(step)

        @pl.when(step > 0)
        def _():
            level23(step - 1)

        return carry

    lax.fori_loop(0, 5, both, 0)

    def settle(step, carry):
        pltpu.make_async_copy(zr.at[0], zr.at[0], sib_send.at[step]).wait()
        return carry

    lax.fori_loop(0, 4, settle, 0)
    for keeps, sem in ((my_x0 == core, in_send), (lax.rem(my_y, 2) == core, out_send)):

        @pl.when(keeps)
        def _(sem=sem):
            pltpu.make_async_copy(sbuf.at[pl.ds(0, 63)], sbuf.at[pl.ds(0, 63)], sem).wait()

        @pl.when(jnp.logical_not(keeps))
        def _(sem=sem):
            pltpu.make_async_copy(sbuf, sbuf, sem).wait()

    def arrive(step, carry):
        pltpu.make_async_copy(orecv.at[pl.ds(0, 16)], orecv.at[pl.ds(0, 16)], out_recv.at[step]).wait()
        z1_from = lax.rem(lax.div(my_z, 2) + 1 + lax.div(step, 2), 2)
        y1_from = lax.rem(lax.div(my_y, 2) + step, 2)

        def scatter_rows(i, carry):
            z, x, y = 2 * z1_from + lax.div(i, 8), lax.rem(lax.div(i, 2), 4), 2 * y1_from + lax.rem(i, 2)
            ell = z * 16 + x * 4 + y
            for tile in range(9):
                out_ref[pl.ds(tile * 512 + ell, 8, stride=64), :] = orecv[ell, 8 * tile : 8 * tile + 8, :]
            return carry

        lax.fori_loop(0, 16, scatter_rows, 0, unroll=4)
        return carry

    lax.fori_loop(0, 4, arrive, 0)


def shards(coefficients, slowness):
    rows = jnp.transpose(coefficients, (0, 1, 3, 2, 4)).reshape(ROWS * 64, LANES)
    operands = (rows, slowness, jnp.asarray(mixing_tables()), jnp.asarray(row_tables()))
    dense = (ROWS, LANES)
    scratch = [pltpu.VMEM(operands[i].shape, operands[i].dtype) for i in range(4)]
    scratch += [
        pltpu.VMEM(shape, jnp.float32)
        for shape in (
            (64,) + dense,
            (2, 2, 4, 4) + dense,
            (2, 2, 2, 2, 4) + dense,
            (4, 2, 2, 4) + dense,
            (4, 2, 2, 4, 40, LANES),
            (2, 2, 4) + dense,
            (4, 2, 2, 2, 2) + dense,
            (64,) + dense,
            (29, TERMS, LANES),
            (32, 4, 2, TERMS, LANES),
            (4, 2 * TERMS, 2 * LANES),
            (4, 2 * TERMS, 2 * LANES),
            (2, 4) + dense,
            (2, 4) + dense,
        )
    ]
    scratch += [
        pltpu.SemaphoreType.DMA((4,)),
        pltpu.SemaphoreType.DMA,
        pltpu.SemaphoreType.DMA((4,)),
        pltpu.SemaphoreType.DMA((4,)),
        pltpu.SemaphoreType.DMA((4,)),
        pltpu.SemaphoreType.DMA,
        pltpu.SemaphoreType.DMA((4,)),
    ]
    out = pl.pallas_call(
        kernel,
        out_shape=jax.ShapeDtypeStruct((ROWS * 64, LANES), jnp.float32),
        in_specs=[pl.BlockSpec(memory_space=pltpu.HBM)] * 4,
        out_specs=pl.BlockSpec(memory_space=pltpu.VMEM),
        scratch_shapes=scratch,
        compiler_params=pltpu.CompilerParams(has_side_effects=True, vmem_limit_bytes=50 << 20),
    )(*operands)
    return jnp.transpose(out.reshape(2, CHEB, CHEB, 64, LANES), (0, 1, 3, 2, 4))


def solution(mesh):
    placed = (P(None, None, "bx", None, "by"), P())
    return jax.shard_map(
        shards,
        mesh=mesh,
        in_specs=placed,
        out_specs=P(None, None, "bx", None, "by"),
        check_vma=False,
    )
```

```python
import math

import jax
import jax.numpy as jnp
import numpy as np
from jax import lax
from jax.experimental import pallas as pl
from jax.experimental.pallas import tpu as pltpu
from jax.sharding import PartitionSpec as P

N = 2048
CHEB = 6
HALF = CHEB * CHEB
ROWS = 2 * HALF
TERMS = 4 * HALF
PAD = 80
DEPTH = 256
LANES = 128
MESH = pl.DeviceIdType.MESH


def cheb_points():
    return np.cos(np.pi * (2 * np.arange(CHEB) + 1) / (2 * CHEB))


def fit(function, degree):
    count = 200
    s = 0.125 * (1 + np.cos(np.pi * (2 * np.arange(count) + 1) / (2 * count)))
    series = np.polynomial.chebyshev.Chebyshev.fit(s, function(np.sqrt(s)), degree, domain=[0, 0.25])
    return [float(c) for c in series.convert(kind=np.polynomial.Polynomial).coef]


SIN = fit(lambda r: math.sqrt(2) * np.sin(np.pi * r) / r, 3)
COS = fit(lambda r: math.sqrt(2) * np.cos(np.pi * r), 4)
WHOLE = 1.5 * 2.0**23


POINTS = [float(point) for point in cheb_points()]
SCALES = [
    float(1 / np.prod([cheb_points()[s] - cheb_points()[j] for j in range(CHEB) if j != s])) for s in range(CHEB)
]


def horner(coefficients, s):
    value = s * coefficients[-1] + coefficients[-2]
    for coefficient in coefficients[-3::-1]:
        value = value * s + coefficient
    return value


def unit(turns):
    r = turns - ((turns + WHOLE) - WHOLE)
    s = r * r
    half = horner(SIN, s) * r
    return 1.0 - half * half, half * horner(COS, s)


def operand(block):
    if block.shape[0] < PAD:
        block = jnp.concatenate([block, jnp.zeros((PAD - block.shape[0], block.shape[1]), jnp.float32)], axis=0)
    high = block.astype(jnp.bfloat16)
    low = (block - high.astype(jnp.float32)).astype(jnp.bfloat16)
    return jnp.concatenate([high, low, high, jnp.zeros((DEPTH - 3 * PAD, block.shape[1]), jnp.bfloat16)], axis=0)


def choose(index, values):
    result = jnp.full(index.shape, values[0], jnp.float32)
    for number, value in enumerate(values[1:], 1):
        result = jnp.where(index == number, value, result)
    return result


def digits(value, *sizes):
    out = []
    for size in sizes[::-1]:
        rest = jnp.floor((value + 0.5) * (1.0 / size))
        out.append(value - rest * size)
        value = rest
    return out[::-1]


def lagrange(at, source):
    product = choose(source, SCALES)
    for number, point in enumerate(POINTS):
        product = product * jnp.where(source == number, 1.0, at - point)
    return product


def mixing_tables(mix_ref, raw_ref):
    shape = (HALF, DEPTH)
    column = lax.broadcasted_iota(jnp.int32, shape, 1).astype(jnp.float32)
    copy, inside = digits(column, 4, PAD)
    row = lax.broadcasted_iota(jnp.int32, shape, 0).astype(jnp.float32)
    t1, t2 = digits(row, CHEB, CHEB)
    second = inside >= 40
    place = inside - jnp.where(second, 40.0, 0.0)
    used = jnp.logical_and(place < HALF, copy < 3)
    s1, s2 = digits(jnp.minimum(place, HALF - 1.0), CHEB, CHEB)
    at1, at2 = choose(t1, POINTS) * 0.5, choose(t2, POINTS) * 0.5
    weights1 = [jnp.where(used, lagrange(q - 0.5 + at1, s1), 0.0) for q in range(2)]
    weights2 = [lagrange(q - 0.5 + at2, s2) for q in range(2)]
    for q1 in range(2):
        for q2 in range(2):
            weights = weights1[q1] * weights2[q2]
            turns1, turns2 = 0.5 * (q1 + 0.5 + at1), 0.5 * (q2 + 0.5 + at2)
            plus, minus = unit(turns1 + turns2), unit(turns1 - turns2)
            for c1 in range(2):
                for c2 in range(2):
                    co, si = plus if c1 == c2 else minus
                    si = si if c1 else -si
                    real, imag = co * weights, si * weights
                    for part, values in enumerate((jnp.where(second, -imag, real), jnp.where(second, real, imag))):
                        high = values.astype(jnp.bfloat16).astype(jnp.float32)
                        values = jnp.where(copy < 2, high, values - high)
                        base = part * TERMS + q1 * ROWS + q2 * HALF
                        raw_ref[2 * c1 + c2, base : base + HALF, :] = values

    shape = (48, DEPTH)
    copy, inside = digits(lax.broadcasted_iota(jnp.int32, shape, 1).astype(jnp.float32), 4, PAD)

    def variants(i, carry):
        table, rows = lax.div(i, 6), pl.ds(pl.multiple_of(48 * lax.rem(i, 6), 16), 48)
        values = raw_ref[table, rows, :]
        dense = jnp.where(inside < HALF, values, pltpu.roll(values, DEPTH - 4, 1))
        dense = jnp.where(inside < ROWS, dense, 0.0)
        for variant, block in enumerate((dense, values, pltpu.roll(values, 4, 1))):
            mix_ref[4 * variant + table, rows, :] = block.astype(jnp.bfloat16)
        return carry

    lax.fori_loop(0, 24, variants, 0)


def reverse6(value):
    total = 0
    for bit in range(6):
        total = total + lax.rem(lax.div(value, 1 << bit), 2) * (1 << (5 - bit))
    return total


def kernel(
    coef_hbm, slow_hbm, out_ref,
    coef_ref, slow_ref, mix_ref, raw_ref,
    sbuf, xin, s0, z1, zr, s2, obuf, orecv, vtab, e_tab, y_a, y_b, acc_a, acc_b,
    load, in_send, in_recv, sib_send, sib_recv, out_send, out_recv,
):
    bx, by = lax.axis_index("bx"), lax.axis_index("by")
    my_z, my_x = lax.div(bx, 4), lax.rem(bx, 4)
    my_y, core = lax.div(by, 2), lax.rem(by, 2)
    my_x0 = lax.rem(my_x, 2)
    chip = bx * 4 + my_y
    low1 = reverse6(chip) * 16

    loads = [
        pltpu.make_async_copy(src, dst, load.at[i])
        for i, (src, dst) in enumerate(
            ((coef_hbm, coef_ref), (slow_hbm, slow_ref))
        )
    ]
    for copy in loads:
        copy.start()

    barrier = pltpu.get_barrier_semaphore()
    me = bx * 8 + by

    def greet(i, carry):
        there = lax.rem(me + i, 128)
        pl.semaphore_signal(barrier, inc=1, device_id=(lax.div(there, 8), lax.rem(there, 8)), device_id_type=MESH)
        return carry

    lax.fori_loop(1, 128, greet, 0)
    loads[0].wait()

    def gather_rows(ell, carry):
        for tile in range(9):
            sbuf[ell, 8 * tile : 8 * tile + 8, :] = coef_ref[pl.ds(tile * 512 + ell, 8, stride=64), :]
        return carry

    lax.fori_loop(0, 64, gather_rows, 0, unroll=8)
    pl.semaphore_wait(barrier, 127)

    def send_in(step, carry):
        part, inner = lax.div(step, 16), lax.rem(step, 16)
        pz, py = lax.div(part, 2), lax.rem(lax.rem(part, 2) + core, 2)
        other = lax.div(inner, 4)
        dx = lax.rem(lax.rem(inner, 4) + other, 4)
        dz, dy = 2 * lax.div(other, 2) + pz, 2 * lax.rem(other, 2) + py
        sign = 1 - 2 * core
        dx, dz, dy = [lax.rem(4 + sign * d, 4) for d in (dx, dz, dy)]
        to_x, to_z, to_y = lax.rem(my_x + dx, 4), lax.rem(my_z + dz, 4), lax.rem(my_y + dy, 4)
        to_bx, to_by = to_z * 4 + to_x, to_y * 2 + my_x0
        ell = to_z * 16 + to_x * 4 + to_y
        src = sbuf.at[ell]
        dst = xin.at[lax.div(dx, 2), core, my_z, my_y]
        here = jnp.logical_and(to_bx == bx, to_by == by)

        @pl.when(here)
        def _():
            pltpu.make_async_copy(src, dst, in_recv.at[part]).start()

        @pl.when(jnp.logical_not(here))
        def _():
            pltpu.make_async_remote_copy(
                src_ref=src, dst_ref=dst, send_sem=in_send, recv_sem=in_recv.at[part],
                device_id=(to_bx, to_by), device_id_type=MESH,
            ).start()

        return carry

    lax.fori_loop(0, 64, send_in, 0)

    loads[1].wait()
    lane = lax.broadcasted_iota(jnp.int32, (TERMS, 96), 1).astype(jnp.float32)
    row = lax.broadcasted_iota(jnp.int32, (TERMS, 96), 0).astype(jnp.float32)
    q1, q2, t1, t2 = digits(row, 2, 2, CHEB, CHEB)
    row_i, row_j = CHEB * q1 + t1, CHEB * q2 + t2

    def spread(level, a1):
        pick = jnp.where(row_i + (12 * a1).astype(jnp.float32) == lane, 1.0, 0.0)
        return jnp.dot(pick, slow_ref[level], precision=lax.Precision.HIGHEST, preferred_element_type=jnp.float32)

    def column(table, a2):
        picked = jnp.where(row_j + (12 * a2).astype(jnp.float32) == lane, table, 0.0)
        return jnp.broadcast_to(jnp.sum(picked, axis=1, keepdims=True), (TERMS, LANES))

    zero, one = jnp.int32(0), jnp.int32(1)
    vtab[0] = column(spread(0, zero), zero)

    def fill1(a1, carry):
        table = spread(1, a1)
        for a2 in range(2):
            vtab[1 + 2 * a1 + a2] = column(table, a2 * one)
        return carry

    lax.fori_loop(0, 2, fill1, 0)

    def fill2(z, carry):
        table = spread(2, z)
        for a2 in range(2):
            vtab[5 + 2 * z + a2] = column(table, 2 * a2 + core)
        return carry

    lax.fori_loop(0, 4, fill2, 0)
    left_rows = lax.broadcasted_iota(jnp.int32, (TERMS, LANES), 1) < 64

    def fill3(a1, carry):
        table = spread(3, a1)
        for a2 in range(2):
            box = 2 * (2 * a2 + core)
            vtab[13 + 2 * a1 + a2] = jnp.where(left_rows, column(table, box), column(table, box + 1))
        return carry

    lax.fori_loop(0, 8, fill3, 0)

    lanes = lax.broadcasted_iota(jnp.int32, (8, LANES), 1)
    low2 = reverse6(lax.rem(lanes, 64)) * 16
    lane2 = lax.div(lanes, 64) * 8 + low2
    back = 127 - lanes
    back_half = lax.div(lanes, 64) * 64 + 63 - lax.rem(lanes, 64)

    def permute(block, index):
        rows = [
            jnp.take_along_axis(block[8 * i : 8 * i + 8], index, axis=1, mode="promise_in_bounds")
            for i in range(block.shape[0] // 8)
        ]
        return jnp.concatenate(rows, axis=0)

    def magnitude(level, r1, c1, r2, c2):
        width = 2.0 ** (level + 1)
        k = (lax.div(r1, 1 << level).astype(jnp.float32) + 0.5) * width - N / 2
        step = (c1 - 0.5) * width
        k0 = k - step
        k2 = (lax.div(r2, jnp.full(r2.shape, 1 << level, jnp.int32)).astype(jnp.float32) + 0.5) * width - N / 2
        step2 = (c2 - 0.5) * width
        k20 = k2 - step2
        above = step * (k + k0) + step2 * (k2 + k20)
        return above / (jnp.sqrt(k * k + k2 * k2) + jnp.sqrt(k0 * k0 + k20 * k20))

    def interpolate(y_ref, child, table, blocks):
        y_ref[child] = jnp.dot(
            mix_ref[table], operand(jnp.concatenate(blocks, axis=1)), preferred_element_type=jnp.float32
        )

    def tiles(body):
        def tile(i, carry):
            body(i, pl.ds(pl.multiple_of(8 * i, 8), 8), pl.ds(pl.multiple_of(8 * i + TERMS, 8), 8))
            return carry

        lax.fori_loop(0, TERMS // 8, tile, 0, unroll=True)

    def added(total, co, si, y_ref, child, at, at_im, side):
        cols = pl.ds(side * LANES, LANES)
        y_re, y_im = y_ref[child, at, cols], y_ref[child, at_im, cols]
        re, im = co * y_re - si * y_im, co * y_im + si * y_re
        return (re, im) if total is None else (total[0] + re, total[1] + im)

    def exponentials(entry, slots, sizes):
        def tile(i, carry):
            at = pl.ds(pl.multiple_of(8 * i, 8), 8)
            for j in range(4):
                co, si = unit(vtab[slots[j], at, :] * sizes[j])
                e_tab[entry, j, 0, at, :] = co
                e_tab[entry, j, 1, at, :] = si
            return carry

        lax.fori_loop(0, TERMS // 8, tile, 0, unroll=3)

    def combine_cores(y_ref, dst, entry):
        def body(i, at, at_im):
            totals = [None, None]
            for c1 in range(2):
                for c2 in range(2):
                    co, si = e_tab[entry, 2 * c1 + c2, 0, at, :], e_tab[entry, 2 * c1 + c2, 1, at, :]
                    totals[0] = added(totals[0], co, si, y_ref, 2 * c1 + c2, at, at_im, 0)
                    totals[1] = added(totals[1], co, si, y_ref, 2 * c1 + 1 - c2, at, at_im, 1)
            for side in range(2):
                put(dst[side], i, totals[side])

        tiles(body)

    def combine_mirrored(y_ref, dst, entry, index):
        def body(i, at, at_im):
            for side in range(2):
                totals = [None, None]
                for c1 in range(2):
                    co, si = e_tab[entry, 2 * c1 + side, 0, at, :], e_tab[entry, 2 * c1 + side, 1, at, :]
                    for c2 in range(2):
                        totals[c2] = added(totals[c2], co, si, y_ref, 2 * c1 + c2, at, at_im, side)
                put(dst[side], i, [totals[0][part] + permute(totals[1][part], index) for part in range(2)])

        tiles(body)

    def put(dst, i, total):
        rows = pl.ds(pl.multiple_of(8 * lax.rem(i, 9), 8), 8)
        for part in range(2):
            dst[2 * part + lax.div(i, 9), rows, :] = total[part]

    def window(src, q1, q2):
        rows = pl.ds(pl.multiple_of(32 * q2, 8), 40)
        return jnp.concatenate([src[q1, rows, :], src[2 + q1, rows, :]], axis=0)

    pairs = ((0, y_a, acc_a), (1, y_b, acc_b))

    def x_of(slot):
        dx = 2 * slot + lax.rem(my_x + core, 2)
        x = lax.rem(my_x - dx + 4, 4)
        return lax.div(x, 2), low1 + 4 * lax.div(x, 2) + 8 * core

    def group_of(part):
        return lax.rem(my_z + lax.div(part, 2), 2), lax.rem(my_y + lax.rem(part, 2), 2)

    def box_of(step):
        return lax.rem(lax.div(my_z, 2) + 1 + lax.div(step, 2), 2), lax.rem(lax.div(my_y, 2) + 1 + step, 2)

    children = [(c1, c2) for c1 in range(2) for c2 in range(2)]

    def phases0(part, carry):
        z0, y0 = group_of(part)
        for slot in range(2):
            r1 = x_of(slot)[1] + 2 * z0
            sizes = [magnitude(0, r1 + c1, c1, lane2 + (c2 + 2 * y0), c2) for c1, c2 in children]
            exponentials(2 * part + slot, (0,) * 4, sizes)
        return carry

    def phases1(step, carry):
        a1, a2 = box_of(step)
        for slot in range(2):
            r1 = x_of(slot)[1]
            sizes = [magnitude(1, r1 + 2 * c1, c1, lane2 + 2 * c2, c2) for c1, c2 in children]
            exponentials(8 + 2 * step + slot, (1 + 2 * a1 + a2,) * 4, sizes)
        return carry

    def phases2(step, carry):
        a1, a2 = box_of(step)
        sizes = [
            magnitude(2, low1 + 4 * c1 + 8 * x0, c1, lane2, 0) for c1 in range(2) for x0 in (core, 1 - core)
        ]
        for z0 in range(2):
            exponentials(16 + 2 * step + z0, (5 + 2 * (2 * a1 + z0) + a2,) * 4, sizes)
        return carry

    def phases3(step, carry):
        a1, a2 = box_of(step)
        sizes = [magnitude(3, low1 + 8 * c1, c1, low2, 0) for c1 in range(2) for side in range(2)]
        for z0 in range(2):
            slot = 13 + 4 * (2 * a1 + z0) + a2
            exponentials(24 + 2 * step + z0, (slot, slot + 2, slot, slot + 2), sizes)
        return carry

    def level0(part, carry):
        pltpu.make_async_copy(xin.at[0, 0], xin.at[0, 0], in_recv.at[part]).wait()
        z0, y0 = group_of(part)
        for slot, y_ref, _ in pairs:
            for c1, c2 in children:
                z = 2 * c1 + z0
                first = xin[slot, 0, z, 2 * c2 + y0]
                second = permute(xin[slot, 1, z, 2 * c2 + 1 - y0], back)
                interpolate(y_ref, 2 * c1 + c2, 2 * c1 + c2, [first, second])
        for slot, y_ref, _ in pairs:
            combine_cores(y_ref, (s0.at[slot, z0, y0, 0], s0.at[slot, z0, 1 - y0, 1]), 2 * part + slot)
        for number, later in ((0, phases1), (1, phases2), (2, phases3)):

            @pl.when(part == number)
            def _(later=later):
                lax.fori_loop(0, 4, later, 0)

        return carry

    lax.fori_loop(0, 4, phases0, 0)
    mixing_tables(mix_ref, raw_ref)
    lax.fori_loop(0, 4, level0, 0)

    def level1(step):
        a1, a2 = box_of(step)
        for slot, y_ref, _ in pairs:
            for c1, c2 in children:
                blocks = [window(s0.at[slot, c1, c2, side], a1, a2) for side in range(2)]
                interpolate(y_ref, 2 * c1 + c2, 4 + 4 * a2 + 2 * c1 + c2, blocks)
        for slot, y_ref, _ in pairs:
            x1 = x_of(slot)[0]
            combine_cores(y_ref, (z1.at[step, x1, 0], z1.at[step, x1, 1]), 8 + 2 * step + slot)
        pltpu.make_async_remote_copy(
            src_ref=z1.at[step, :, :, :, pl.ds(pl.multiple_of(32 * (1 - core), 8), 40), :],
            dst_ref=zr.at[step],
            send_sem=sib_send.at[step],
            recv_sem=sib_recv.at[step],
            device_id=(bx, my_y * 2 + 1 - core),
            device_id_type=MESH,
        ).start()

    left = lax.broadcasted_iota(jnp.int32, (PAD, LANES), 1) < 64
    left_half = lax.broadcasted_iota(jnp.int32, (HALF, LANES), 1) < 64

    def level23(step):
        a1, a2 = box_of(step)
        y = 2 * a2 + core
        pltpu.make_async_copy(zr.at[0], zr.at[0], sib_recv.at[step]).wait()
        near_z0 = lax.rem(my_z, 2)
        z0_of = (near_z0, 1 - near_z0)
        for i, y_ref, _ in pairs:
            z0 = z0_of[i]
            for c1, c2 in children:
                other = zr.at[step, c1, c2]
                blocks = [
                    window(z1.at[step, c1, c2], z0, core),
                    jnp.concatenate([other[z0], other[2 + z0]], axis=0),
                ]
                interpolate(y_ref, 2 * c1 + c2, 4 + 4 * core + 2 * c1 + c2, blocks)
        for i, y_ref, _ in pairs:
            combine_mirrored(y_ref, (s2.at[i, 0], s2.at[i, 1]), 16 + 2 * step + z0_of[i], back)
        for i, y_ref, _ in pairs:
            for c1 in range(2):
                src = s2.at[i, lax.rem(c1 + core, 2)]
                near, far = [], []
                for x1 in range(2):
                    first = window(src, x1, 0)
                    second = window(src, x1, 1)
                    second = jnp.concatenate([second[4:40], second[36:40], second[44:80], second[76:80]], axis=0)
                    near.append(jnp.where(left, first, pltpu.roll(second, 64, 1)))
                    far.append(jnp.where(left, permute(first, back), permute(second, back_half)))
                interpolate(y_ref, 2 * c1, 4 + 2 * c1, near)
                interpolate(y_ref, 2 * c1 + 1, 4 + 2 * c1 + 1, far)
        for i, y_ref, acc_ref in pairs:
            z0 = z0_of[i]
            z = 2 * a1 + z0
            combine_mirrored(y_ref, (acc_ref.at[0], acc_ref.at[1]), 24 + 2 * step + z0, back_half)
            for x1 in range(2):
                for q1 in range(2):
                    for part in range(2):
                        upper = acc_ref[x1, 2 * part + q1, 0:HALF, :]
                        lower = acc_ref[x1, 2 * part + q1, HALF:ROWS, :]
                        rows = pl.ds(HALF * part, HALF)
                        obuf[step, i, x1, q1, 0, rows, :] = jnp.where(left_half, upper, pltpu.roll(lower, 64, 1))
                        obuf[step, i, x1, q1, 1, rows, :] = jnp.where(left_half, pltpu.roll(upper, 64, 1), lower)

            def send_out(target, carry, z=z, i=i):
                hop = lax.div(target, 2)
                x = lax.rem(my_x + 5 + 2 * core + hop, 4)
                c = lax.rem(target + core, 2)
                to_bx, to_by = z * 4 + x, 2 * y + c
                src, dst = obuf.at[step, i, lax.div(x, 2), lax.rem(x, 2), c], orecv.at[chip]
                here = jnp.logical_and(to_bx == bx, to_by == by)

                @pl.when(here)
                def _():
                    pltpu.make_async_copy(src, dst, out_recv.at[step]).start()

                @pl.when(jnp.logical_not(here))
                def _():
                    pltpu.make_async_remote_copy(
                        src_ref=src, dst_ref=dst, send_sem=out_send, recv_sem=out_recv.at[step],
                        device_id=(to_bx, to_by), device_id_type=MESH,
                    ).start()

                return carry

            lax.fori_loop(0, 8, send_out, 0)

    def both(step, carry):
        @pl.when(step < 4)
        def _():
            level1(step)

        @pl.when(step > 0)
        def _():
            level23(step - 1)

        return carry

    lax.fori_loop(0, 5, both, 0)

    def settle(step, carry):
        pltpu.make_async_copy(zr.at[0], zr.at[0], sib_send.at[step]).wait()
        return carry

    lax.fori_loop(0, 4, settle, 0)
    for keeps, sem in ((my_x0 == core, in_send), (lax.rem(my_y, 2) == core, out_send)):

        @pl.when(keeps)
        def _(sem=sem):
            pltpu.make_async_copy(sbuf.at[pl.ds(0, 63)], sbuf.at[pl.ds(0, 63)], sem).wait()

        @pl.when(jnp.logical_not(keeps))
        def _(sem=sem):
            pltpu.make_async_copy(sbuf, sbuf, sem).wait()

    def arrive(step, carry):
        pltpu.make_async_copy(orecv.at[pl.ds(0, 16)], orecv.at[pl.ds(0, 16)], out_recv.at[step]).wait()
        z1_from = lax.rem(lax.div(my_z, 2) + 1 + lax.div(step, 2), 2)
        y1_from = lax.rem(lax.div(my_y, 2) + 1 + step, 2)

        def scatter_rows(i, carry):
            z, x, y = 2 * z1_from + lax.div(i, 8), lax.rem(lax.div(i, 2), 4), 2 * y1_from + lax.rem(i, 2)
            ell = z * 16 + x * 4 + y
            for tile in range(9):
                out_ref[pl.ds(tile * 512 + ell, 8, stride=64), :] = orecv[ell, 8 * tile : 8 * tile + 8, :]
            return carry

        lax.fori_loop(0, 16, scatter_rows, 0, unroll=4)
        return carry

    lax.fori_loop(0, 4, arrive, 0)


def shards(coefficients, slowness):
    rows = jnp.transpose(coefficients, (0, 1, 3, 2, 4)).reshape(ROWS * 64, LANES)
    operands = (rows, slowness)
    dense = (ROWS, LANES)
    scratch = [pltpu.VMEM(operands[i].shape, jnp.float32) for i in range(2)]
    scratch += [pltpu.VMEM((12, 2 * TERMS, DEPTH), jnp.bfloat16), pltpu.VMEM((4, 2 * TERMS, DEPTH), jnp.float32)]
    scratch += [
        pltpu.VMEM(shape, jnp.float32)
        for shape in (
            (64,) + dense,
            (2, 2, 4, 4) + dense,
            (2, 2, 2, 2, 4) + dense,
            (4, 2, 2, 4) + dense,
            (4, 2, 2, 4, 40, LANES),
            (2, 2, 4) + dense,
            (4, 2, 2, 2, 2) + dense,
            (64,) + dense,
            (29, TERMS, LANES),
            (32, 4, 2, TERMS, LANES),
            (4, 2 * TERMS, 2 * LANES),
            (4, 2 * TERMS, 2 * LANES),
            (2, 4) + dense,
            (2, 4) + dense,
        )
    ]
    scratch += [
        pltpu.SemaphoreType.DMA((4,)),
        pltpu.SemaphoreType.DMA,
        pltpu.SemaphoreType.DMA((4,)),
        pltpu.SemaphoreType.DMA((4,)),
        pltpu.SemaphoreType.DMA((4,)),
        pltpu.SemaphoreType.DMA,
        pltpu.SemaphoreType.DMA((4,)),
    ]
    out = pl.pallas_call(
        kernel,
        out_shape=jax.ShapeDtypeStruct((ROWS * 64, LANES), jnp.float32),
        in_specs=[pl.BlockSpec(memory_space=pl.ANY)] * 2,
        out_specs=pl.BlockSpec(memory_space=pltpu.VMEM),
        scratch_shapes=scratch,
        compiler_params=pltpu.CompilerParams(collective_id=0, has_side_effects=True, vmem_limit_bytes=50 << 20),
    )(*operands)
    return jnp.transpose(out.reshape(2, CHEB, CHEB, 64, LANES), (0, 1, 3, 2, 4))


def solution(mesh):
    placed = (P(None, None, "bx", None, "by"), P())
    return jax.shard_map(
        shards,
        mesh=mesh,
        in_specs=placed,
        out_specs=P(None, None, "bx", None, "by"),
        check_vma=False,
    )
```

```python
import math

import jax
import jax.numpy as jnp
import numpy as np
from jax import lax
from jax.experimental import pallas as pl
from jax.experimental.pallas import tpu as pltpu
from jax.sharding import PartitionSpec as P

N = 2048
CHEB = 6
HALF = CHEB * CHEB
ROWS = 2 * HALF
TERMS = 4 * HALF
PAD = 80
DEPTH = 256
LANES = 128
MESH = pl.DeviceIdType.MESH


def cheb_points():
    return np.cos(np.pi * (2 * np.arange(CHEB) + 1) / (2 * CHEB))


def fit(function, degree):
    count = 200
    s = 0.125 * (1 + np.cos(np.pi * (2 * np.arange(count) + 1) / (2 * count)))
    series = np.polynomial.chebyshev.Chebyshev.fit(s, function(np.sqrt(s)), degree, domain=[0, 0.25])
    return [float(c) for c in series.convert(kind=np.polynomial.Polynomial).coef]


SIN = fit(lambda r: math.sqrt(2) * np.sin(np.pi * r) / r, 3)
COS = fit(lambda r: math.sqrt(2) * np.cos(np.pi * r), 4)
WHOLE = 1.5 * 2.0**23


POINTS = [float(point) for point in cheb_points()]
SCALES = [
    float(1 / np.prod([cheb_points()[s] - cheb_points()[j] for j in range(CHEB) if j != s])) for s in range(CHEB)
]


def horner(coefficients, s):
    value = s * coefficients[-1] + coefficients[-2]
    for coefficient in coefficients[-3::-1]:
        value = value * s + coefficient
    return value


def unit(turns):
    r = turns - ((turns + WHOLE) - WHOLE)
    s = r * r
    half = horner(SIN, s) * r
    return 1.0 - half * half, half * horner(COS, s)


def operand(block):
    if block.shape[0] < PAD:
        block = jnp.concatenate([block, jnp.zeros((PAD - block.shape[0], block.shape[1]), jnp.float32)], axis=0)
    high = block.astype(jnp.bfloat16)
    low = (block - high.astype(jnp.float32)).astype(jnp.bfloat16)
    return jnp.concatenate([high, low, high, jnp.zeros((DEPTH - 3 * PAD, block.shape[1]), jnp.bfloat16)], axis=0)


def choose(index, values):
    result = jnp.full(index.shape, values[0], jnp.float32)
    for number, value in enumerate(values[1:], 1):
        result = jnp.where(index == number, value, result)
    return result


def digits(value, *sizes):
    out = []
    for size in sizes[::-1]:
        rest = jnp.floor((value + 0.5) * (1.0 / size))
        out.append(value - rest * size)
        value = rest
    return out[::-1]


def lagrange(at, source):
    product = choose(source, SCALES)
    for number, point in enumerate(POINTS):
        product = product * jnp.where(source == number, 1.0, at - point)
    return product


def mixing_tables(mix_ref, raw_ref):
    shape = (HALF, DEPTH)
    column = lax.broadcasted_iota(jnp.int32, shape, 1).astype(jnp.float32)
    copy, inside = digits(column, 4, PAD)
    row = lax.broadcasted_iota(jnp.int32, shape, 0).astype(jnp.float32)
    t1, t2 = digits(row, CHEB, CHEB)
    second = inside >= 40
    place = inside - jnp.where(second, 40.0, 0.0)
    used = jnp.logical_and(place < HALF, copy < 3)
    s1, s2 = digits(jnp.minimum(place, HALF - 1.0), CHEB, CHEB)
    at1, at2 = choose(t1, POINTS) * 0.5, choose(t2, POINTS) * 0.5
    weights1 = [jnp.where(used, lagrange(q - 0.5 + at1, s1), 0.0) for q in range(2)]
    weights2 = [lagrange(q - 0.5 + at2, s2) for q in range(2)]
    for q1 in range(2):
        for q2 in range(2):
            weights = weights1[q1] * weights2[q2]
            turns1, turns2 = 0.5 * (q1 + 0.5 + at1), 0.5 * (q2 + 0.5 + at2)
            plus, minus = unit(turns1 + turns2), unit(turns1 - turns2)
            for c1 in range(2):
                for c2 in range(2):
                    co, si = plus if c1 == c2 else minus
                    si = si if c1 else -si
                    real, imag = co * weights, si * weights
                    for part, values in enumerate((jnp.where(second, -imag, real), jnp.where(second, real, imag))):
                        high = values.astype(jnp.bfloat16).astype(jnp.float32)
                        values = jnp.where(copy < 2, high, values - high)
                        base = part * TERMS + q1 * ROWS + q2 * HALF
                        raw_ref[2 * c1 + c2, base : base + HALF, :] = values

    shape = (48, DEPTH)
    copy, inside = digits(lax.broadcasted_iota(jnp.int32, shape, 1).astype(jnp.float32), 4, PAD)

    def variants(i, carry):
        table, rows = lax.div(i, 6), pl.ds(pl.multiple_of(48 * lax.rem(i, 6), 16), 48)
        values = raw_ref[table, rows, :]
        dense = jnp.where(inside < HALF, values, pltpu.roll(values, DEPTH - 4, 1))
        dense = jnp.where(inside < ROWS, dense, 0.0)
        for variant, block in enumerate((dense, values, pltpu.roll(values, 4, 1))):
            mix_ref[4 * variant + table, rows, :] = block.astype(jnp.bfloat16)
        return carry

    lax.fori_loop(0, 24, variants, 0)


def reverse6(value):
    total = 0
    for bit in range(6):
        total = total + lax.rem(lax.div(value, 1 << bit), 2) * (1 << (5 - bit))
    return total


def kernel(
    coef_hbm, slow_hbm, out_ref,
    coef_ref, slow_ref, mix_ref, raw_ref,
    sbuf, xin, s0, z1, zr, s2, obuf, orecv, vtab, e_tab, y_a, y_b, acc_a, acc_b,
    load, in_send, in_recv, sib_send, sib_recv, out_send, out_recv,
):
    bx, by = lax.axis_index("bx"), lax.axis_index("by")
    my_z, my_x = lax.div(bx, 4), lax.rem(bx, 4)
    my_y, core = lax.div(by, 2), lax.rem(by, 2)
    my_x0 = lax.rem(my_x, 2)
    chip = bx * 4 + my_y
    low1 = reverse6(chip) * 16

    loads = [
        pltpu.make_async_copy(src, dst, load.at[i])
        for i, (src, dst) in enumerate(
            ((coef_hbm, coef_ref), (slow_hbm, slow_ref))
        )
    ]
    for copy in loads:
        copy.start()

    barrier = pltpu.get_barrier_semaphore()
    me = bx * 8 + by

    def greet(i, carry):
        there = lax.rem(me + i, 128)
        pl.semaphore_signal(barrier, inc=1, device_id=(lax.div(there, 8), lax.rem(there, 8)), device_id_type=MESH)
        return carry

    lax.fori_loop(1, 128, greet, 0)
    loads[0].wait()

    def gather_rows(ell, carry):
        for tile in range(9):
            sbuf[ell, 8 * tile : 8 * tile + 8, :] = coef_ref[pl.ds(tile * 512 + ell, 8, stride=64), :]
        return carry

    lax.fori_loop(0, 64, gather_rows, 0, unroll=8)
    pl.semaphore_wait(barrier, 127)

    def send_in(step, carry):
        half, inner = lax.div(step, 32), lax.rem(step, 32)
        dx, group = lax.rem(inner, 4), lax.div(inner, 4)
        dy = lax.rem(dx + group, 4)
        dz = half + 2 * lax.rem(lax.div(group, 4) + dx, 2)
        dx, dz, dy = [lax.rem(d + 2 * core, 4) for d in (dx, dz, dy)]
        to_x, to_z, to_y = lax.rem(my_x + dx, 4), lax.rem(my_z + dz, 4), lax.rem(my_y + dy, 4)
        to_bx, to_by = to_z * 4 + to_x, to_y * 2 + my_x0
        ell = to_z * 16 + to_x * 4 + to_y
        src = sbuf.at[ell]
        dst = xin.at[lax.div(dx, 2), core, my_z, my_y]
        here = jnp.logical_and(to_bx == bx, to_by == by)

        @pl.when(here)
        def _():
            pltpu.make_async_copy(src, dst, in_recv.at[half]).start()

        @pl.when(jnp.logical_not(here))
        def _():
            pltpu.make_async_remote_copy(
                src_ref=src, dst_ref=dst, send_sem=in_send, recv_sem=in_recv.at[half],
                device_id=(to_bx, to_by), device_id_type=MESH,
            ).start()

        return carry

    lax.fori_loop(0, 64, send_in, 0)

    loads[1].wait()
    lane = lax.broadcasted_iota(jnp.int32, (TERMS, 96), 1).astype(jnp.float32)
    row = lax.broadcasted_iota(jnp.int32, (TERMS, 96), 0).astype(jnp.float32)
    q1, q2, t1, t2 = digits(row, 2, 2, CHEB, CHEB)
    row_i, row_j = CHEB * q1 + t1, CHEB * q2 + t2

    def spread(level, a1):
        pick = jnp.where(row_i + (12 * a1).astype(jnp.float32) == lane, 1.0, 0.0)
        return jnp.dot(pick, slow_ref[level], precision=lax.Precision.HIGHEST, preferred_element_type=jnp.float32)

    def column(table, a2):
        picked = jnp.where(row_j + (12 * a2).astype(jnp.float32) == lane, table, 0.0)
        return jnp.broadcast_to(jnp.sum(picked, axis=1, keepdims=True), (TERMS, LANES))

    zero, one = jnp.int32(0), jnp.int32(1)
    vtab[0] = column(spread(0, zero), zero)

    def fill1(a1, carry):
        table = spread(1, a1)
        for a2 in range(2):
            vtab[1 + 2 * a1 + a2] = column(table, a2 * one)
        return carry

    lax.fori_loop(0, 2, fill1, 0)

    def fill2(z, carry):
        table = spread(2, z)
        for a2 in range(2):
            vtab[5 + 2 * z + a2] = column(table, 2 * a2 + core)
        return carry

    lax.fori_loop(0, 4, fill2, 0)
    left_rows = lax.broadcasted_iota(jnp.int32, (TERMS, LANES), 1) < 64

    def fill3(a1, carry):
        table = spread(3, a1)
        for a2 in range(2):
            box = 2 * (2 * a2 + core)
            vtab[13 + 2 * a1 + a2] = jnp.where(left_rows, column(table, box), column(table, box + 1))
        return carry

    lax.fori_loop(0, 8, fill3, 0)

    lanes = lax.broadcasted_iota(jnp.int32, (8, LANES), 1)
    low2 = reverse6(lax.rem(lanes, 64)) * 16
    lane2 = lax.div(lanes, 64) * 8 + low2
    back = 127 - lanes
    back_half = lax.div(lanes, 64) * 64 + 63 - lax.rem(lanes, 64)

    def permute(block, index):
        rows = [
            jnp.take_along_axis(block[8 * i : 8 * i + 8], index, axis=1, mode="promise_in_bounds")
            for i in range(block.shape[0] // 8)
        ]
        return jnp.concatenate(rows, axis=0)

    def magnitude(level, r1, c1, r2, c2):
        width = 2.0 ** (level + 1)
        k = (lax.div(r1, 1 << level).astype(jnp.float32) + 0.5) * width - N / 2
        step = (c1 - 0.5) * width
        k0 = k - step
        k2 = (lax.div(r2, jnp.full(r2.shape, 1 << level, jnp.int32)).astype(jnp.float32) + 0.5) * width - N / 2
        step2 = (c2 - 0.5) * width
        k20 = k2 - step2
        above = step * (k + k0) + step2 * (k2 + k20)
        return above / (jnp.sqrt(k * k + k2 * k2) + jnp.sqrt(k0 * k0 + k20 * k20))

    def interpolate(y_ref, child, table, blocks):
        y_ref[child] = jnp.dot(
            mix_ref[table], operand(jnp.concatenate(blocks, axis=1)), preferred_element_type=jnp.float32
        )

    def tiles(body):
        def tile(i, carry):
            body(i, pl.ds(pl.multiple_of(8 * i, 8), 8), pl.ds(pl.multiple_of(8 * i + TERMS, 8), 8))
            return carry

        lax.fori_loop(0, TERMS // 8, tile, 0, unroll=True)

    def added(total, co, si, y_ref, child, at, at_im, side):
        cols = pl.ds(side * LANES, LANES)
        y_re, y_im = y_ref[child, at, cols], y_ref[child, at_im, cols]
        re, im = co * y_re - si * y_im, co * y_im + si * y_re
        return (re, im) if total is None else (total[0] + re, total[1] + im)

    def exponentials(entry, slots, sizes):
        def tile(i, carry):
            at = pl.ds(pl.multiple_of(8 * i, 8), 8)
            for j in range(4):
                co, si = unit(vtab[slots[j], at, :] * sizes[j])
                e_tab[entry, j, 0, at, :] = co
                e_tab[entry, j, 1, at, :] = si
            return carry

        lax.fori_loop(0, TERMS // 8, tile, 0, unroll=3)

    def combine_cores(y_ref, dst, entry):
        def body(i, at, at_im):
            totals = [None, None]
            for c1 in range(2):
                for c2 in range(2):
                    co, si = e_tab[entry, 2 * c1 + c2, 0, at, :], e_tab[entry, 2 * c1 + c2, 1, at, :]
                    totals[0] = added(totals[0], co, si, y_ref, 2 * c1 + c2, at, at_im, 0)
                    totals[1] = added(totals[1], co, si, y_ref, 2 * c1 + 1 - c2, at, at_im, 1)
            for side in range(2):
                put(dst[side], i, totals[side])

        tiles(body)

    def combine_mirrored(y_ref, dst, entry, index):
        def body(i, at, at_im):
            for side in range(2):
                totals = [None, None]
                for c1 in range(2):
                    co, si = e_tab[entry, 2 * c1 + side, 0, at, :], e_tab[entry, 2 * c1 + side, 1, at, :]
                    for c2 in range(2):
                        totals[c2] = added(totals[c2], co, si, y_ref, 2 * c1 + c2, at, at_im, side)
                put(dst[side], i, [totals[0][part] + permute(totals[1][part], index) for part in range(2)])

        tiles(body)

    def put(dst, i, total):
        rows = pl.ds(pl.multiple_of(8 * lax.rem(i, 9), 8), 8)
        for part in range(2):
            dst[2 * part + lax.div(i, 9), rows, :] = total[part]

    def window(src, q1, q2):
        rows = pl.ds(pl.multiple_of(32 * q2, 8), 40)
        return jnp.concatenate([src[q1, rows, :], src[2 + q1, rows, :]], axis=0)

    pairs = ((0, y_a, acc_a), (1, y_b, acc_b))

    def x_of(slot):
        dx = 2 * slot + lax.rem(my_x + core, 2)
        x = lax.rem(my_x - dx + 4, 4)
        return lax.div(x, 2), low1 + 4 * lax.div(x, 2) + 8 * core

    def box_of(box):
        other1 = 1 - lax.rem(box, 2)
        other2 = 1 - lax.rem(lax.rem(box, 2) + lax.div(box, 2), 2)
        return lax.rem(lax.div(my_z, 2) + other1, 2), lax.rem(lax.div(my_y, 2) + other2, 2)

    def turn_of(step, on_core):
        return step + on_core * (1 - 2 * lax.rem(step, 2))

    children = [(c1, c2) for c1 in range(2) for c2 in range(2)]

    def phases0(part, carry):
        z0, y0 = lax.rem(my_z + lax.div(part, 2), 2), lax.rem(part, 2)
        for slot in range(2):
            r1 = x_of(slot)[1] + 2 * z0
            sizes = [magnitude(0, r1 + c1, c1, lane2 + (c2 + 2 * y0), c2) for c1, c2 in children]
            exponentials(2 * part + slot, (0,) * 4, sizes)
        return carry

    def phases1(step, carry):
        a1, a2 = box_of(step)
        for slot in range(2):
            r1 = x_of(slot)[1]
            sizes = [magnitude(1, r1 + 2 * c1, c1, lane2 + 2 * c2, c2) for c1, c2 in children]
            exponentials(8 + 2 * step + slot, (1 + 2 * a1 + a2,) * 4, sizes)
        return carry

    def phases2(step, carry):
        a1, a2 = box_of(step)
        sizes = [
            magnitude(2, low1 + 4 * c1 + 8 * x0, c1, lane2, 0) for c1 in range(2) for x0 in (core, 1 - core)
        ]
        for z0 in range(2):
            exponentials(16 + 2 * step + z0, (5 + 2 * (2 * a1 + z0) + a2,) * 4, sizes)
        return carry

    def phases3(step, carry):
        a1, a2 = box_of(step)
        sizes = [magnitude(3, low1 + 8 * c1, c1, low2, 0) for c1 in range(2) for side in range(2)]
        for z0 in range(2):
            slot = 13 + 4 * (2 * a1 + z0) + a2
            exponentials(24 + 2 * step + z0, (slot, slot + 2, slot, slot + 2), sizes)
        return carry

    def level0(part, carry):
        z0, y0 = lax.rem(my_z + lax.div(part, 2), 2), lax.rem(part, 2)
        for slot, y_ref, _ in pairs:
            for c1, c2 in children:
                z = 2 * c1 + z0
                first = xin[slot, 0, z, 2 * c2 + y0]
                second = permute(xin[slot, 1, z, 2 * c2 + 1 - y0], back)
                interpolate(y_ref, 2 * c1 + c2, 2 * c1 + c2, [first, second])
        for slot, y_ref, _ in pairs:
            combine_cores(y_ref, (s0.at[slot, z0, y0, 0], s0.at[slot, z0, 1 - y0, 1]), 2 * part + slot)
        return carry

    mixing_tables(mix_ref, raw_ref)
    for phases in (phases0, phases1, phases2):
        lax.fori_loop(0, 4, phases, 0)

    def arrived(half, carry):
        pltpu.make_async_copy(xin.at[0], xin.at[0], in_recv.at[half]).wait()
        lax.fori_loop(2 * half, 2 * half + 2, level0, 0)

        @pl.when(half == 0)
        def _():
            lax.fori_loop(0, 4, phases3, 0)

        return carry

    lax.fori_loop(0, 2, arrived, 0)

    def level1(step):
        a1, a2 = box_of(step)
        for slot, y_ref, _ in pairs:
            for c1, c2 in children:
                blocks = [window(s0.at[slot, c1, c2, side], a1, a2) for side in range(2)]
                interpolate(y_ref, 2 * c1 + c2, 4 + 4 * a2 + 2 * c1 + c2, blocks)
        for slot, y_ref, _ in pairs:
            x1 = x_of(slot)[0]
            combine_cores(y_ref, (z1.at[step, x1, 0], z1.at[step, x1, 1]), 8 + 2 * step + slot)
        pltpu.make_async_remote_copy(
            src_ref=z1.at[step, :, :, :, pl.ds(pl.multiple_of(32 * (1 - core), 8), 40), :],
            dst_ref=zr.at[step],
            send_sem=sib_send.at[step],
            recv_sem=sib_recv.at[step],
            device_id=(bx, my_y * 2 + 1 - core),
            device_id_type=MESH,
        ).start()

    left = lax.broadcasted_iota(jnp.int32, (PAD, LANES), 1) < 64
    left_half = lax.broadcasted_iota(jnp.int32, (HALF, LANES), 1) < 64

    def level23(step):
        a1, a2 = box_of(step)
        y = 2 * a2 + core
        pltpu.make_async_copy(zr.at[0], zr.at[0], sib_recv.at[step]).wait()
        near_z0 = lax.rem(my_z, 2)
        z0_of = (near_z0, 1 - near_z0)
        for i, y_ref, _ in pairs:
            z0 = z0_of[i]
            for c1, c2 in children:
                other = zr.at[step, c1, c2]
                blocks = [
                    window(z1.at[step, c1, c2], z0, core),
                    jnp.concatenate([other[z0], other[2 + z0]], axis=0),
                ]
                interpolate(y_ref, 2 * c1 + c2, 4 + 4 * core + 2 * c1 + c2, blocks)
        for i, y_ref, _ in pairs:
            combine_mirrored(y_ref, (s2.at[i, 0], s2.at[i, 1]), 16 + 2 * step + z0_of[i], back)
        for i, y_ref, _ in pairs:
            for c1 in range(2):
                src = s2.at[i, lax.rem(c1 + core, 2)]
                near, far = [], []
                for x1 in range(2):
                    first = window(src, x1, 0)
                    second = window(src, x1, 1)
                    second = jnp.concatenate([second[4:40], second[36:40], second[44:80], second[76:80]], axis=0)
                    near.append(jnp.where(left, first, pltpu.roll(second, 64, 1)))
                    far.append(jnp.where(left, permute(first, back), permute(second, back_half)))
                interpolate(y_ref, 2 * c1, 4 + 2 * c1, near)
                interpolate(y_ref, 2 * c1 + 1, 4 + 2 * c1 + 1, far)
        for i, y_ref, acc_ref in pairs:
            z0 = z0_of[i]
            z = 2 * a1 + z0
            combine_mirrored(y_ref, (acc_ref.at[0], acc_ref.at[1]), 24 + 2 * step + z0, back_half)
            for x1 in range(2):
                for q1 in range(2):
                    for part in range(2):
                        upper = acc_ref[x1, 2 * part + q1, 0:HALF, :]
                        lower = acc_ref[x1, 2 * part + q1, HALF:ROWS, :]
                        rows = pl.ds(HALF * part, HALF)
                        obuf[step, i, x1, q1, 0, rows, :] = jnp.where(left_half, upper, pltpu.roll(lower, 64, 1))
                        obuf[step, i, x1, q1, 1, rows, :] = jnp.where(left_half, pltpu.roll(upper, 64, 1), lower)

            def send_out(target, carry, z=z, i=i):
                hop = lax.div(target, 2)
                x = lax.rem(my_x + 5 + 2 * core + hop, 4)
                c = lax.rem(target + core, 2)
                to_bx, to_by = z * 4 + x, 2 * y + c
                src, dst = obuf.at[step, i, lax.div(x, 2), lax.rem(x, 2), c], orecv.at[chip]
                here = jnp.logical_and(to_bx == bx, to_by == by)

                @pl.when(here)
                def _():
                    pltpu.make_async_copy(src, dst, out_recv.at[step]).start()

                @pl.when(jnp.logical_not(here))
                def _():
                    pltpu.make_async_remote_copy(
                        src_ref=src, dst_ref=dst, send_sem=out_send, recv_sem=out_recv.at[step],
                        device_id=(to_bx, to_by), device_id_type=MESH,
                    ).start()

                return carry

            lax.fori_loop(0, 8, send_out, 0)

    def both(step, carry):
        @pl.when(step < 4)
        def _():
            level1(step)

        @pl.when(step > 0)
        def _():
            level23(turn_of(step - 1, core))

        return carry

    lax.fori_loop(0, 5, both, 0)

    def settle(step, carry):
        pltpu.make_async_copy(zr.at[0], zr.at[0], sib_send.at[step]).wait()
        return carry

    lax.fori_loop(0, 4, settle, 0)
    for keeps, sem in ((my_x0 == core, in_send), (lax.rem(my_y, 2) == core, out_send)):

        @pl.when(keeps)
        def _(sem=sem):
            pltpu.make_async_copy(sbuf.at[pl.ds(0, 63)], sbuf.at[pl.ds(0, 63)], sem).wait()

        @pl.when(jnp.logical_not(keeps))
        def _(sem=sem):
            pltpu.make_async_copy(sbuf, sbuf, sem).wait()

    def arrive(step, carry):
        box = turn_of(step, lax.rem(my_y, 2))
        pltpu.make_async_copy(orecv.at[pl.ds(0, 16)], orecv.at[pl.ds(0, 16)], out_recv.at[box]).wait()
        z1_from, y1_from = box_of(box)

        def scatter_rows(i, carry):
            z, x, y = 2 * z1_from + lax.div(i, 8), lax.rem(lax.div(i, 2), 4), 2 * y1_from + lax.rem(i, 2)
            ell = z * 16 + x * 4 + y
            for tile in range(9):
                out_ref[pl.ds(tile * 512 + ell, 8, stride=64), :] = orecv[ell, 8 * tile : 8 * tile + 8, :]
            return carry

        lax.fori_loop(0, 16, scatter_rows, 0, unroll=4)
        return carry

    lax.fori_loop(0, 4, arrive, 0)


def shards(coefficients, slowness):
    rows = jnp.transpose(coefficients, (0, 1, 3, 2, 4)).reshape(ROWS * 64, LANES)
    operands = (rows, slowness)
    dense = (ROWS, LANES)
    scratch = [pltpu.VMEM(operands[i].shape, jnp.float32) for i in range(2)]
    scratch += [pltpu.VMEM((12, 2 * TERMS, DEPTH), jnp.bfloat16), pltpu.VMEM((4, 2 * TERMS, DEPTH), jnp.float32)]
    scratch += [
        pltpu.VMEM(shape, jnp.float32)
        for shape in (
            (64,) + dense,
            (2, 2, 4, 4) + dense,
            (2, 2, 2, 2, 4) + dense,
            (4, 2, 2, 4) + dense,
            (4, 2, 2, 4, 40, LANES),
            (2, 2, 4) + dense,
            (4, 2, 2, 2, 2) + dense,
            (64,) + dense,
            (29, TERMS, LANES),
            (32, 4, 2, TERMS, LANES),
            (4, 2 * TERMS, 2 * LANES),
            (4, 2 * TERMS, 2 * LANES),
            (2, 4) + dense,
            (2, 4) + dense,
        )
    ]
    scratch += [
        pltpu.SemaphoreType.DMA((4,)),
        pltpu.SemaphoreType.DMA,
        pltpu.SemaphoreType.DMA((2,)),
        pltpu.SemaphoreType.DMA((4,)),
        pltpu.SemaphoreType.DMA((4,)),
        pltpu.SemaphoreType.DMA,
        pltpu.SemaphoreType.DMA((4,)),
    ]
    out = pl.pallas_call(
        kernel,
        out_shape=jax.ShapeDtypeStruct((ROWS * 64, LANES), jnp.float32),
        in_specs=[pl.BlockSpec(memory_space=pl.ANY)] * 2,
        out_specs=pl.BlockSpec(memory_space=pltpu.VMEM),
        scratch_shapes=scratch,
        compiler_params=pltpu.CompilerParams(collective_id=0, has_side_effects=True, vmem_limit_bytes=50 << 20),
    )(*operands)
    return jnp.transpose(out.reshape(2, CHEB, CHEB, 64, LANES), (0, 1, 3, 2, 4))


def solution(mesh):
    placed = (P(None, None, "bx", None, "by"), P())
    return jax.shard_map(
        shards,
        mesh=mesh,
        in_specs=placed,
        out_specs=P(None, None, "bx", None, "by"),
        check_vma=False,
    )
```

```python
import math

import jax
import jax.numpy as jnp
import numpy as np
from jax import lax
from jax.experimental import pallas as pl
from jax.experimental.pallas import tpu as pltpu
from jax.sharding import PartitionSpec as P

N = 2048
CHEB = 6
HALF = CHEB * CHEB
ROWS = 2 * HALF
TERMS = 4 * HALF
PAD = 80
DEPTH = 256
LANES = 128
MESH = pl.DeviceIdType.MESH


def cheb_points():
    return np.cos(np.pi * (2 * np.arange(CHEB) + 1) / (2 * CHEB))


def fit(function, degree):
    count = 200
    s = 0.125 * (1 + np.cos(np.pi * (2 * np.arange(count) + 1) / (2 * count)))
    series = np.polynomial.chebyshev.Chebyshev.fit(s, function(np.sqrt(s)), degree, domain=[0, 0.25])
    return [float(c) for c in series.convert(kind=np.polynomial.Polynomial).coef]


SIN = fit(lambda r: math.sqrt(2) * np.sin(np.pi * r) / r, 3)
COS = fit(lambda r: math.sqrt(2) * np.cos(np.pi * r), 4)
WHOLE = 1.5 * 2.0**23


POINTS = [float(point) for point in cheb_points()]
SCALES = [
    float(1 / np.prod([cheb_points()[s] - cheb_points()[j] for j in range(CHEB) if j != s])) for s in range(CHEB)
]


def horner(coefficients, s):
    value = s * coefficients[-1] + coefficients[-2]
    for coefficient in coefficients[-3::-1]:
        value = value * s + coefficient
    return value


def unit(turns):
    r = turns - ((turns + WHOLE) - WHOLE)
    s = r * r
    half = horner(SIN, s) * r
    return 1.0 - half * half, half * horner(COS, s)


def operand(block):
    if block.shape[0] < PAD:
        block = jnp.concatenate([block, jnp.zeros((PAD - block.shape[0], block.shape[1]), jnp.float32)], axis=0)
    high = block.astype(jnp.bfloat16)
    low = (block - high.astype(jnp.float32)).astype(jnp.bfloat16)
    return jnp.concatenate([high, low, high, jnp.zeros((DEPTH - 3 * PAD, block.shape[1]), jnp.bfloat16)], axis=0)


def choose(index, values):
    result = jnp.full(index.shape, values[0], jnp.float32)
    for number, value in enumerate(values[1:], 1):
        result = jnp.where(index == number, value, result)
    return result


def digits(value, *sizes):
    out = []
    for size in sizes[::-1]:
        rest = jnp.floor((value + 0.5) * (1.0 / size))
        out.append(value - rest * size)
        value = rest
    return out[::-1]


def lagrange(at, source):
    product = choose(source, SCALES)
    for number, point in enumerate(POINTS):
        product = product * jnp.where(source == number, 1.0, at - point)
    return product


def mixing_tables(mix_ref, raw_ref):
    shape = (HALF, DEPTH)
    column = lax.broadcasted_iota(jnp.int32, shape, 1).astype(jnp.float32)
    copy, inside = digits(column, 4, PAD)
    row = lax.broadcasted_iota(jnp.int32, shape, 0).astype(jnp.float32)
    t1, t2 = digits(row, CHEB, CHEB)
    second = inside >= 40
    place = inside - jnp.where(second, 40.0, 0.0)
    used = jnp.logical_and(place < HALF, copy < 3)
    s1, s2 = digits(jnp.minimum(place, HALF - 1.0), CHEB, CHEB)
    at1, at2 = choose(t1, POINTS) * 0.5, choose(t2, POINTS) * 0.5
    weights1 = [jnp.where(used, lagrange(q - 0.5 + at1, s1), 0.0) for q in range(2)]
    weights2 = [lagrange(q - 0.5 + at2, s2) for q in range(2)]
    for q1 in range(2):
        for q2 in range(2):
            weights = weights1[q1] * weights2[q2]
            turns1, turns2 = 0.5 * (q1 + 0.5 + at1), 0.5 * (q2 + 0.5 + at2)
            plus, minus = unit(turns1 + turns2), unit(turns1 - turns2)
            for c1 in range(2):
                for c2 in range(2):
                    co, si = plus if c1 == c2 else minus
                    si = si if c1 else -si
                    real, imag = co * weights, si * weights
                    for part, values in enumerate((jnp.where(second, -imag, real), jnp.where(second, real, imag))):
                        high = values.astype(jnp.bfloat16).astype(jnp.float32)
                        values = jnp.where(copy < 2, high, values - high)
                        base = part * TERMS + q1 * ROWS + q2 * HALF
                        raw_ref[2 * c1 + c2, base : base + HALF, :] = values

    shape = (48, DEPTH)
    copy, inside = digits(lax.broadcasted_iota(jnp.int32, shape, 1).astype(jnp.float32), 4, PAD)

    def variants(i, carry):
        table, rows = lax.div(i, 6), pl.ds(pl.multiple_of(48 * lax.rem(i, 6), 16), 48)
        values = raw_ref[table, rows, :]
        dense = jnp.where(inside < HALF, values, pltpu.roll(values, DEPTH - 4, 1))
        dense = jnp.where(inside < ROWS, dense, 0.0)
        for variant, block in enumerate((dense, values, pltpu.roll(values, 4, 1))):
            mix_ref[4 * variant + table, rows, :] = block.astype(jnp.bfloat16)
        return carry

    lax.fori_loop(0, 24, variants, 0)


def reverse6(value):
    total = 0
    for bit in range(6):
        total = total + lax.rem(lax.div(value, 1 << bit), 2) * (1 << (5 - bit))
    return total


def kernel(
    coef_hbm, slow_hbm, out_ref,
    coef_ref, slow_ref, mix_ref, raw_ref,
    sbuf, xin, s0, z1, zr, s2, obuf, orecv, vtab, e_tab, y_a, y_b, acc_a, acc_b,
    load, in_send, in_recv, sib_send, sib_recv, out_send, out_recv,
):
    bx, by = lax.axis_index("bx"), lax.axis_index("by")
    my_z, my_x = lax.div(bx, 4), lax.rem(bx, 4)
    my_y, core = lax.div(by, 2), lax.rem(by, 2)
    my_x0 = lax.rem(my_x, 2)
    chip = bx * 4 + my_y
    low1 = reverse6(chip) * 16

    loads = [
        pltpu.make_async_copy(src, dst, load.at[i])
        for i, (src, dst) in enumerate(
            ((coef_hbm, coef_ref), (slow_hbm, slow_ref))
        )
    ]
    for copy in loads:
        copy.start()

    barrier = pltpu.get_barrier_semaphore()
    me = bx * 8 + by

    def greet(i, carry):
        there = lax.rem(me + i, 128)
        pl.semaphore_signal(barrier, inc=1, device_id=(lax.div(there, 8), lax.rem(there, 8)), device_id_type=MESH)
        return carry

    lax.fori_loop(1, 121, greet, 0, unroll=8)
    lax.fori_loop(121, 128, greet, 0, unroll=7)
    loads[0].wait()

    def gather_rows(ell, carry):
        for tile in range(9):
            sbuf[ell, 8 * tile : 8 * tile + 8, :] = coef_ref[pl.ds(tile * 512 + ell, 8, stride=64), :]
        return carry

    lax.fori_loop(0, 64, gather_rows, 0, unroll=8)
    pl.semaphore_wait(barrier, 127)

    def send_in(step, carry):
        half, inner = lax.div(step, 32), lax.rem(step, 32)
        dx, group = lax.rem(inner, 4), lax.div(inner, 4)
        dy = lax.rem(dx + group, 4)
        dz = half + 2 * lax.rem(lax.div(group, 4) + dx, 2)
        dx, dz, dy = [lax.rem(d + 2 * core, 4) for d in (dx, dz, dy)]
        to_x, to_z, to_y = lax.rem(my_x + dx, 4), lax.rem(my_z + dz, 4), lax.rem(my_y + dy, 4)
        to_bx, to_by = to_z * 4 + to_x, to_y * 2 + my_x0
        ell = to_z * 16 + to_x * 4 + to_y
        src = sbuf.at[ell]
        dst = xin.at[lax.div(dx, 2), core, my_z, my_y]
        here = jnp.logical_and(to_bx == bx, to_by == by)

        @pl.when(here)
        def _():
            pltpu.make_async_copy(src, dst, in_recv.at[half]).start()

        @pl.when(jnp.logical_not(here))
        def _():
            pltpu.make_async_remote_copy(
                src_ref=src, dst_ref=dst, send_sem=in_send, recv_sem=in_recv.at[half],
                device_id=(to_bx, to_by), device_id_type=MESH,
            ).start()

        return carry

    lax.fori_loop(0, 64, send_in, 0)

    loads[1].wait()
    lane = lax.broadcasted_iota(jnp.int32, (TERMS, 96), 1).astype(jnp.float32)
    row = lax.broadcasted_iota(jnp.int32, (TERMS, 96), 0).astype(jnp.float32)
    q1, q2, t1, t2 = digits(row, 2, 2, CHEB, CHEB)
    row_i, row_j = CHEB * q1 + t1, CHEB * q2 + t2

    def spread(level, a1):
        pick = jnp.where(row_i + (12 * a1).astype(jnp.float32) == lane, 1.0, 0.0)
        return jnp.dot(pick, slow_ref[level], precision=lax.Precision.HIGHEST, preferred_element_type=jnp.float32)

    def column(table, a2):
        picked = jnp.where(row_j + (12 * a2).astype(jnp.float32) == lane, table, 0.0)
        return jnp.broadcast_to(jnp.sum(picked, axis=1, keepdims=True), (TERMS, LANES))

    zero, one = jnp.int32(0), jnp.int32(1)
    vtab[0] = column(spread(0, zero), zero)

    def fill1(a1, carry):
        table = spread(1, a1)
        for a2 in range(2):
            vtab[1 + 2 * a1 + a2] = column(table, a2 * one)
        return carry

    lax.fori_loop(0, 2, fill1, 0)

    def fill2(z, carry):
        table = spread(2, z)
        for a2 in range(2):
            vtab[5 + 2 * z + a2] = column(table, 2 * a2 + core)
        return carry

    lax.fori_loop(0, 4, fill2, 0)
    left_rows = lax.broadcasted_iota(jnp.int32, (TERMS, LANES), 1) < 64

    def fill3(a1, carry):
        table = spread(3, a1)
        for a2 in range(2):
            box = 2 * (2 * a2 + core)
            vtab[13 + 2 * a1 + a2] = jnp.where(left_rows, column(table, box), column(table, box + 1))
        return carry

    lax.fori_loop(0, 8, fill3, 0)

    lanes = lax.broadcasted_iota(jnp.int32, (8, LANES), 1)
    low2 = reverse6(lax.rem(lanes, 64)) * 16
    lane2 = lax.div(lanes, 64) * 8 + low2
    back = 127 - lanes
    back_half = lax.div(lanes, 64) * 64 + 63 - lax.rem(lanes, 64)

    def permute(block, index):
        rows = [
            jnp.take_along_axis(block[8 * i : 8 * i + 8], index, axis=1, mode="promise_in_bounds")
            for i in range(block.shape[0] // 8)
        ]
        return jnp.concatenate(rows, axis=0)

    def magnitude(level, r1, c1, r2, c2):
        width = 2.0 ** (level + 1)
        k = (lax.div(r1, 1 << level).astype(jnp.float32) + 0.5) * width - N / 2
        step = (c1 - 0.5) * width
        k0 = k - step
        k2 = (lax.div(r2, jnp.full(r2.shape, 1 << level, jnp.int32)).astype(jnp.float32) + 0.5) * width - N / 2
        step2 = (c2 - 0.5) * width
        k20 = k2 - step2
        above = step * (k + k0) + step2 * (k2 + k20)
        return above / (jnp.sqrt(k * k + k2 * k2) + jnp.sqrt(k0 * k0 + k20 * k20))

    def interpolate(y_ref, child, table, blocks):
        y_ref[child] = jnp.dot(
            mix_ref[table], operand(jnp.concatenate(blocks, axis=1)), preferred_element_type=jnp.float32
        )

    def tiles(body):
        def tile(i, carry):
            body(i, pl.ds(pl.multiple_of(8 * i, 8), 8), pl.ds(pl.multiple_of(8 * i + TERMS, 8), 8))
            return carry

        lax.fori_loop(0, TERMS // 8, tile, 0, unroll=True)

    def added(total, co, si, y_ref, child, at, at_im, side):
        cols = pl.ds(side * LANES, LANES)
        y_re, y_im = y_ref[child, at, cols], y_ref[child, at_im, cols]
        re, im = co * y_re - si * y_im, co * y_im + si * y_re
        return (re, im) if total is None else (total[0] + re, total[1] + im)

    def exponentials(entry, slots, sizes):
        def tile(i, carry):
            at = pl.ds(pl.multiple_of(8 * i, 8), 8)
            for j in range(4):
                co, si = unit(vtab[slots[j], at, :] * sizes[j])
                e_tab[entry, j, 0, at, :] = co
                e_tab[entry, j, 1, at, :] = si
            return carry

        lax.fori_loop(0, TERMS // 8, tile, 0, unroll=3)

    def combine_cores(y_ref, dst, entry):
        def body(i, at, at_im):
            totals = [None, None]
            for c1 in range(2):
                for c2 in range(2):
                    co, si = e_tab[entry, 2 * c1 + c2, 0, at, :], e_tab[entry, 2 * c1 + c2, 1, at, :]
                    totals[0] = added(totals[0], co, si, y_ref, 2 * c1 + c2, at, at_im, 0)
                    totals[1] = added(totals[1], co, si, y_ref, 2 * c1 + 1 - c2, at, at_im, 1)
            for side in range(2):
                put(dst[side], i, totals[side])

        tiles(body)

    def combine_mirrored(y_ref, dst, entry, index):
        def body(i, at, at_im):
            for side in range(2):
                totals = [None, None]
                for c1 in range(2):
                    co, si = e_tab[entry, 2 * c1 + side, 0, at, :], e_tab[entry, 2 * c1 + side, 1, at, :]
                    for c2 in range(2):
                        totals[c2] = added(totals[c2], co, si, y_ref, 2 * c1 + c2, at, at_im, side)
                put(dst[side], i, [totals[0][part] + permute(totals[1][part], index) for part in range(2)])

        tiles(body)

    def put(dst, i, total):
        rows = pl.ds(pl.multiple_of(8 * lax.rem(i, 9), 8), 8)
        for part in range(2):
            dst[2 * part + lax.div(i, 9), rows, :] = total[part]

    def window(src, q1, q2):
        rows = pl.ds(pl.multiple_of(32 * q2, 8), 40)
        return jnp.concatenate([src[q1, rows, :], src[2 + q1, rows, :]], axis=0)

    pairs = ((0, y_a, acc_a), (1, y_b, acc_b))

    def x_of(slot):
        dx = 2 * slot + lax.rem(my_x + core, 2)
        x = lax.rem(my_x - dx + 4, 4)
        return lax.div(x, 2), low1 + 4 * lax.div(x, 2) + 8 * core

    def box_of(box):
        other1 = 1 - lax.rem(box, 2)
        other2 = 1 - lax.rem(lax.rem(box, 2) + lax.div(box, 2), 2)
        return lax.rem(lax.div(my_z, 2) + other1, 2), lax.rem(lax.div(my_y, 2) + other2, 2)

    def order_of(step):
        return step + lax.div(step, 2) * (1 - 2 * lax.rem(step, 2))

    def turn_of(step, on_core):
        return order_of(step + on_core * (1 - 2 * lax.rem(step, 2)))

    children = [(c1, c2) for c1 in range(2) for c2 in range(2)]

    def phases0(part, carry):
        z0, y0 = lax.rem(my_z + lax.div(part, 2), 2), lax.rem(part, 2)
        for slot in range(2):
            r1 = x_of(slot)[1] + 2 * z0
            sizes = [magnitude(0, r1 + c1, c1, lane2 + (c2 + 2 * y0), c2) for c1, c2 in children]
            exponentials(2 * part + slot, (0,) * 4, sizes)
        return carry

    def phases1(step, carry):
        a1, a2 = box_of(step)
        for slot in range(2):
            r1 = x_of(slot)[1]
            sizes = [magnitude(1, r1 + 2 * c1, c1, lane2 + 2 * c2, c2) for c1, c2 in children]
            exponentials(8 + 2 * step + slot, (1 + 2 * a1 + a2,) * 4, sizes)
        return carry

    def phases2(step, carry):
        a1, a2 = box_of(step)
        sizes = [
            magnitude(2, low1 + 4 * c1 + 8 * x0, c1, lane2, 0) for c1 in range(2) for x0 in (core, 1 - core)
        ]
        for z0 in range(2):
            exponentials(16 + 2 * step + z0, (5 + 2 * (2 * a1 + z0) + a2,) * 4, sizes)
        return carry

    def phases3(step, carry):
        a1, a2 = box_of(step)
        sizes = [magnitude(3, low1 + 8 * c1, c1, low2, 0) for c1 in range(2) for side in range(2)]
        for z0 in range(2):
            slot = 13 + 4 * (2 * a1 + z0) + a2
            exponentials(24 + 2 * step + z0, (slot, slot + 2, slot, slot + 2), sizes)
        return carry

    def level0(part, carry):
        z0, y0 = lax.rem(my_z + lax.div(part, 2), 2), lax.rem(part, 2)
        for slot, y_ref, _ in pairs:
            for c1, c2 in children:
                z = 2 * c1 + z0
                first = xin[slot, 0, z, 2 * c2 + y0]
                second = permute(xin[slot, 1, z, 2 * c2 + 1 - y0], back)
                interpolate(y_ref, 2 * c1 + c2, 2 * c1 + c2, [first, second])
        for slot, y_ref, _ in pairs:
            combine_cores(y_ref, (s0.at[slot, z0, y0, 0], s0.at[slot, z0, 1 - y0, 1]), 2 * part + slot)
        return carry

    mixing_tables(mix_ref, raw_ref)
    for phases in (phases0, phases1, phases2):
        lax.fori_loop(0, 4, phases, 0)

    def arrived(half, carry):
        pltpu.make_async_copy(xin.at[0], xin.at[0], in_recv.at[half]).wait()
        lax.fori_loop(2 * half, 2 * half + 2, level0, 0)

        @pl.when(half == 0)
        def _():
            lax.fori_loop(0, 4, phases3, 0)

        return carry

    lax.fori_loop(0, 2, arrived, 0)

    def level1(step):
        a1, a2 = box_of(step)
        for slot, y_ref, _ in pairs:
            for c1, c2 in children:
                blocks = [window(s0.at[slot, c1, c2, side], a1, a2) for side in range(2)]
                interpolate(y_ref, 2 * c1 + c2, 4 + 4 * a2 + 2 * c1 + c2, blocks)
        for slot, y_ref, _ in pairs:
            x1 = x_of(slot)[0]
            combine_cores(y_ref, (z1.at[step, x1, 0], z1.at[step, x1, 1]), 8 + 2 * step + slot)
        pltpu.make_async_remote_copy(
            src_ref=z1.at[step, :, :, :, pl.ds(pl.multiple_of(32 * (1 - core), 8), 40), :],
            dst_ref=zr.at[step],
            send_sem=sib_send.at[step],
            recv_sem=sib_recv.at[step],
            device_id=(bx, my_y * 2 + 1 - core),
            device_id_type=MESH,
        ).start()

    left = lax.broadcasted_iota(jnp.int32, (PAD, LANES), 1) < 64
    left_half = lax.broadcasted_iota(jnp.int32, (HALF, LANES), 1) < 64

    def level23(step):
        pltpu.make_async_copy(zr.at[0], zr.at[0], sib_recv.at[step]).wait()
        near_z0 = lax.rem(my_z, 2)
        z0_of = (near_z0, 1 - near_z0)
        for i, y_ref, _ in pairs:
            z0 = z0_of[i]
            for c1, c2 in children:
                other = zr.at[step, c1, c2]
                blocks = [
                    window(z1.at[step, c1, c2], z0, core),
                    jnp.concatenate([other[z0], other[2 + z0]], axis=0),
                ]
                interpolate(y_ref, 2 * c1 + c2, 4 + 4 * core + 2 * c1 + c2, blocks)
        for i, y_ref, _ in pairs:
            combine_mirrored(y_ref, (s2.at[i, 0], s2.at[i, 1]), 16 + 2 * step + z0_of[i], back)
        for i, y_ref, _ in pairs:
            for c1 in range(2):
                src = s2.at[i, lax.rem(c1 + core, 2)]
                near, far = [], []
                for x1 in range(2):
                    first = window(src, x1, 0)
                    second = window(src, x1, 1)
                    second = jnp.concatenate([second[4:40], second[36:40], second[44:80], second[76:80]], axis=0)
                    near.append(jnp.where(left, first, pltpu.roll(second, 64, 1)))
                    far.append(jnp.where(left, permute(first, back), permute(second, back_half)))
                interpolate(y_ref, 2 * c1, 4 + 2 * c1, near)
                interpolate(y_ref, 2 * c1 + 1, 4 + 2 * c1 + 1, far)
        for i, y_ref, acc_ref in pairs:
            combine_mirrored(y_ref, (acc_ref.at[0], acc_ref.at[1]), 24 + 2 * step + z0_of[i], back_half)
            for x1 in range(2):
                for q1 in range(2):
                    for part in range(2):
                        upper = acc_ref[x1, 2 * part + q1, 0:HALF, :]
                        lower = acc_ref[x1, 2 * part + q1, HALF:ROWS, :]
                        rows = pl.ds(HALF * part, HALF)
                        obuf[step, i, x1, q1, 0, rows, :] = jnp.where(left_half, upper, pltpu.roll(lower, 64, 1))
                        obuf[step, i, x1, q1, 1, rows, :] = jnp.where(left_half, pltpu.roll(upper, 64, 1), lower)

    def send_out(box, number):
        i, hop, later = lax.rem(number, 2), lax.div(number, 2), lax.div(number, 8)
        a1, a2 = box_of(box)
        x = lax.rem(my_x + 1 + 2 * core + hop, 4)
        c = lax.rem(later + core, 2)
        to_bx, to_by = (2 * a1 + lax.rem(my_z + i, 2)) * 4 + x, 2 * (2 * a2 + core) + c
        src, dst = obuf.at[box, i, lax.div(x, 2), lax.rem(x, 2), c], orecv.at[chip]
        here = jnp.logical_and(to_bx == bx, to_by == by)

        @pl.when(here)
        def _():
            pltpu.make_async_copy(src, dst, out_recv.at[box]).start()

        @pl.when(jnp.logical_not(here))
        def _():
            pltpu.make_async_remote_copy(
                src_ref=src, dst_ref=dst, send_sem=out_send, recv_sem=out_recv.at[box],
                device_id=(to_bx, to_by), device_id_type=MESH,
            ).start()

    def both(step, carry):
        @pl.when(step < 4)
        def _():
            level1(order_of(step))

        @pl.when(jnp.logical_and(step > 0, step < 5))
        def _():
            level23(turn_of(step - 1, core))

        def send_some(number, carry):
            @pl.when(jnp.logical_and(step > 0, step < 5))
            def _():
                send_out(turn_of(step - 1, core), number)

            @pl.when(step > 1)
            def _():
                send_out(turn_of(step - 2, core), number + 8)

            return carry

        lax.fori_loop(0, 8, send_some, 0)
        return carry

    lax.fori_loop(0, 6, both, 0)

    def settle(step, carry):
        pltpu.make_async_copy(zr.at[0], zr.at[0], sib_send.at[step]).wait()
        return carry

    lax.fori_loop(0, 4, settle, 0)
    for keeps, sem in ((my_x0 == core, in_send), (lax.rem(my_y, 2) == core, out_send)):

        @pl.when(keeps)
        def _(sem=sem):
            pltpu.make_async_copy(sbuf.at[pl.ds(0, 63)], sbuf.at[pl.ds(0, 63)], sem).wait()

        @pl.when(jnp.logical_not(keeps))
        def _(sem=sem):
            pltpu.make_async_copy(sbuf, sbuf, sem).wait()

    def arrive(step, carry):
        box = turn_of(step, lax.rem(my_y, 2))
        pltpu.make_async_copy(orecv.at[pl.ds(0, 16)], orecv.at[pl.ds(0, 16)], out_recv.at[box]).wait()
        z1_from, y1_from = box_of(box)

        def scatter_rows(i, carry):
            z, x, y = 2 * z1_from + lax.div(i, 8), lax.rem(lax.div(i, 2), 4), 2 * y1_from + lax.rem(i, 2)
            ell = z * 16 + x * 4 + y
            for tile in range(9):
                out_ref[pl.ds(tile * 512 + ell, 8, stride=64), :] = orecv[ell, 8 * tile : 8 * tile + 8, :]
            return carry

        lax.fori_loop(0, 16, scatter_rows, 0, unroll=4)
        return carry

    lax.fori_loop(0, 4, arrive, 0)


def shards(coefficients, slowness):
    rows = jnp.transpose(coefficients, (0, 1, 3, 2, 4)).reshape(ROWS * 64, LANES)
    operands = (rows, pltpu.with_memory_space_constraint(slowness, pltpu.HBM))
    dense = (ROWS, LANES)
    scratch = [pltpu.VMEM(operands[i].shape, jnp.float32) for i in range(2)]
    scratch += [pltpu.VMEM((12, 2 * TERMS, DEPTH), jnp.bfloat16), pltpu.VMEM((4, 2 * TERMS, DEPTH), jnp.float32)]
    scratch += [
        pltpu.VMEM(shape, jnp.float32)
        for shape in (
            (64,) + dense,
            (2, 2, 4, 4) + dense,
            (2, 2, 2, 2, 4) + dense,
            (4, 2, 2, 4) + dense,
            (4, 2, 2, 4, 40, LANES),
            (2, 2, 4) + dense,
            (4, 2, 2, 2, 2) + dense,
            (64,) + dense,
            (29, TERMS, LANES),
            (32, 4, 2, TERMS, LANES),
            (4, 2 * TERMS, 2 * LANES),
            (4, 2 * TERMS, 2 * LANES),
            (2, 4) + dense,
            (2, 4) + dense,
        )
    ]
    scratch += [
        pltpu.SemaphoreType.DMA((4,)),
        pltpu.SemaphoreType.DMA,
        pltpu.SemaphoreType.DMA((2,)),
        pltpu.SemaphoreType.DMA((4,)),
        pltpu.SemaphoreType.DMA((4,)),
        pltpu.SemaphoreType.DMA,
        pltpu.SemaphoreType.DMA((4,)),
    ]
    out = pl.pallas_call(
        kernel,
        out_shape=jax.ShapeDtypeStruct((ROWS * 64, LANES), jnp.float32),
        in_specs=[pl.BlockSpec(memory_space=pl.ANY), pl.BlockSpec(memory_space=pltpu.HBM)],
        out_specs=pl.BlockSpec(memory_space=pltpu.VMEM),
        scratch_shapes=scratch,
        compiler_params=pltpu.CompilerParams(collective_id=0, has_side_effects=True, vmem_limit_bytes=50 << 20),
    )(*operands)
    return jnp.transpose(out.reshape(2, CHEB, CHEB, 64, LANES), (0, 1, 3, 2, 4))


def solution(mesh):
    placed = (P(None, None, "bx", None, "by"), P())
    return jax.shard_map(
        shards,
        mesh=mesh,
        in_specs=placed,
        out_specs=P(None, None, "bx", None, "by"),
        check_vma=False,
    )
```

```python
import math

import jax
import jax.numpy as jnp
import numpy as np
from jax import lax
from jax.experimental import pallas as pl
from jax.experimental.pallas import tpu as pltpu
from jax.sharding import PartitionSpec as P

N = 2048
CHEB = 6
HALF = CHEB * CHEB
ROWS = 2 * HALF
TERMS = 4 * HALF
PAD = 80
DEPTH = 256
LANES = 128
MESH = pl.DeviceIdType.MESH


def cheb_points():
    return np.cos(np.pi * (2 * np.arange(CHEB) + 1) / (2 * CHEB))


def fit(function, degree):
    count = 200
    s = 0.125 * (1 + np.cos(np.pi * (2 * np.arange(count) + 1) / (2 * count)))
    series = np.polynomial.chebyshev.Chebyshev.fit(s, function(np.sqrt(s)), degree, domain=[0, 0.25])
    return [float(c) for c in series.convert(kind=np.polynomial.Polynomial).coef]


SIN = fit(lambda r: math.sqrt(2) * np.sin(np.pi * r) / r, 3)
COS = fit(lambda r: math.sqrt(2) * np.cos(np.pi * r), 4)
WHOLE = 1.5 * 2.0**23


POINTS = [float(point) for point in cheb_points()]
SCALES = [
    float(1 / np.prod([cheb_points()[s] - cheb_points()[j] for j in range(CHEB) if j != s])) for s in range(CHEB)
]


def horner(coefficients, s):
    value = s * coefficients[-1] + coefficients[-2]
    for coefficient in coefficients[-3::-1]:
        value = value * s + coefficient
    return value


def unit(turns):
    r = turns - ((turns + WHOLE) - WHOLE)
    s = r * r
    half = horner(SIN, s) * r
    return 1.0 - half * half, half * horner(COS, s)


def operand(block):
    if block.shape[0] < PAD:
        block = jnp.concatenate([block, jnp.zeros((PAD - block.shape[0], block.shape[1]), jnp.float32)], axis=0)
    high = block.astype(jnp.bfloat16)
    low = (block - high.astype(jnp.float32)).astype(jnp.bfloat16)
    return jnp.concatenate([high, low, high, jnp.zeros((DEPTH - 3 * PAD, block.shape[1]), jnp.bfloat16)], axis=0)


def choose(index, values):
    result = jnp.full(index.shape, values[0], jnp.float32)
    for number, value in enumerate(values[1:], 1):
        result = jnp.where(index == number, value, result)
    return result


def digits(value, *sizes):
    out = []
    for size in sizes[::-1]:
        rest = jnp.floor((value + 0.5) * (1.0 / size))
        out.append(value - rest * size)
        value = rest
    return out[::-1]


def lagrange(at, source):
    product = choose(source, SCALES)
    for number, point in enumerate(POINTS):
        product = product * jnp.where(source == number, 1.0, at - point)
    return product


def mixing_tables(mix_ref, raw_ref):
    shape = (HALF, DEPTH)
    column = lax.broadcasted_iota(jnp.int32, shape, 1).astype(jnp.float32)
    copy, inside = digits(column, 4, PAD)
    row = lax.broadcasted_iota(jnp.int32, shape, 0).astype(jnp.float32)
    t1, t2 = digits(row, CHEB, CHEB)
    second = inside >= 40
    place = inside - jnp.where(second, 40.0, 0.0)
    used = jnp.logical_and(place < HALF, copy < 3)
    s1, s2 = digits(jnp.minimum(place, HALF - 1.0), CHEB, CHEB)
    at1, at2 = choose(t1, POINTS) * 0.5, choose(t2, POINTS) * 0.5
    weights1 = [jnp.where(used, lagrange(q - 0.5 + at1, s1), 0.0) for q in range(2)]
    weights2 = [lagrange(q - 0.5 + at2, s2) for q in range(2)]
    for q1 in range(2):
        for q2 in range(2):
            weights = weights1[q1] * weights2[q2]
            turns1, turns2 = 0.5 * (q1 + 0.5 + at1), 0.5 * (q2 + 0.5 + at2)
            plus, minus = unit(turns1 + turns2), unit(turns1 - turns2)
            for c1 in range(2):
                for c2 in range(2):
                    co, si = plus if c1 == c2 else minus
                    si = si if c1 else -si
                    real, imag = co * weights, si * weights
                    for part, values in enumerate((jnp.where(second, -imag, real), jnp.where(second, real, imag))):
                        high = values.astype(jnp.bfloat16).astype(jnp.float32)
                        values = jnp.where(copy < 2, high, values - high)
                        base = part * TERMS + q1 * ROWS + q2 * HALF
                        raw_ref[2 * c1 + c2, base : base + HALF, :] = values

    shape = (48, DEPTH)
    copy, inside = digits(lax.broadcasted_iota(jnp.int32, shape, 1).astype(jnp.float32), 4, PAD)

    def variants(i, carry):
        table, rows = lax.div(i, 6), pl.ds(pl.multiple_of(48 * lax.rem(i, 6), 16), 48)
        values = raw_ref[table, rows, :]
        dense = jnp.where(inside < HALF, values, pltpu.roll(values, DEPTH - 4, 1))
        dense = jnp.where(inside < ROWS, dense, 0.0)
        for variant, block in enumerate((dense, values, pltpu.roll(values, 4, 1))):
            mix_ref[4 * variant + table, rows, :] = block.astype(jnp.bfloat16)
        return carry

    lax.fori_loop(0, 24, variants, 0)


def reverse6(value):
    total = 0
    for bit in range(6):
        total = total + lax.rem(lax.div(value, 1 << bit), 2) * (1 << (5 - bit))
    return total


def kernel(
    coef_hbm, slow_hbm, out_ref,
    coef_ref, slow_ref, mix_ref, raw_ref,
    sbuf, xin, s0, z1, zr, s2, obuf, orecv, vtab, e_tab, y_a, y_b, acc_a, acc_b,
    load, in_send, in_recv, sib_send, sib_recv, out_send, out_recv,
):
    bx, by = lax.axis_index("bx"), lax.axis_index("by")
    my_z, my_x = lax.div(bx, 4), lax.rem(bx, 4)
    my_y, core = lax.div(by, 2), lax.rem(by, 2)
    my_x0 = lax.rem(my_x, 2)
    chip = bx * 4 + my_y
    low1 = reverse6(chip) * 16

    loads = [
        pltpu.make_async_copy(src, dst, load.at[i])
        for i, (src, dst) in enumerate(
            ((coef_hbm, coef_ref), (slow_hbm, slow_ref))
        )
    ]
    for copy in loads:
        copy.start()

    barrier = pltpu.get_barrier_semaphore()
    me = bx * 8 + by

    def greet(i, carry):
        there = lax.rem(me + i, 128)
        pl.semaphore_signal(barrier, inc=1, device_id=(lax.div(there, 8), lax.rem(there, 8)), device_id_type=MESH)
        return carry

    lax.fori_loop(1, 121, greet, 0, unroll=8)
    lax.fori_loop(121, 128, greet, 0, unroll=7)
    loads[0].wait()

    def gather_rows(ell, carry):
        for tile in range(9):
            sbuf[ell, 8 * tile : 8 * tile + 8, :] = coef_ref[pl.ds(tile * 512 + ell, 8, stride=64), :]
        return carry

    lax.fori_loop(0, 64, gather_rows, 0, unroll=8)
    pl.semaphore_wait(barrier, 127)

    def send_in(step, carry):
        half, inner = lax.div(step, 32), lax.rem(step, 32)
        dx, group = lax.rem(inner, 4), lax.div(inner, 4)
        dy = lax.rem(dx + group, 4)
        dz = half + 2 * lax.rem(lax.div(group, 4) + dx, 2)
        dx, dz, dy = [lax.rem(d + 2 * core, 4) for d in (dx, dz, dy)]
        to_x, to_z, to_y = lax.rem(my_x + dx, 4), lax.rem(my_z + dz, 4), lax.rem(my_y + dy, 4)
        to_bx, to_by = to_z * 4 + to_x, to_y * 2 + my_x0
        ell = to_z * 16 + to_x * 4 + to_y
        src = sbuf.at[ell]
        dst = xin.at[lax.div(dx, 2), core, my_z, my_y]
        here = jnp.logical_and(to_bx == bx, to_by == by)

        @pl.when(here)
        def _():
            pltpu.make_async_copy(src, dst, in_recv.at[half]).start()

        @pl.when(jnp.logical_not(here))
        def _():
            pltpu.make_async_remote_copy(
                src_ref=src, dst_ref=dst, send_sem=in_send, recv_sem=in_recv.at[half],
                device_id=(to_bx, to_by), device_id_type=MESH,
            ).start()

        return carry

    lax.fori_loop(0, 64, send_in, 0)

    loads[1].wait()
    lane = lax.broadcasted_iota(jnp.int32, (TERMS, 96), 1).astype(jnp.float32)
    row = lax.broadcasted_iota(jnp.int32, (TERMS, 96), 0).astype(jnp.float32)
    q1, q2, t1, t2 = digits(row, 2, 2, CHEB, CHEB)
    row_i, row_j = CHEB * q1 + t1, CHEB * q2 + t2

    def spread(level, a1):
        pick = jnp.where(row_i + (12 * a1).astype(jnp.float32) == lane, 1.0, 0.0)
        return jnp.dot(pick, slow_ref[level], precision=lax.Precision.HIGHEST, preferred_element_type=jnp.float32)

    def column(table, a2):
        picked = jnp.where(row_j + (12 * a2).astype(jnp.float32) == lane, table, 0.0)
        return jnp.broadcast_to(jnp.sum(picked, axis=1, keepdims=True), (TERMS, LANES))

    zero, one = jnp.int32(0), jnp.int32(1)
    vtab[0] = column(spread(0, zero), zero)

    def fill1(a1, carry):
        table = spread(1, a1)
        for a2 in range(2):
            vtab[1 + 2 * a1 + a2] = column(table, a2 * one)
        return carry

    lax.fori_loop(0, 2, fill1, 0)

    def fill2(z, carry):
        table = spread(2, z)
        for a2 in range(2):
            vtab[5 + 2 * z + a2] = column(table, 2 * a2 + core)
        return carry

    lax.fori_loop(0, 4, fill2, 0)
    left_rows = lax.broadcasted_iota(jnp.int32, (TERMS, LANES), 1) < 64

    def fill3(a1, carry):
        table = spread(3, a1)
        for a2 in range(2):
            box = 2 * (2 * a2 + core)
            vtab[13 + 2 * a1 + a2] = jnp.where(left_rows, column(table, box), column(table, box + 1))
        return carry

    lax.fori_loop(0, 8, fill3, 0)

    lanes = lax.broadcasted_iota(jnp.int32, (8, LANES), 1)
    low2 = reverse6(lax.rem(lanes, 64)) * 16
    lane2 = lax.div(lanes, 64) * 8 + low2
    back = 127 - lanes
    back_half = lax.div(lanes, 64) * 64 + 63 - lax.rem(lanes, 64)

    def permute(block, index):
        rows = [
            jnp.take_along_axis(block[8 * i : 8 * i + 8], index, axis=1, mode="promise_in_bounds")
            for i in range(block.shape[0] // 8)
        ]
        return jnp.concatenate(rows, axis=0)

    def magnitude(level, r1, c1, r2, c2):
        width = 2.0 ** (level + 1)
        k = (lax.div(r1, 1 << level).astype(jnp.float32) + 0.5) * width - N / 2
        step = (c1 - 0.5) * width
        k0 = k - step
        k2 = (lax.div(r2, jnp.full(r2.shape, 1 << level, jnp.int32)).astype(jnp.float32) + 0.5) * width - N / 2
        step2 = (c2 - 0.5) * width
        k20 = k2 - step2
        above = step * (k + k0) + step2 * (k2 + k20)
        return above / (jnp.sqrt(k * k + k2 * k2) + jnp.sqrt(k0 * k0 + k20 * k20))

    def interpolate(y_ref, child, table, blocks):
        y_ref[child] = jnp.dot(
            mix_ref[table], operand(jnp.concatenate(blocks, axis=1)), preferred_element_type=jnp.float32
        )

    def tiles(body):
        def tile(i, carry):
            body(i, pl.ds(pl.multiple_of(8 * i, 8), 8), pl.ds(pl.multiple_of(8 * i + TERMS, 8), 8))
            return carry

        lax.fori_loop(0, TERMS // 8, tile, 0, unroll=True)

    def added(total, co, si, y_ref, child, at, at_im, side):
        cols = pl.ds(side * LANES, LANES)
        y_re, y_im = y_ref[child, at, cols], y_ref[child, at_im, cols]
        re, im = co * y_re - si * y_im, co * y_im + si * y_re
        return (re, im) if total is None else (total[0] + re, total[1] + im)

    def exponentials(entry, slots, sizes):
        def tile(i, carry):
            at = pl.ds(pl.multiple_of(8 * i, 8), 8)
            for j in range(4):
                co, si = unit(vtab[slots[j], at, :] * sizes[j])
                e_tab[entry, j, 0, at, :] = co
                e_tab[entry, j, 1, at, :] = si
            return carry

        lax.fori_loop(0, TERMS // 8, tile, 0, unroll=3)

    def combine_cores(y_ref, dst, entry):
        def body(i, at, at_im):
            totals = [None, None]
            for c1 in range(2):
                for c2 in range(2):
                    co, si = e_tab[entry, 2 * c1 + c2, 0, at, :], e_tab[entry, 2 * c1 + c2, 1, at, :]
                    totals[0] = added(totals[0], co, si, y_ref, 2 * c1 + c2, at, at_im, 0)
                    totals[1] = added(totals[1], co, si, y_ref, 2 * c1 + 1 - c2, at, at_im, 1)
            for side in range(2):
                put(dst[side], i, totals[side])

        tiles(body)

    def combine_mirrored(y_ref, dst, entry, index):
        def body(i, at, at_im):
            for side in range(2):
                totals = [None, None]
                for c1 in range(2):
                    co, si = e_tab[entry, 2 * c1 + side, 0, at, :], e_tab[entry, 2 * c1 + side, 1, at, :]
                    for c2 in range(2):
                        totals[c2] = added(totals[c2], co, si, y_ref, 2 * c1 + c2, at, at_im, side)
                put(dst[side], i, [totals[0][part] + permute(totals[1][part], index) for part in range(2)])

        tiles(body)

    def put(dst, i, total):
        rows = pl.ds(pl.multiple_of(8 * lax.rem(i, 9), 8), 8)
        for part in range(2):
            dst[2 * part + lax.div(i, 9), rows, :] = total[part]

    def window(src, q1, q2):
        rows = pl.ds(pl.multiple_of(32 * q2, 8), 40)
        return jnp.concatenate([src[q1, rows, :], src[2 + q1, rows, :]], axis=0)

    pairs = ((0, y_a, acc_a), (1, y_b, acc_b))

    def x_of(slot):
        dx = 2 * slot + lax.rem(my_x + core, 2)
        x = lax.rem(my_x - dx + 4, 4)
        return lax.div(x, 2), low1 + 4 * lax.div(x, 2) + 8 * core

    def box_of(box):
        other1 = 1 - lax.rem(box, 2)
        other2 = 1 - lax.rem(lax.rem(box, 2) + lax.div(box, 2), 2)
        return lax.rem(lax.div(my_z, 2) + other1, 2), lax.rem(lax.div(my_y, 2) + other2, 2)

    children = [(c1, c2) for c1 in range(2) for c2 in range(2)]

    def phases0(part, carry):
        z0, y0 = lax.rem(my_z + lax.div(part, 2), 2), lax.rem(part, 2)
        for slot in range(2):
            r1 = x_of(slot)[1] + 2 * z0
            sizes = [magnitude(0, r1 + c1, c1, lane2 + (c2 + 2 * y0), c2) for c1, c2 in children]
            exponentials(2 * part + slot, (0,) * 4, sizes)
        return carry

    def phases1(step, carry):
        a1, a2 = box_of(step)
        for slot in range(2):
            r1 = x_of(slot)[1]
            sizes = [magnitude(1, r1 + 2 * c1, c1, lane2 + 2 * c2, c2) for c1, c2 in children]
            exponentials(8 + 2 * step + slot, (1 + 2 * a1 + a2,) * 4, sizes)
        return carry

    def phases2(step, carry):
        a1, a2 = box_of(step)
        sizes = [
            magnitude(2, low1 + 4 * c1 + 8 * x0, c1, lane2, 0) for c1 in range(2) for x0 in (core, 1 - core)
        ]
        for z0 in range(2):
            exponentials(16 + 2 * step + z0, (5 + 2 * (2 * a1 + z0) + a2,) * 4, sizes)
        return carry

    def phases3(step, carry):
        a1, a2 = box_of(step)
        sizes = [magnitude(3, low1 + 8 * c1, c1, low2, 0) for c1 in range(2) for side in range(2)]
        for z0 in range(2):
            slot = 13 + 4 * (2 * a1 + z0) + a2
            exponentials(24 + 2 * step + z0, (slot, slot + 2, slot, slot + 2), sizes)
        return carry

    def level0(part, carry):
        z0, y0 = lax.rem(my_z + lax.div(part, 2), 2), lax.rem(part, 2)
        for slot, y_ref, _ in pairs:
            for c1, c2 in children:
                z = 2 * c1 + z0
                first = xin[slot, 0, z, 2 * c2 + y0]
                second = permute(xin[slot, 1, z, 2 * c2 + 1 - y0], back)
                interpolate(y_ref, 2 * c1 + c2, 2 * c1 + c2, [first, second])
        for slot, y_ref, _ in pairs:
            combine_cores(y_ref, (s0.at[slot, z0, y0, 0], s0.at[slot, z0, 1 - y0, 1]), 2 * part + slot)
        return carry

    mixing_tables(mix_ref, raw_ref)
    for phases in (phases0, phases1, phases2):
        lax.fori_loop(0, 4, phases, 0)

    def arrived(half, carry):
        pltpu.make_async_copy(xin.at[0], xin.at[0], in_recv.at[half]).wait()
        lax.fori_loop(2 * half, 2 * half + 2, level0, 0)

        @pl.when(half == 0)
        def _():
            lax.fori_loop(0, 4, phases3, 0)

        return carry

    lax.fori_loop(0, 2, arrived, 0)

    def level1(step):
        a1, a2 = box_of(step)
        for slot, y_ref, _ in pairs:
            for c1, c2 in children:
                blocks = [window(s0.at[slot, c1, c2, side], a1, a2) for side in range(2)]
                interpolate(y_ref, 2 * c1 + c2, 4 + 4 * a2 + 2 * c1 + c2, blocks)
        for slot, y_ref, _ in pairs:
            x1 = x_of(slot)[0]
            combine_cores(y_ref, (z1.at[step, x1, 0], z1.at[step, x1, 1]), 8 + 2 * step + slot)
        pltpu.make_async_remote_copy(
            src_ref=z1.at[step, :, :, :, pl.ds(pl.multiple_of(32 * (1 - core), 8), 40), :],
            dst_ref=zr.at[step],
            send_sem=sib_send.at[step],
            recv_sem=sib_recv.at[step],
            device_id=(bx, my_y * 2 + 1 - core),
            device_id_type=MESH,
        ).start()

    left = lax.broadcasted_iota(jnp.int32, (PAD, LANES), 1) < 64
    left_half = lax.broadcasted_iota(jnp.int32, (HALF, LANES), 1) < 64

    def level23(step):
        pltpu.make_async_copy(zr.at[0], zr.at[0], sib_recv.at[step]).wait()
        near_z0 = lax.rem(my_z, 2)
        z0_of = (near_z0, 1 - near_z0)
        for i, y_ref, _ in pairs:
            z0 = z0_of[i]
            for c1, c2 in children:
                other = zr.at[step, c1, c2]
                blocks = [
                    window(z1.at[step, c1, c2], z0, core),
                    jnp.concatenate([other[z0], other[2 + z0]], axis=0),
                ]
                interpolate(y_ref, 2 * c1 + c2, 4 + 4 * core + 2 * c1 + c2, blocks)
        for i, y_ref, _ in pairs:
            combine_mirrored(y_ref, (s2.at[i, 0], s2.at[i, 1]), 16 + 2 * step + z0_of[i], back)
        for i, y_ref, _ in pairs:
            for c1 in range(2):
                src = s2.at[i, lax.rem(c1 + core, 2)]
                near, far = [], []
                for x1 in range(2):
                    first = window(src, x1, 0)
                    second = window(src, x1, 1)
                    second = jnp.concatenate([second[4:40], second[36:40], second[44:80], second[76:80]], axis=0)
                    near.append(jnp.where(left, first, pltpu.roll(second, 64, 1)))
                    far.append(jnp.where(left, permute(first, back), permute(second, back_half)))
                interpolate(y_ref, 2 * c1, 4 + 2 * c1, near)
                interpolate(y_ref, 2 * c1 + 1, 4 + 2 * c1 + 1, far)
        for i, y_ref, acc_ref in pairs:
            combine_mirrored(y_ref, (acc_ref.at[0], acc_ref.at[1]), 24 + 2 * step + z0_of[i], back_half)
            for x1 in range(2):
                for q1 in range(2):
                    for part in range(2):
                        upper = acc_ref[x1, 2 * part + q1, 0:HALF, :]
                        lower = acc_ref[x1, 2 * part + q1, HALF:ROWS, :]
                        rows = pl.ds(HALF * part, HALF)
                        obuf[step, i, x1, q1, 0, rows, :] = jnp.where(left_half, upper, pltpu.roll(lower, 64, 1))
                        obuf[step, i, x1, q1, 1, rows, :] = jnp.where(left_half, pltpu.roll(upper, 64, 1), lower)

    def send_out(half, number):
        turn, round_ = lax.rem(number, 4), lax.div(number, 4)
        box = 2 * half + lax.rem(lax.div(turn + 1, 2) + core, 2)
        i = lax.rem(turn, 2)
        a1, a2 = box_of(box)
        x = lax.rem(my_x + 1 + 2 * core + round_ + turn, 4)
        c = lax.rem(lax.div(round_, 4) + core, 2)
        to_bx, to_by = (2 * a1 + lax.rem(my_z + i, 2)) * 4 + x, 2 * (2 * a2 + core) + c
        src, dst = obuf.at[box, i, lax.div(x, 2), lax.rem(x, 2), c], orecv.at[chip]
        here = jnp.logical_and(to_bx == bx, to_by == by)

        @pl.when(here)
        def _():
            pltpu.make_async_copy(src, dst, out_recv.at[box]).start()

        @pl.when(jnp.logical_not(here))
        def _():
            pltpu.make_async_remote_copy(
                src_ref=src, dst_ref=dst, send_sem=out_send, recv_sem=out_recv.at[box],
                device_id=(to_bx, to_by), device_id_type=MESH,
            ).start()

    def two_boxes(half, carry):
        for level in (level1, level23):
            for box in range(2):
                level(2 * half + box)

        def send_some(number, carry):
            send_out(half, number)
            return carry

        lax.fori_loop(0, 32, send_some, 0)
        return carry

    lax.fori_loop(0, 2, two_boxes, 0)

    def settle(step, carry):
        pltpu.make_async_copy(zr.at[0], zr.at[0], sib_send.at[step]).wait()
        return carry

    lax.fori_loop(0, 4, settle, 0)
    for keeps, sem in ((my_x0 == core, in_send), (lax.rem(my_y, 2) == core, out_send)):

        @pl.when(keeps)
        def _(sem=sem):
            pltpu.make_async_copy(sbuf.at[pl.ds(0, 63)], sbuf.at[pl.ds(0, 63)], sem).wait()

        @pl.when(jnp.logical_not(keeps))
        def _(sem=sem):
            pltpu.make_async_copy(sbuf, sbuf, sem).wait()

    def arrive(step, carry):
        pltpu.make_async_copy(orecv.at[pl.ds(0, 16)], orecv.at[pl.ds(0, 16)], out_recv.at[step]).wait()
        z1_from, y1_from = box_of(step)

        def scatter_rows(i, carry):
            z, x, y = 2 * z1_from + lax.div(i, 8), lax.rem(lax.div(i, 2), 4), 2 * y1_from + lax.rem(i, 2)
            ell = z * 16 + x * 4 + y
            for tile in range(9):
                out_ref[pl.ds(tile * 512 + ell, 8, stride=64), :] = orecv[ell, 8 * tile : 8 * tile + 8, :]
            return carry

        lax.fori_loop(0, 16, scatter_rows, 0, unroll=4)
        return carry

    lax.fori_loop(0, 4, arrive, 0)


def shards(coefficients, slowness):
    rows = jnp.transpose(coefficients, (0, 1, 3, 2, 4)).reshape(ROWS * 64, LANES)
    operands = (rows, pltpu.with_memory_space_constraint(slowness, pltpu.HBM))
    dense = (ROWS, LANES)
    scratch = [pltpu.VMEM(operands[i].shape, jnp.float32) for i in range(2)]
    scratch += [pltpu.VMEM((12, 2 * TERMS, DEPTH), jnp.bfloat16), pltpu.VMEM((4, 2 * TERMS, DEPTH), jnp.float32)]
    scratch += [
        pltpu.VMEM(shape, jnp.float32)
        for shape in (
            (64,) + dense,
            (2, 2, 4, 4) + dense,
            (2, 2, 2, 2, 4) + dense,
            (4, 2, 2, 4) + dense,
            (4, 2, 2, 4, 40, LANES),
            (2, 2, 4) + dense,
            (4, 2, 2, 2, 2) + dense,
            (64,) + dense,
            (29, TERMS, LANES),
            (32, 4, 2, TERMS, LANES),
            (4, 2 * TERMS, 2 * LANES),
            (4, 2 * TERMS, 2 * LANES),
            (2, 4) + dense,
            (2, 4) + dense,
        )
    ]
    scratch += [
        pltpu.SemaphoreType.DMA((4,)),
        pltpu.SemaphoreType.DMA,
        pltpu.SemaphoreType.DMA((2,)),
        pltpu.SemaphoreType.DMA((4,)),
        pltpu.SemaphoreType.DMA((4,)),
        pltpu.SemaphoreType.DMA,
        pltpu.SemaphoreType.DMA((4,)),
    ]
    out = pl.pallas_call(
        kernel,
        out_shape=jax.ShapeDtypeStruct((ROWS * 64, LANES), jnp.float32),
        in_specs=[pl.BlockSpec(memory_space=pl.ANY), pl.BlockSpec(memory_space=pltpu.HBM)],
        out_specs=pl.BlockSpec(memory_space=pltpu.VMEM),
        scratch_shapes=scratch,
        compiler_params=pltpu.CompilerParams(collective_id=0, has_side_effects=True, vmem_limit_bytes=50 << 20),
    )(*operands)
    return jnp.transpose(out.reshape(2, CHEB, CHEB, 64, LANES), (0, 1, 3, 2, 4))


def solution(mesh):
    placed = (P(None, None, "bx", None, "by"), P())
    return jax.shard_map(
        shards,
        mesh=mesh,
        in_specs=placed,
        out_specs=P(None, None, "bx", None, "by"),
        check_vma=False,
    )
```

```python
import math

import jax
import jax.numpy as jnp
import numpy as np
from jax import lax
from jax.experimental import pallas as pl
from jax.experimental.pallas import tpu as pltpu
from jax.sharding import PartitionSpec as P

N = 2048
CHEB = 6
HALF = CHEB * CHEB
ROWS = 2 * HALF
TERMS = 4 * HALF
PAD = 80
DEPTH = 256
LANES = 128
MESH = pl.DeviceIdType.MESH


def cheb_points():
    return np.cos(np.pi * (2 * np.arange(CHEB) + 1) / (2 * CHEB))


def fit(function, degree):
    count = 200
    s = 0.125 * (1 + np.cos(np.pi * (2 * np.arange(count) + 1) / (2 * count)))
    series = np.polynomial.chebyshev.Chebyshev.fit(s, function(np.sqrt(s)), degree, domain=[0, 0.25])
    return [float(c) for c in series.convert(kind=np.polynomial.Polynomial).coef]


SIN = fit(lambda r: math.sqrt(2) * np.sin(np.pi * r) / r, 3)
COS = fit(lambda r: math.sqrt(2) * np.cos(np.pi * r), 4)
WHOLE = 1.5 * 2.0**23


POINTS = [float(point) for point in cheb_points()]
SCALES = [
    float(1 / np.prod([cheb_points()[s] - cheb_points()[j] for j in range(CHEB) if j != s])) for s in range(CHEB)
]


def horner(coefficients, s):
    value = s * coefficients[-1] + coefficients[-2]
    for coefficient in coefficients[-3::-1]:
        value = value * s + coefficient
    return value


def unit(turns):
    r = turns - ((turns + WHOLE) - WHOLE)
    s = r * r
    half = horner(SIN, s) * r
    return 1.0 - half * half, half * horner(COS, s)


def operand(block):
    if block.shape[0] < PAD:
        block = jnp.concatenate([block, jnp.zeros((PAD - block.shape[0], block.shape[1]), jnp.float32)], axis=0)
    high = block.astype(jnp.bfloat16)
    low = (block - high.astype(jnp.float32)).astype(jnp.bfloat16)
    return jnp.concatenate([high, low, high, jnp.zeros((DEPTH - 3 * PAD, block.shape[1]), jnp.bfloat16)], axis=0)


def choose(index, values):
    result = jnp.full(index.shape, values[0], jnp.float32)
    for number, value in enumerate(values[1:], 1):
        result = jnp.where(index == number, value, result)
    return result


def digits(value, *sizes):
    out = []
    for size in sizes[::-1]:
        rest = jnp.floor((value + 0.5) * (1.0 / size))
        out.append(value - rest * size)
        value = rest
    return out[::-1]


def lagrange(at, source):
    product = choose(source, SCALES)
    for number, point in enumerate(POINTS):
        product = product * jnp.where(source == number, 1.0, at - point)
    return product


def mixing_tables(mix_ref, raw_ref):
    shape = (HALF, DEPTH)
    column = lax.broadcasted_iota(jnp.int32, shape, 1).astype(jnp.float32)
    copy, inside = digits(column, 4, PAD)
    row = lax.broadcasted_iota(jnp.int32, shape, 0).astype(jnp.float32)
    t1, t2 = digits(row, CHEB, CHEB)
    second = inside >= 40
    place = inside - jnp.where(second, 40.0, 0.0)
    used = jnp.logical_and(place < HALF, copy < 3)
    s1, s2 = digits(jnp.minimum(place, HALF - 1.0), CHEB, CHEB)
    at1, at2 = choose(t1, POINTS) * 0.5, choose(t2, POINTS) * 0.5
    weights1 = [jnp.where(used, lagrange(q - 0.5 + at1, s1), 0.0) for q in range(2)]
    weights2 = [lagrange(q - 0.5 + at2, s2) for q in range(2)]
    for q1 in range(2):
        for q2 in range(2):
            weights = weights1[q1] * weights2[q2]
            turns1, turns2 = 0.5 * (q1 + 0.5 + at1), 0.5 * (q2 + 0.5 + at2)
            plus, minus = unit(turns1 + turns2), unit(turns1 - turns2)
            for c1 in range(2):
                for c2 in range(2):
                    co, si = plus if c1 == c2 else minus
                    si = si if c1 else -si
                    real, imag = co * weights, si * weights
                    for part, values in enumerate((jnp.where(second, -imag, real), jnp.where(second, real, imag))):
                        high = values.astype(jnp.bfloat16).astype(jnp.float32)
                        values = jnp.where(copy < 2, high, values - high)
                        base = part * TERMS + q1 * ROWS + q2 * HALF
                        raw_ref[2 * c1 + c2, base : base + HALF, :] = values

    shape = (48, DEPTH)
    copy, inside = digits(lax.broadcasted_iota(jnp.int32, shape, 1).astype(jnp.float32), 4, PAD)

    def variants(i, carry):
        table, rows = lax.div(i, 6), pl.ds(pl.multiple_of(48 * lax.rem(i, 6), 16), 48)
        values = raw_ref[table, rows, :]
        dense = jnp.where(inside < HALF, values, pltpu.roll(values, DEPTH - 4, 1))
        dense = jnp.where(inside < ROWS, dense, 0.0)
        for variant, block in enumerate((dense, values, pltpu.roll(values, 4, 1))):
            mix_ref[4 * variant + table, rows, :] = block.astype(jnp.bfloat16)
        return carry

    lax.fori_loop(0, 24, variants, 0)


def reverse6(value):
    total = 0
    for bit in range(6):
        total = total + lax.rem(lax.div(value, 1 << bit), 2) * (1 << (5 - bit))
    return total


def kernel(
    coef_hbm, slow_hbm, out_ref,
    coef_ref, slow_ref, mix_ref, raw_ref,
    sbuf, xin, s0, z1, zr, s2, obuf, orecv, vtab, e_tab, y_a, y_b, y_c, y_d, acc_a, acc_b,
    load, in_send, in_recv, sib_send, sib_recv, out_send, out_recv,
):
    bx, by = lax.axis_index("bx"), lax.axis_index("by")
    my_z, my_x = lax.div(bx, 4), lax.rem(bx, 4)
    my_y, core = lax.div(by, 2), lax.rem(by, 2)
    my_x0 = lax.rem(my_x, 2)
    chip = bx * 4 + my_y
    low1 = reverse6(chip) * 16

    loads = [
        pltpu.make_async_copy(src, dst, load.at[i])
        for i, (src, dst) in enumerate(
            ((coef_hbm, coef_ref), (slow_hbm, slow_ref))
        )
    ]
    for copy in loads:
        copy.start()

    barrier = pltpu.get_barrier_semaphore()
    me = bx * 8 + by

    def greet(i, carry):
        there = lax.rem(me + i, 128)
        pl.semaphore_signal(barrier, inc=1, device_id=(lax.div(there, 8), lax.rem(there, 8)), device_id_type=MESH)
        return carry

    lax.fori_loop(1, 121, greet, 0, unroll=8)
    lax.fori_loop(121, 128, greet, 0, unroll=7)
    loads[0].wait()

    def gather_rows(ell, carry):
        for tile in range(9):
            sbuf[ell, 8 * tile : 8 * tile + 8, :] = coef_ref[pl.ds(tile * 512 + ell, 8, stride=64), :]
        return carry

    lax.fori_loop(0, 64, gather_rows, 0, unroll=8)
    pl.semaphore_wait(barrier, 127)

    def send_in(step, carry):
        half, inner = lax.div(step, 32), lax.rem(step, 32)
        dx, group = lax.rem(inner, 4), lax.div(inner, 4)
        dy = lax.rem(dx + group, 4)
        dz = half + 2 * lax.rem(lax.div(group, 4) + dx, 2)
        dx, dz, dy = [lax.rem(d + 2 * core, 4) for d in (dx, dz, dy)]
        to_x, to_z, to_y = lax.rem(my_x + dx, 4), lax.rem(my_z + dz, 4), lax.rem(my_y + dy, 4)
        to_bx, to_by = to_z * 4 + to_x, to_y * 2 + my_x0
        ell = to_z * 16 + to_x * 4 + to_y
        src = sbuf.at[ell]
        dst = xin.at[lax.div(dx, 2), core, my_z, my_y]
        here = jnp.logical_and(to_bx == bx, to_by == by)

        @pl.when(here)
        def _():
            pltpu.make_async_copy(src, dst, in_recv.at[half]).start()

        @pl.when(jnp.logical_not(here))
        def _():
            pltpu.make_async_remote_copy(
                src_ref=src, dst_ref=dst, send_sem=in_send, recv_sem=in_recv.at[half],
                device_id=(to_bx, to_by), device_id_type=MESH,
            ).start()

        return carry

    lax.fori_loop(0, 64, send_in, 0)

    loads[1].wait()
    lane = lax.broadcasted_iota(jnp.int32, (TERMS, 96), 1).astype(jnp.float32)
    row = lax.broadcasted_iota(jnp.int32, (TERMS, 96), 0).astype(jnp.float32)
    q1, q2, t1, t2 = digits(row, 2, 2, CHEB, CHEB)
    row_i, row_j = CHEB * q1 + t1, CHEB * q2 + t2

    def spread(level, a1):
        pick = jnp.where(row_i + (12 * a1).astype(jnp.float32) == lane, 1.0, 0.0)
        return jnp.dot(pick, slow_ref[level], precision=lax.Precision.HIGHEST, preferred_element_type=jnp.float32)

    def column(table, a2):
        picked = jnp.where(row_j + (12 * a2).astype(jnp.float32) == lane, table, 0.0)
        return jnp.broadcast_to(jnp.sum(picked, axis=1, keepdims=True), (TERMS, LANES))

    zero, one = jnp.int32(0), jnp.int32(1)
    vtab[0] = column(spread(0, zero), zero)

    def fill1(a1, carry):
        table = spread(1, a1)
        for a2 in range(2):
            vtab[1 + 2 * a1 + a2] = column(table, a2 * one)
        return carry

    lax.fori_loop(0, 2, fill1, 0)

    def fill2(z, carry):
        table = spread(2, z)
        for a2 in range(2):
            vtab[5 + 2 * z + a2] = column(table, 2 * a2 + core)
        return carry

    lax.fori_loop(0, 4, fill2, 0)
    left_rows = lax.broadcasted_iota(jnp.int32, (TERMS, LANES), 1) < 64

    def fill3(a1, carry):
        table = spread(3, a1)
        for a2 in range(2):
            box = 2 * (2 * a2 + core)
            vtab[13 + 2 * a1 + a2] = jnp.where(left_rows, column(table, box), column(table, box + 1))
        return carry

    lax.fori_loop(0, 8, fill3, 0)

    lanes = lax.broadcasted_iota(jnp.int32, (8, LANES), 1)
    low2 = reverse6(lax.rem(lanes, 64)) * 16
    lane2 = lax.div(lanes, 64) * 8 + low2
    back = 127 - lanes
    back_half = lax.div(lanes, 64) * 64 + 63 - lax.rem(lanes, 64)

    def permute(block, index):
        rows = [
            jnp.take_along_axis(block[8 * i : 8 * i + 8], index, axis=1, mode="promise_in_bounds")
            for i in range(block.shape[0] // 8)
        ]
        return jnp.concatenate(rows, axis=0)

    def magnitude(level, r1, c1, r2, c2):
        width = 2.0 ** (level + 1)
        k = (lax.div(r1, 1 << level).astype(jnp.float32) + 0.5) * width - N / 2
        step = (c1 - 0.5) * width
        k0 = k - step
        k2 = (lax.div(r2, jnp.full(r2.shape, 1 << level, jnp.int32)).astype(jnp.float32) + 0.5) * width - N / 2
        step2 = (c2 - 0.5) * width
        k20 = k2 - step2
        above = step * (k + k0) + step2 * (k2 + k20)
        return above / (jnp.sqrt(k * k + k2 * k2) + jnp.sqrt(k0 * k0 + k20 * k20))

    def interpolate(y_ref, child, table, blocks):
        y_ref[child] = jnp.dot(
            mix_ref[table], operand(jnp.concatenate(blocks, axis=1)), preferred_element_type=jnp.float32
        )

    def tiles(body):
        def tile(i, carry):
            body(i, pl.ds(pl.multiple_of(8 * i, 8), 8), pl.ds(pl.multiple_of(8 * i + TERMS, 8), 8))
            return carry

        lax.fori_loop(0, TERMS // 8, tile, 0, unroll=True)

    def added(total, co, si, y_ref, child, at, at_im, side):
        cols = pl.ds(side * LANES, LANES)
        y_re, y_im = y_ref[child, at, cols], y_ref[child, at_im, cols]
        re, im = co * y_re - si * y_im, co * y_im + si * y_re
        return (re, im) if total is None else (total[0] + re, total[1] + im)

    def exponentials(entry, slots, sizes):
        def tile(i, carry):
            at = pl.ds(pl.multiple_of(8 * i, 8), 8)
            for j in range(4):
                co, si = unit(vtab[slots[j], at, :] * sizes[j])
                e_tab[entry, j, 0, at, :] = co
                e_tab[entry, j, 1, at, :] = si
            return carry

        lax.fori_loop(0, TERMS // 8, tile, 0, unroll=3)

    def combine_cores(y_ref, dst, entry):
        def body(i, at, at_im):
            totals = [None, None]
            for c1 in range(2):
                for c2 in range(2):
                    co, si = e_tab[entry, 2 * c1 + c2, 0, at, :], e_tab[entry, 2 * c1 + c2, 1, at, :]
                    totals[0] = added(totals[0], co, si, y_ref, 2 * c1 + c2, at, at_im, 0)
                    totals[1] = added(totals[1], co, si, y_ref, 2 * c1 + 1 - c2, at, at_im, 1)
            for side in range(2):
                put(dst[side], i, totals[side])

        tiles(body)

    def combine_mirrored(y_ref, dst, entry, index):
        def body(i, at, at_im):
            for side in range(2):
                totals = [None, None]
                for c1 in range(2):
                    co, si = e_tab[entry, 2 * c1 + side, 0, at, :], e_tab[entry, 2 * c1 + side, 1, at, :]
                    for c2 in range(2):
                        totals[c2] = added(totals[c2], co, si, y_ref, 2 * c1 + c2, at, at_im, side)
                put(dst[side], i, [totals[0][part] + permute(totals[1][part], index) for part in range(2)])

        tiles(body)

    def put(dst, i, total):
        rows = pl.ds(pl.multiple_of(8 * lax.rem(i, 9), 8), 8)
        for part in range(2):
            dst[2 * part + lax.div(i, 9), rows, :] = total[part]

    def window(src, q1, q2):
        rows = pl.ds(pl.multiple_of(32 * q2, 8), 40)
        return jnp.concatenate([src[q1, rows, :], src[2 + q1, rows, :]], axis=0)

    products = (y_a, y_b, y_c, y_d)
    pairs = ((0, y_a, acc_a), (1, y_b, acc_b))

    def x_of(slot):
        dx = 2 * slot + lax.rem(my_x + core, 2)
        x = lax.rem(my_x - dx + 4, 4)
        return lax.div(x, 2), low1 + 4 * lax.div(x, 2) + 8 * core

    def box_of(box):
        other1 = 1 - lax.rem(box, 2)
        other2 = 1 - lax.rem(lax.rem(box, 2) + lax.div(box, 2), 2)
        return lax.rem(lax.div(my_z, 2) + other1, 2), lax.rem(lax.div(my_y, 2) + other2, 2)

    children = [(c1, c2) for c1 in range(2) for c2 in range(2)]

    def phases0(part, carry):
        z0, y0 = lax.rem(my_z + lax.div(part, 2), 2), lax.rem(part, 2)
        for slot in range(2):
            r1 = x_of(slot)[1] + 2 * z0
            sizes = [magnitude(0, r1 + c1, c1, lane2 + (c2 + 2 * y0), c2) for c1, c2 in children]
            exponentials(2 * part + slot, (0,) * 4, sizes)
        return carry

    def phases1(step, carry):
        a1, a2 = box_of(step)
        for slot in range(2):
            r1 = x_of(slot)[1]
            sizes = [magnitude(1, r1 + 2 * c1, c1, lane2 + 2 * c2, c2) for c1, c2 in children]
            exponentials(8 + 2 * step + slot, (1 + 2 * a1 + a2,) * 4, sizes)
        return carry

    def phases2(step, carry):
        a1, a2 = box_of(step)
        sizes = [
            magnitude(2, low1 + 4 * c1 + 8 * x0, c1, lane2, 0) for c1 in range(2) for x0 in (core, 1 - core)
        ]
        for z0 in range(2):
            exponentials(16 + 2 * step + z0, (5 + 2 * (2 * a1 + z0) + a2,) * 4, sizes)
        return carry

    def phases3(step, carry):
        a1, a2 = box_of(step)
        sizes = [magnitude(3, low1 + 8 * c1, c1, low2, 0) for c1 in range(2) for side in range(2)]
        for z0 in range(2):
            slot = 13 + 4 * (2 * a1 + z0) + a2
            exponentials(24 + 2 * step + z0, (slot, slot + 2, slot, slot + 2), sizes)
        return carry

    def level0(half):
        pltpu.make_async_copy(xin.at[0], xin.at[0], in_recv.at[half]).wait()
        z0 = lax.rem(my_z + half, 2)
        jobs = [(slot, y0, products[2 * y0 + slot]) for y0 in range(2) for slot in range(2)]
        for slot, y0, y_ref in jobs:
            for c1, c2 in children:
                z = 2 * c1 + z0
                first = xin[slot, 0, z, 2 * c2 + y0]
                second = permute(xin[slot, 1, z, 2 * c2 + 1 - y0], back)
                interpolate(y_ref, 2 * c1 + c2, 2 * c1 + c2, [first, second])
        for slot, y0, y_ref in jobs:
            combine_cores(y_ref, (s0.at[slot, z0, y0, 0], s0.at[slot, z0, 1 - y0, 1]), 4 * half + 2 * y0 + slot)

    mixing_tables(mix_ref, raw_ref)
    for phases in (phases0, phases1, phases2):
        lax.fori_loop(0, 4, phases, 0)

    def arrived(half, carry):
        level0(half)

        @pl.when(half == 0)
        def _():
            lax.fori_loop(0, 4, phases3, 0)

        return carry

    lax.fori_loop(0, 2, arrived, 0)

    def level1(half):
        jobs = [(2 * half + i, slot, products[2 * i + slot]) for i in range(2) for slot in range(2)]
        for box, slot, y_ref in jobs:
            a1, a2 = box_of(box)
            for c1, c2 in children:
                blocks = [window(s0.at[slot, c1, c2, side], a1, a2) for side in range(2)]
                interpolate(y_ref, 2 * c1 + c2, 4 + 4 * a2 + 2 * c1 + c2, blocks)
        for box, slot, y_ref in jobs:
            x1 = x_of(slot)[0]
            combine_cores(y_ref, (z1.at[box, x1, 0], z1.at[box, x1, 1]), 8 + 2 * box + slot)
            if slot == 1:
                pltpu.make_async_remote_copy(
                    src_ref=z1.at[box, :, :, :, pl.ds(pl.multiple_of(32 * (1 - core), 8), 40), :],
                    dst_ref=zr.at[box],
                    send_sem=sib_send.at[box],
                    recv_sem=sib_recv.at[box],
                    device_id=(bx, my_y * 2 + 1 - core),
                    device_id_type=MESH,
                ).start()

    left = lax.broadcasted_iota(jnp.int32, (PAD, LANES), 1) < 64
    left_half = lax.broadcasted_iota(jnp.int32, (HALF, LANES), 1) < 64

    def level23(half, i):
        z0 = lax.rem(my_z + i, 2)
        jobs = [(2 * half + j, j, y_ref, acc_ref) for j, y_ref, acc_ref in pairs]
        for box, j, y_ref, _ in jobs:
            for c1, c2 in children:
                other = zr.at[box, c1, c2]
                blocks = [
                    window(z1.at[box, c1, c2], z0, core),
                    jnp.concatenate([other[z0], other[2 + z0]], axis=0),
                ]
                interpolate(y_ref, 2 * c1 + c2, 4 + 4 * core + 2 * c1 + c2, blocks)
        for box, j, y_ref, _ in jobs:
            combine_mirrored(y_ref, (s2.at[j, 0], s2.at[j, 1]), 16 + 2 * box + z0, back)
        for box, j, y_ref, _ in jobs:
            for c1 in range(2):
                src = s2.at[j, lax.rem(c1 + core, 2)]
                near, far = [], []
                for x1 in range(2):
                    first = window(src, x1, 0)
                    second = window(src, x1, 1)
                    second = jnp.concatenate([second[4:40], second[36:40], second[44:80], second[76:80]], axis=0)
                    near.append(jnp.where(left, first, pltpu.roll(second, 64, 1)))
                    far.append(jnp.where(left, permute(first, back), permute(second, back_half)))
                interpolate(y_ref, 2 * c1, 4 + 2 * c1, near)
                interpolate(y_ref, 2 * c1 + 1, 4 + 2 * c1 + 1, far)
        for box, j, y_ref, acc_ref in jobs:
            combine_mirrored(y_ref, (acc_ref.at[0], acc_ref.at[1]), 24 + 2 * box + z0, back_half)
            for x1 in range(2):
                for q1 in range(2):
                    for part in range(2):
                        upper = acc_ref[x1, 2 * part + q1, 0:HALF, :]
                        lower = acc_ref[x1, 2 * part + q1, HALF:ROWS, :]
                        rows = pl.ds(HALF * part, HALF)
                        obuf[box, i, x1, q1, 0, rows, :] = jnp.where(left_half, upper, pltpu.roll(lower, 64, 1))
                        obuf[box, i, x1, q1, 1, rows, :] = jnp.where(left_half, pltpu.roll(upper, 64, 1), lower)

    def send_out(half, i, number):
        turn, round_ = lax.rem(number, 2), lax.div(number, 2)
        box = 2 * half + lax.rem(turn + core, 2)
        a1, a2 = box_of(box)
        x = lax.rem(my_x + 1 + 2 * core + round_ + 2 * turn, 4)
        c = lax.rem(lax.div(round_, 4) + core, 2)
        to_bx, to_by = (2 * a1 + lax.rem(my_z + i, 2)) * 4 + x, 2 * (2 * a2 + core) + c
        src, dst = obuf.at[box, i, lax.div(x, 2), lax.rem(x, 2), c], orecv.at[chip]
        here = jnp.logical_and(to_bx == bx, to_by == by)

        @pl.when(here)
        def _():
            pltpu.make_async_copy(src, dst, out_recv.at[box]).start()

        @pl.when(jnp.logical_not(here))
        def _():
            pltpu.make_async_remote_copy(
                src_ref=src, dst_ref=dst, send_sem=out_send, recv_sem=out_recv.at[box],
                device_id=(to_bx, to_by), device_id_type=MESH,
            ).start()

    def two_boxes(half, carry):
        level1(half)
        for box in range(2):
            pltpu.make_async_copy(zr.at[0], zr.at[0], sib_recv.at[2 * half + box]).wait()

        def both_z(i, carry):
            level23(half, i)

            def send_some(number, carry):
                send_out(half, i, number)
                return carry

            lax.fori_loop(0, 16, send_some, 0)
            return carry

        lax.fori_loop(0, 2, both_z, 0)
        return carry

    lax.fori_loop(0, 2, two_boxes, 0)

    def settle(step, carry):
        pltpu.make_async_copy(zr.at[0], zr.at[0], sib_send.at[step]).wait()
        return carry

    lax.fori_loop(0, 4, settle, 0)
    for keeps, sem in ((my_x0 == core, in_send), (lax.rem(my_y, 2) == core, out_send)):

        @pl.when(keeps)
        def _(sem=sem):
            pltpu.make_async_copy(sbuf.at[pl.ds(0, 63)], sbuf.at[pl.ds(0, 63)], sem).wait()

        @pl.when(jnp.logical_not(keeps))
        def _(sem=sem):
            pltpu.make_async_copy(sbuf, sbuf, sem).wait()

    def arrive(step, carry):
        pltpu.make_async_copy(orecv.at[pl.ds(0, 16)], orecv.at[pl.ds(0, 16)], out_recv.at[step]).wait()
        z1_from, y1_from = box_of(step)

        def scatter_rows(i, carry):
            z, x, y = 2 * z1_from + lax.div(i, 8), lax.rem(lax.div(i, 2), 4), 2 * y1_from + lax.rem(i, 2)
            ell = z * 16 + x * 4 + y
            for tile in range(9):
                out_ref[pl.ds(tile * 512 + ell, 8, stride=64), :] = orecv[ell, 8 * tile : 8 * tile + 8, :]
            return carry

        lax.fori_loop(0, 16, scatter_rows, 0, unroll=4)
        return carry

    lax.fori_loop(0, 4, arrive, 0)


def shards(coefficients, slowness):
    rows = jnp.transpose(coefficients, (0, 1, 3, 2, 4)).reshape(ROWS * 64, LANES)
    operands = (rows, pltpu.with_memory_space_constraint(slowness, pltpu.HBM))
    dense = (ROWS, LANES)
    scratch = [pltpu.VMEM(operands[i].shape, jnp.float32) for i in range(2)]
    scratch += [pltpu.VMEM((12, 2 * TERMS, DEPTH), jnp.bfloat16), pltpu.VMEM((4, 2 * TERMS, DEPTH), jnp.float32)]
    scratch += [
        pltpu.VMEM(shape, jnp.float32)
        for shape in (
            (64,) + dense,
            (2, 2, 4, 4) + dense,
            (2, 2, 2, 2, 4) + dense,
            (4, 2, 2, 4) + dense,
            (4, 2, 2, 4, 40, LANES),
            (2, 2, 4) + dense,
            (4, 2, 2, 2, 2) + dense,
            (64,) + dense,
            (29, TERMS, LANES),
            (32, 4, 2, TERMS, LANES),
            (4, 2 * TERMS, 2 * LANES),
            (4, 2 * TERMS, 2 * LANES),
            (4, 2 * TERMS, 2 * LANES),
            (4, 2 * TERMS, 2 * LANES),
            (2, 4) + dense,
            (2, 4) + dense,
        )
    ]
    scratch += [
        pltpu.SemaphoreType.DMA((4,)),
        pltpu.SemaphoreType.DMA,
        pltpu.SemaphoreType.DMA((2,)),
        pltpu.SemaphoreType.DMA((4,)),
        pltpu.SemaphoreType.DMA((4,)),
        pltpu.SemaphoreType.DMA,
        pltpu.SemaphoreType.DMA((4,)),
    ]
    out = pl.pallas_call(
        kernel,
        out_shape=jax.ShapeDtypeStruct((ROWS * 64, LANES), jnp.float32),
        in_specs=[pl.BlockSpec(memory_space=pl.ANY), pl.BlockSpec(memory_space=pltpu.HBM)],
        out_specs=pl.BlockSpec(memory_space=pltpu.VMEM),
        scratch_shapes=scratch,
        compiler_params=pltpu.CompilerParams(collective_id=0, has_side_effects=True, vmem_limit_bytes=50 << 20),
    )(*operands)
    return jnp.transpose(out.reshape(2, CHEB, CHEB, 64, LANES), (0, 1, 3, 2, 4))


def solution(mesh):
    placed = (P(None, None, "bx", None, "by"), P())
    return jax.shard_map(
        shards,
        mesh=mesh,
        in_specs=placed,
        out_specs=P(None, None, "bx", None, "by"),
        check_vma=False,
    )
```

```python
import math

import jax
import jax.numpy as jnp
import numpy as np
from jax import lax
from jax.experimental import pallas as pl
from jax.experimental.pallas import tpu as pltpu
from jax.sharding import PartitionSpec as P

N = 2048
CHEB = 6
HALF = CHEB * CHEB
ROWS = 2 * HALF
TERMS = 4 * HALF
PAD = 80
DEPTH = 256
LANES = 128
MESH = pl.DeviceIdType.MESH


def cheb_points():
    return np.cos(np.pi * (2 * np.arange(CHEB) + 1) / (2 * CHEB))


def fit(function, degree):
    count = 200
    s = 0.125 * (1 + np.cos(np.pi * (2 * np.arange(count) + 1) / (2 * count)))
    series = np.polynomial.chebyshev.Chebyshev.fit(s, function(np.sqrt(s)), degree, domain=[0, 0.25])
    return [float(c) for c in series.convert(kind=np.polynomial.Polynomial).coef]


SIN = fit(lambda r: math.sqrt(2) * np.sin(np.pi * r) / r, 3)
COS = fit(lambda r: math.sqrt(2) * np.cos(np.pi * r), 4)
WHOLE = 1.5 * 2.0**23


POINTS = [float(point) for point in cheb_points()]
SCALES = [
    float(1 / np.prod([cheb_points()[s] - cheb_points()[j] for j in range(CHEB) if j != s])) for s in range(CHEB)
]


def horner(coefficients, s):
    value = s * coefficients[-1] + coefficients[-2]
    for coefficient in coefficients[-3::-1]:
        value = value * s + coefficient
    return value


def unit(turns):
    r = turns - ((turns + WHOLE) - WHOLE)
    s = r * r
    half = horner(SIN, s) * r
    return 1.0 - half * half, half * horner(COS, s)


def operand(block):
    if block.shape[0] < PAD:
        block = jnp.concatenate([block, jnp.zeros((PAD - block.shape[0], block.shape[1]), jnp.float32)], axis=0)
    high = block.astype(jnp.bfloat16)
    low = (block - high.astype(jnp.float32)).astype(jnp.bfloat16)
    return jnp.concatenate([high, low, high, jnp.zeros((DEPTH - 3 * PAD, block.shape[1]), jnp.bfloat16)], axis=0)


def choose(index, values):
    result = jnp.full(index.shape, values[0], jnp.float32)
    for number, value in enumerate(values[1:], 1):
        result = jnp.where(index == number, value, result)
    return result


def digits(value, *sizes):
    out = []
    for size in sizes[::-1]:
        rest = jnp.floor((value + 0.5) * (1.0 / size))
        out.append(value - rest * size)
        value = rest
    return out[::-1]


def lagrange(at, source):
    product = choose(source, SCALES)
    for number, point in enumerate(POINTS):
        product = product * jnp.where(source == number, 1.0, at - point)
    return product


def mixing_tables(mix_ref, raw_ref):
    shape = (HALF, DEPTH)
    column = lax.broadcasted_iota(jnp.int32, shape, 1).astype(jnp.float32)
    copy, inside = digits(column, 4, PAD)
    row = lax.broadcasted_iota(jnp.int32, shape, 0).astype(jnp.float32)
    t1, t2 = digits(row, CHEB, CHEB)
    second = inside >= 40
    place = inside - jnp.where(second, 40.0, 0.0)
    used = jnp.logical_and(place < HALF, copy < 3)
    s1, s2 = digits(jnp.minimum(place, HALF - 1.0), CHEB, CHEB)
    at1, at2 = choose(t1, POINTS) * 0.5, choose(t2, POINTS) * 0.5
    weights1 = [jnp.where(used, lagrange(q - 0.5 + at1, s1), 0.0) for q in range(2)]
    weights2 = [lagrange(q - 0.5 + at2, s2) for q in range(2)]
    for q1 in range(2):
        for q2 in range(2):
            weights = weights1[q1] * weights2[q2]
            turns1, turns2 = 0.5 * (q1 + 0.5 + at1), 0.5 * (q2 + 0.5 + at2)
            plus, minus = unit(turns1 + turns2), unit(turns1 - turns2)
            for c1 in range(2):
                for c2 in range(2):
                    co, si = plus if c1 == c2 else minus
                    si = si if c1 else -si
                    real, imag = co * weights, si * weights
                    for part, values in enumerate((jnp.where(second, -imag, real), jnp.where(second, real, imag))):
                        high = values.astype(jnp.bfloat16).astype(jnp.float32)
                        values = jnp.where(copy < 2, high, values - high)
                        base = part * TERMS + q1 * ROWS + q2 * HALF
                        raw_ref[2 * c1 + c2, base : base + HALF, :] = values

    shape = (48, DEPTH)
    copy, inside = digits(lax.broadcasted_iota(jnp.int32, shape, 1).astype(jnp.float32), 4, PAD)

    def variants(i, carry):
        table, rows = lax.div(i, 6), pl.ds(pl.multiple_of(48 * lax.rem(i, 6), 16), 48)
        values = raw_ref[table, rows, :]
        dense = jnp.where(inside < HALF, values, pltpu.roll(values, DEPTH - 4, 1))
        dense = jnp.where(inside < ROWS, dense, 0.0)
        for variant, block in enumerate((dense, values, pltpu.roll(values, 4, 1))):
            mix_ref[4 * variant + table, rows, :] = block.astype(jnp.bfloat16)
        return carry

    lax.fori_loop(0, 24, variants, 0)


def reverse6(value):
    total = 0
    for bit in range(6):
        total = total + lax.rem(lax.div(value, 1 << bit), 2) * (1 << (5 - bit))
    return total


def kernel(
    coef_hbm, slow_hbm, out_ref,
    coef_ref, slow_ref, mix_ref, raw_ref,
    sbuf, xin, s0, z1, zr, s2, obuf, orecv, vtab, e_tab, y_a, y_b, acc_a, acc_b,
    load, in_send, in_recv, sib_send, sib_recv, out_send, out_recv,
):
    bx, by = lax.axis_index("bx"), lax.axis_index("by")
    my_z, my_x = lax.div(bx, 4), lax.rem(bx, 4)
    my_y, core = lax.div(by, 2), lax.rem(by, 2)
    my_x0 = lax.rem(my_x, 2)
    chip = bx * 4 + my_y
    low1 = reverse6(chip) * 16

    loads = [
        pltpu.make_async_copy(src, dst, load.at[i])
        for i, (src, dst) in enumerate(
            ((coef_hbm, coef_ref), (slow_hbm, slow_ref))
        )
    ]
    for copy in loads:
        copy.start()

    barrier = pltpu.get_barrier_semaphore()
    me = bx * 8 + by

    def greet(i, carry):
        there = lax.rem(me + i, 128)
        pl.semaphore_signal(barrier, inc=1, device_id=(lax.div(there, 8), lax.rem(there, 8)), device_id_type=MESH)
        return carry

    lax.fori_loop(1, 121, greet, 0, unroll=8)
    lax.fori_loop(121, 128, greet, 0, unroll=7)
    loads[0].wait()

    def gather_rows(ell, carry):
        for tile in range(9):
            sbuf[ell, 8 * tile : 8 * tile + 8, :] = coef_ref[pl.ds(tile * 512 + ell, 8, stride=64), :]
        return carry

    lax.fori_loop(0, 64, gather_rows, 0, unroll=8)
    pl.semaphore_wait(barrier, 127)

    def send_in(step, carry):
        half, part, inner = lax.div(step, 32), lax.div(step, 16), lax.rem(step, 16)
        even, far_z = lax.rem(inner + core, 2), lax.rem(lax.div(inner, 2), 2)
        dx = (1 - even) * (2 * half + 1) + even * 2 * lax.rem(half + my_x0, 2)
        dy = lax.rem(lax.div(inner, 4) + lax.rem(inner, 2) + 2 * far_z + 2 * core, 4)
        dz = lax.rem(lax.rem(part, 2) + 2 * far_z + 2 * core, 4)
        to_x, to_z, to_y = lax.rem(my_x + dx, 4), lax.rem(my_z + dz, 4), lax.rem(my_y + dy, 4)
        to_bx, to_by = to_z * 4 + to_x, to_y * 2 + my_x0
        ell = to_z * 16 + to_x * 4 + to_y
        src = sbuf.at[ell]
        dst = xin.at[half, core, my_z, my_y]
        here = jnp.logical_and(to_bx == bx, to_by == by)

        @pl.when(here)
        def _():
            pltpu.make_async_copy(src, dst, in_recv.at[part]).start()

        @pl.when(jnp.logical_not(here))
        def _():
            pltpu.make_async_remote_copy(
                src_ref=src, dst_ref=dst, send_sem=in_send, recv_sem=in_recv.at[part],
                device_id=(to_bx, to_by), device_id_type=MESH,
            ).start()

        return carry

    lax.fori_loop(0, 64, send_in, 0)

    loads[1].wait()
    lane = lax.broadcasted_iota(jnp.int32, (TERMS, 96), 1).astype(jnp.float32)
    row = lax.broadcasted_iota(jnp.int32, (TERMS, 96), 0).astype(jnp.float32)
    q1, q2, t1, t2 = digits(row, 2, 2, CHEB, CHEB)
    row_i, row_j = CHEB * q1 + t1, CHEB * q2 + t2

    def spread(level, a1):
        pick = jnp.where(row_i + (12 * a1).astype(jnp.float32) == lane, 1.0, 0.0)
        return jnp.dot(pick, slow_ref[level], precision=lax.Precision.HIGHEST, preferred_element_type=jnp.float32)

    def column(table, a2):
        picked = jnp.where(row_j + (12 * a2).astype(jnp.float32) == lane, table, 0.0)
        return jnp.broadcast_to(jnp.sum(picked, axis=1, keepdims=True), (TERMS, LANES))

    zero, one = jnp.int32(0), jnp.int32(1)
    vtab[0] = column(spread(0, zero), zero)

    def fill1(a1, carry):
        table = spread(1, a1)
        for a2 in range(2):
            vtab[1 + 2 * a1 + a2] = column(table, a2 * one)
        return carry

    lax.fori_loop(0, 2, fill1, 0)

    def fill2(z, carry):
        table = spread(2, z)
        for a2 in range(2):
            vtab[5 + 2 * z + a2] = column(table, 2 * a2 + core)
        return carry

    lax.fori_loop(0, 4, fill2, 0)
    left_rows = lax.broadcasted_iota(jnp.int32, (TERMS, LANES), 1) < 64

    def fill3(a1, carry):
        table = spread(3, a1)
        for a2 in range(2):
            box = 2 * (2 * a2 + core)
            vtab[13 + 2 * a1 + a2] = jnp.where(left_rows, column(table, box), column(table, box + 1))
        return carry

    lax.fori_loop(0, 8, fill3, 0)

    lanes = lax.broadcasted_iota(jnp.int32, (8, LANES), 1)
    low2 = reverse6(lax.rem(lanes, 64)) * 16
    lane2 = lax.div(lanes, 64) * 8 + low2
    back = 127 - lanes
    back_half = lax.div(lanes, 64) * 64 + 63 - lax.rem(lanes, 64)

    def permute(block, index):
        rows = [
            jnp.take_along_axis(block[8 * i : 8 * i + 8], index, axis=1, mode="promise_in_bounds")
            for i in range(block.shape[0] // 8)
        ]
        return jnp.concatenate(rows, axis=0)

    def magnitude(level, r1, c1, r2, c2):
        width = 2.0 ** (level + 1)
        k = (lax.div(r1, 1 << level).astype(jnp.float32) + 0.5) * width - N / 2
        step = (c1 - 0.5) * width
        k0 = k - step
        k2 = (lax.div(r2, jnp.full(r2.shape, 1 << level, jnp.int32)).astype(jnp.float32) + 0.5) * width - N / 2
        step2 = (c2 - 0.5) * width
        k20 = k2 - step2
        above = step * (k + k0) + step2 * (k2 + k20)
        return above / (jnp.sqrt(k * k + k2 * k2) + jnp.sqrt(k0 * k0 + k20 * k20))

    def interpolate(y_ref, child, table, blocks):
        y_ref[child] = jnp.dot(
            mix_ref[table], operand(jnp.concatenate(blocks, axis=1)), preferred_element_type=jnp.float32
        )

    def tiles(body):
        def tile(i, carry):
            body(i, pl.ds(pl.multiple_of(8 * i, 8), 8), pl.ds(pl.multiple_of(8 * i + TERMS, 8), 8))
            return carry

        lax.fori_loop(0, TERMS // 8, tile, 0, unroll=True)

    def added(total, co, si, y_ref, child, at, at_im, side):
        cols = pl.ds(side * LANES, LANES)
        y_re, y_im = y_ref[child, at, cols], y_ref[child, at_im, cols]
        re, im = co * y_re - si * y_im, co * y_im + si * y_re
        return (re, im) if total is None else (total[0] + re, total[1] + im)

    def exponentials(entry, slots, sizes):
        def tile(i, carry):
            at = pl.ds(pl.multiple_of(8 * i, 8), 8)
            for j in range(4):
                co, si = unit(vtab[slots[j], at, :] * sizes[j])
                e_tab[entry, j, 0, at, :] = co
                e_tab[entry, j, 1, at, :] = si
            return carry

        lax.fori_loop(0, TERMS // 8, tile, 0, unroll=3)

    def combine_cores(y_ref, dst, entry):
        def body(i, at, at_im):
            totals = [None, None]
            for c1 in range(2):
                for c2 in range(2):
                    co, si = e_tab[entry, 2 * c1 + c2, 0, at, :], e_tab[entry, 2 * c1 + c2, 1, at, :]
                    totals[0] = added(totals[0], co, si, y_ref, 2 * c1 + c2, at, at_im, 0)
                    totals[1] = added(totals[1], co, si, y_ref, 2 * c1 + 1 - c2, at, at_im, 1)
            for side in range(2):
                put(dst[side], i, totals[side])

        tiles(body)

    def combine_mirrored(y_ref, dst, entry, index):
        def body(i, at, at_im):
            for side in range(2):
                totals = [None, None]
                for c1 in range(2):
                    co, si = e_tab[entry, 2 * c1 + side, 0, at, :], e_tab[entry, 2 * c1 + side, 1, at, :]
                    for c2 in range(2):
                        totals[c2] = added(totals[c2], co, si, y_ref, 2 * c1 + c2, at, at_im, side)
                put(dst[side], i, [totals[0][part] + permute(totals[1][part], index) for part in range(2)])

        tiles(body)

    def put(dst, i, total):
        rows = pl.ds(pl.multiple_of(8 * lax.rem(i, 9), 8), 8)
        for part in range(2):
            dst[2 * part + lax.div(i, 9), rows, :] = total[part]

    def window(src, q1, q2):
        rows = pl.ds(pl.multiple_of(32 * q2, 8), 40)
        return jnp.concatenate([src[q1, rows, :], src[2 + q1, rows, :]], axis=0)

    pairs = ((0, y_a, acc_a), (1, y_b, acc_b))

    def x_of(slot):
        odd = lax.rem(my_x + core, 2)
        dx = odd * (2 * slot + 1) + (1 - odd) * 2 * lax.rem(slot + core, 2)
        x = lax.rem(my_x - dx + 4, 4)
        return lax.div(x, 2), low1 + 4 * lax.div(x, 2) + 8 * core

    def box_of(box):
        other1 = 1 - lax.rem(box, 2)
        other2 = 1 - lax.rem(lax.rem(box, 2) + lax.div(box, 2), 2)
        return lax.rem(lax.div(my_z, 2) + other1, 2), lax.rem(lax.div(my_y, 2) + other2, 2)

    children = [(c1, c2) for c1 in range(2) for c2 in range(2)]

    def phases0(part, carry):
        z0 = lax.rem(my_z + part, 2)
        r1 = x_of(lax.div(part, 2))[1] + 2 * z0
        for y0 in range(2):
            sizes = [magnitude(0, r1 + c1, c1, lane2 + (c2 + 2 * y0), c2) for c1, c2 in children]
            exponentials(2 * part + y0, (0,) * 4, sizes)
        return carry

    def phases1(step, carry):
        a1, a2 = box_of(step)
        for slot in range(2):
            r1 = x_of(slot)[1]
            sizes = [magnitude(1, r1 + 2 * c1, c1, lane2 + 2 * c2, c2) for c1, c2 in children]
            exponentials(8 + 2 * step + slot, (1 + 2 * a1 + a2,) * 4, sizes)
        return carry

    def phases2(step, carry):
        a1, a2 = box_of(step)
        sizes = [
            magnitude(2, low1 + 4 * c1 + 8 * x0, c1, lane2, 0) for c1 in range(2) for x0 in (core, 1 - core)
        ]
        for z0 in range(2):
            exponentials(16 + 2 * step + z0, (5 + 2 * (2 * a1 + z0) + a2,) * 4, sizes)
        return carry

    def phases3(step, carry):
        a1, a2 = box_of(step)
        sizes = [magnitude(3, low1 + 8 * c1, c1, low2, 0) for c1 in range(2) for side in range(2)]
        for z0 in range(2):
            slot = 13 + 4 * (2 * a1 + z0) + a2
            exponentials(24 + 2 * step + z0, (slot, slot + 2, slot, slot + 2), sizes)
        return carry

    def level0(part, carry):
        pltpu.make_async_copy(xin.at[0, 0], xin.at[0, 0], in_recv.at[part]).wait()
        slot, z0 = lax.div(part, 2), lax.rem(my_z + part, 2)
        for y0, y_ref, _ in pairs:
            for c1, c2 in children:
                z = 2 * c1 + z0
                first = xin[slot, 0, z, 2 * c2 + y0]
                second = permute(xin[slot, 1, z, 2 * c2 + 1 - y0], back)
                interpolate(y_ref, 2 * c1 + c2, 2 * c1 + c2, [first, second])
        for y0, y_ref, _ in pairs:
            combine_cores(y_ref, (s0.at[slot, z0, y0, 0], s0.at[slot, z0, 1 - y0, 1]), 2 * part + y0)
        return carry

    def level1(half, slot):
        x1 = x_of(slot)[0]
        for i, y_ref, _ in pairs:
            a1, a2 = box_of(2 * half + i)
            for c1, c2 in children:
                blocks = [window(s0.at[slot, c1, c2, side], a1, a2) for side in range(2)]
                interpolate(y_ref, 2 * c1 + c2, 4 + 4 * a2 + 2 * c1 + c2, blocks)
        for i, y_ref, _ in pairs:
            box = 2 * half + i
            combine_cores(y_ref, (z1.at[box, x1, 0], z1.at[box, x1, 1]), 8 + 2 * box + slot)
            pltpu.make_async_remote_copy(
                src_ref=z1.at[box, x1, :, :, pl.ds(pl.multiple_of(32 * (1 - core), 8), 40), :],
                dst_ref=zr.at[box, x1],
                send_sem=sib_send.at[box],
                recv_sem=sib_recv.at[box],
                device_id=(bx, my_y * 2 + 1 - core),
                device_id_type=MESH,
            ).start()

    mixing_tables(mix_ref, raw_ref)
    for phases, boxes in ((phases0, 4), (phases1, 4), (phases2, 2), (phases3, 2)):
        lax.fori_loop(0, boxes, phases, 0)

    def first_slot(half, carry):
        level1(half, 0)
        return carry

    lax.fori_loop(0, 2, level0, 0)
    lax.fori_loop(0, 2, first_slot, 0)
    lax.fori_loop(2, 4, level0, 0)

    left = lax.broadcasted_iota(jnp.int32, (PAD, LANES), 1) < 64
    left_half = lax.broadcasted_iota(jnp.int32, (HALF, LANES), 1) < 64

    def level23(half, i):
        z0 = lax.rem(my_z + i, 2)
        jobs = [(2 * half + j, j, y_ref, acc_ref) for j, y_ref, acc_ref in pairs]
        for box, j, y_ref, _ in jobs:
            for c1, c2 in children:
                other = zr.at[box, c1, c2]
                blocks = [
                    window(z1.at[box, c1, c2], z0, core),
                    jnp.concatenate([other[z0], other[2 + z0]], axis=0),
                ]
                interpolate(y_ref, 2 * c1 + c2, 4 + 4 * core + 2 * c1 + c2, blocks)
        for box, j, y_ref, _ in jobs:
            combine_mirrored(y_ref, (s2.at[j, 0], s2.at[j, 1]), 16 + 2 * box + z0, back)
        for box, j, y_ref, _ in jobs:
            for c1 in range(2):
                src = s2.at[j, lax.rem(c1 + core, 2)]
                near, far = [], []
                for x1 in range(2):
                    first = window(src, x1, 0)
                    second = window(src, x1, 1)
                    second = jnp.concatenate([second[4:40], second[36:40], second[44:80], second[76:80]], axis=0)
                    near.append(jnp.where(left, first, pltpu.roll(second, 64, 1)))
                    far.append(jnp.where(left, permute(first, back), permute(second, back_half)))
                interpolate(y_ref, 2 * c1, 4 + 2 * c1, near)
                interpolate(y_ref, 2 * c1 + 1, 4 + 2 * c1 + 1, far)
        for box, j, y_ref, acc_ref in jobs:
            combine_mirrored(y_ref, (acc_ref.at[0], acc_ref.at[1]), 24 + 2 * box + z0, back_half)
            for x1 in range(2):
                for q1 in range(2):
                    for part in range(2):
                        upper = acc_ref[x1, 2 * part + q1, 0:HALF, :]
                        lower = acc_ref[x1, 2 * part + q1, HALF:ROWS, :]
                        rows = pl.ds(HALF * part, HALF)
                        obuf[box, i, x1, q1, 0, rows, :] = jnp.where(left_half, upper, pltpu.roll(lower, 64, 1))
                        obuf[box, i, x1, q1, 1, rows, :] = jnp.where(left_half, pltpu.roll(upper, 64, 1), lower)

    def send_out(half, i, number):
        turn, round_ = lax.rem(number, 2), lax.div(number, 2)
        box = 2 * half + lax.rem(turn + core, 2)
        a1, a2 = box_of(box)
        x = lax.rem(my_x + 1 + 2 * core + round_ + 2 * turn, 4)
        c = lax.rem(lax.div(round_, 4) + core, 2)
        to_bx, to_by = (2 * a1 + lax.rem(my_z + i, 2)) * 4 + x, 2 * (2 * a2 + core) + c
        src, dst = obuf.at[box, i, lax.div(x, 2), lax.rem(x, 2), c], orecv.at[chip]
        here = jnp.logical_and(to_bx == bx, to_by == by)

        @pl.when(here)
        def _():
            pltpu.make_async_copy(src, dst, out_recv.at[box]).start()

        @pl.when(jnp.logical_not(here))
        def _():
            pltpu.make_async_remote_copy(
                src_ref=src, dst_ref=dst, send_sem=out_send, recv_sem=out_recv.at[box],
                device_id=(to_bx, to_by), device_id_type=MESH,
            ).start()

    def two_boxes(half, carry):
        level1(half, 1)
        for box in range(2):
            pltpu.make_async_copy(zr.at[0], zr.at[0], sib_recv.at[2 * half + box]).wait()

        def both_z(i, carry):
            level23(half, i)

            def send_some(number, carry):
                send_out(half, i, number)
                return carry

            lax.fori_loop(0, 16, send_some, 0)
            return carry

        lax.fori_loop(0, 2, both_z, 0)

        @pl.when(half == 0)
        def _():
            for phases in (phases2, phases3):
                lax.fori_loop(2, 4, phases, 0)

        return carry

    lax.fori_loop(0, 2, two_boxes, 0)

    def settle(step, carry):
        pltpu.make_async_copy(zr.at[0], zr.at[0], sib_send.at[step]).wait()
        return carry

    lax.fori_loop(0, 4, settle, 0)
    for keeps, sem in ((my_x0 == core, in_send), (lax.rem(my_y, 2) == core, out_send)):

        @pl.when(keeps)
        def _(sem=sem):
            pltpu.make_async_copy(sbuf.at[pl.ds(0, 63)], sbuf.at[pl.ds(0, 63)], sem).wait()

        @pl.when(jnp.logical_not(keeps))
        def _(sem=sem):
            pltpu.make_async_copy(sbuf, sbuf, sem).wait()

    def arrive(step, carry):
        pltpu.make_async_copy(orecv.at[pl.ds(0, 16)], orecv.at[pl.ds(0, 16)], out_recv.at[step]).wait()
        z1_from, y1_from = box_of(step)

        def scatter_rows(i, carry):
            z, x, y = 2 * z1_from + lax.div(i, 8), lax.rem(lax.div(i, 2), 4), 2 * y1_from + lax.rem(i, 2)
            ell = z * 16 + x * 4 + y
            for tile in range(9):
                out_ref[pl.ds(tile * 512 + ell, 8, stride=64), :] = orecv[ell, 8 * tile : 8 * tile + 8, :]
            return carry

        lax.fori_loop(0, 16, scatter_rows, 0, unroll=4)
        return carry

    lax.fori_loop(0, 4, arrive, 0)


def shards(coefficients, slowness):
    rows = jnp.transpose(coefficients, (0, 1, 3, 2, 4)).reshape(ROWS * 64, LANES)
    operands = (rows, pltpu.with_memory_space_constraint(slowness, pltpu.HBM))
    dense = (ROWS, LANES)
    scratch = [pltpu.VMEM(operands[i].shape, jnp.float32) for i in range(2)]
    scratch += [pltpu.VMEM((12, 2 * TERMS, DEPTH), jnp.bfloat16), pltpu.VMEM((4, 2 * TERMS, DEPTH), jnp.float32)]
    scratch += [
        pltpu.VMEM(shape, jnp.float32)
        for shape in (
            (64,) + dense,
            (2, 2, 4, 4) + dense,
            (2, 2, 2, 2, 4) + dense,
            (4, 2, 2, 4) + dense,
            (4, 2, 2, 4, 40, LANES),
            (2, 2, 4) + dense,
            (4, 2, 2, 2, 2) + dense,
            (64,) + dense,
            (29, TERMS, LANES),
            (32, 4, 2, TERMS, LANES),
            (4, 2 * TERMS, 2 * LANES),
            (4, 2 * TERMS, 2 * LANES),
            (2, 4) + dense,
            (2, 4) + dense,
        )
    ]
    scratch += [
        pltpu.SemaphoreType.DMA((4,)),
        pltpu.SemaphoreType.DMA,
        pltpu.SemaphoreType.DMA((4,)),
        pltpu.SemaphoreType.DMA((4,)),
        pltpu.SemaphoreType.DMA((4,)),
        pltpu.SemaphoreType.DMA,
        pltpu.SemaphoreType.DMA((4,)),
    ]
    out = pl.pallas_call(
        kernel,
        out_shape=jax.ShapeDtypeStruct((ROWS * 64, LANES), jnp.float32),
        in_specs=[pl.BlockSpec(memory_space=pl.ANY), pl.BlockSpec(memory_space=pltpu.HBM)],
        out_specs=pl.BlockSpec(memory_space=pltpu.VMEM),
        scratch_shapes=scratch,
        compiler_params=pltpu.CompilerParams(collective_id=0, has_side_effects=True, vmem_limit_bytes=50 << 20),
    )(*operands)
    return jnp.transpose(out.reshape(2, CHEB, CHEB, 64, LANES), (0, 1, 3, 2, 4))


def solution(mesh):
    placed = (P(None, None, "bx", None, "by"), P())
    return jax.shard_map(
        shards,
        mesh=mesh,
        in_specs=placed,
        out_specs=P(None, None, "bx", None, "by"),
        check_vma=False,
    )
```

```python
import math

import jax
import jax.numpy as jnp
import numpy as np
from jax import lax
from jax.experimental import pallas as pl
from jax.experimental.pallas import tpu as pltpu
from jax.sharding import PartitionSpec as P

N = 2048
CHEB = 6
HALF = CHEB * CHEB
ROWS = 2 * HALF
TERMS = 4 * HALF
PAD = 80
DEPTH = 256
LANES = 128
MESH = pl.DeviceIdType.MESH


def cheb_points():
    return np.cos(np.pi * (2 * np.arange(CHEB) + 1) / (2 * CHEB))


def fit(function, degree):
    count = 200
    s = 0.125 * (1 + np.cos(np.pi * (2 * np.arange(count) + 1) / (2 * count)))
    series = np.polynomial.chebyshev.Chebyshev.fit(s, function(np.sqrt(s)), degree, domain=[0, 0.25])
    return [float(c) for c in series.convert(kind=np.polynomial.Polynomial).coef]


SIN = fit(lambda r: math.sqrt(2) * np.sin(np.pi * r) / r, 3)
COS = fit(lambda r: math.sqrt(2) * np.cos(np.pi * r), 4)
WHOLE = 1.5 * 2.0**23


POINTS = [float(point) for point in cheb_points()]
SCALES = [
    float(1 / np.prod([cheb_points()[s] - cheb_points()[j] for j in range(CHEB) if j != s])) for s in range(CHEB)
]


def horner(coefficients, s):
    value = s * coefficients[-1] + coefficients[-2]
    for coefficient in coefficients[-3::-1]:
        value = value * s + coefficient
    return value


def unit(turns):
    r = turns - ((turns + WHOLE) - WHOLE)
    s = r * r
    half = horner(SIN, s) * r
    return 1.0 - half * half, half * horner(COS, s)


def operand(block):
    if block.shape[0] < PAD:
        block = jnp.concatenate([block, jnp.zeros((PAD - block.shape[0], block.shape[1]), jnp.float32)], axis=0)
    high = block.astype(jnp.bfloat16)
    low = (block - high.astype(jnp.float32)).astype(jnp.bfloat16)
    return jnp.concatenate([high, low, high, jnp.zeros((DEPTH - 3 * PAD, block.shape[1]), jnp.bfloat16)], axis=0)


def choose(index, values):
    result = jnp.full(index.shape, values[0], jnp.float32)
    for number, value in enumerate(values[1:], 1):
        result = jnp.where(index == number, value, result)
    return result


def digits(value, *sizes):
    out = []
    for size in sizes[::-1]:
        rest = jnp.floor((value + 0.5) * (1.0 / size))
        out.append(value - rest * size)
        value = rest
    return out[::-1]


def lagrange(at, source):
    product = choose(source, SCALES)
    for number, point in enumerate(POINTS):
        product = product * jnp.where(source == number, 1.0, at - point)
    return product


def mixing_tables(mix_ref, raw_ref):
    shape = (HALF, DEPTH)
    column = lax.broadcasted_iota(jnp.int32, shape, 1).astype(jnp.float32)
    copy, inside = digits(column, 4, PAD)
    row = lax.broadcasted_iota(jnp.int32, shape, 0).astype(jnp.float32)
    t1, t2 = digits(row, CHEB, CHEB)
    second = inside >= 40
    place = inside - jnp.where(second, 40.0, 0.0)
    used = jnp.logical_and(place < HALF, copy < 3)
    s1, s2 = digits(jnp.minimum(place, HALF - 1.0), CHEB, CHEB)
    at1, at2 = choose(t1, POINTS) * 0.5, choose(t2, POINTS) * 0.5
    weights1 = [jnp.where(used, lagrange(q - 0.5 + at1, s1), 0.0) for q in range(2)]
    weights2 = [lagrange(q - 0.5 + at2, s2) for q in range(2)]
    for q1 in range(2):
        for q2 in range(2):
            weights = weights1[q1] * weights2[q2]
            turns1, turns2 = 0.5 * (q1 + 0.5 + at1), 0.5 * (q2 + 0.5 + at2)
            plus, minus = unit(turns1 + turns2), unit(turns1 - turns2)
            for c1 in range(2):
                for c2 in range(2):
                    co, si = plus if c1 == c2 else minus
                    si = si if c1 else -si
                    real, imag = co * weights, si * weights
                    for part, values in enumerate((jnp.where(second, -imag, real), jnp.where(second, real, imag))):
                        high = values.astype(jnp.bfloat16).astype(jnp.float32)
                        values = jnp.where(copy < 2, high, values - high)
                        base = part * TERMS + q1 * ROWS + q2 * HALF
                        raw_ref[2 * c1 + c2, base : base + HALF, :] = values

    shape = (48, DEPTH)
    copy, inside = digits(lax.broadcasted_iota(jnp.int32, shape, 1).astype(jnp.float32), 4, PAD)

    def variants(i, carry):
        table, rows = lax.div(i, 6), pl.ds(pl.multiple_of(48 * lax.rem(i, 6), 16), 48)
        values = raw_ref[table, rows, :]
        dense = jnp.where(inside < HALF, values, pltpu.roll(values, DEPTH - 4, 1))
        dense = jnp.where(inside < ROWS, dense, 0.0)
        for variant, block in enumerate((dense, values, pltpu.roll(values, 4, 1))):
            mix_ref[4 * variant + table, rows, :] = block.astype(jnp.bfloat16)
        return carry

    lax.fori_loop(0, 24, variants, 0)


def reverse6(value):
    total = 0
    for bit in range(6):
        total = total + lax.rem(lax.div(value, 1 << bit), 2) * (1 << (5 - bit))
    return total


def kernel(
    coef_hbm, slow_hbm, out_ref,
    coef_ref, slow_ref, mix_ref, raw_ref,
    sbuf, xin, s0, z1, zr, s2, obuf, orecv, vtab, e_tab, y_a, y_b, acc_a, acc_b,
    load, in_send, in_recv, sib_send, sib_recv, out_send, out_recv,
):
    bx, by = lax.axis_index("bx"), lax.axis_index("by")
    my_z, my_x = lax.div(bx, 4), lax.rem(bx, 4)
    my_y, core = lax.div(by, 2), lax.rem(by, 2)
    my_x0 = lax.rem(my_x, 2)
    chip = bx * 4 + my_y
    low1 = reverse6(chip) * 16

    chunks = [coef_ref.at[pl.ds(1536 * i, 1536)] for i in range(3)]
    loads = [pltpu.make_async_copy(coef_hbm.at[pl.ds(1536 * i, 1536)], chunks[i], load.at[i]) for i in range(3)]
    loads.append(pltpu.make_async_copy(slow_hbm, slow_ref, load.at[3]))
    for copy in loads:
        copy.start()

    barrier = pltpu.get_barrier_semaphore()
    me = bx * 8 + by

    def greet(i, carry):
        there = lax.rem(me + i, 128)
        pl.semaphore_signal(barrier, inc=1, device_id=(lax.div(there, 8), lax.rem(there, 8)), device_id_type=MESH)
        return carry

    lax.fori_loop(1, 121, greet, 0, unroll=8)
    lax.fori_loop(121, 128, greet, 0, unroll=7)
    def target_in(step):
        half, part, inner = lax.div(step, 32), lax.div(step, 16), lax.rem(step, 16)
        even, far_z = lax.rem(inner + core, 2), lax.rem(lax.div(inner, 2), 2)
        dx = (1 - even) * (2 * half + 1) + even * 2 * lax.rem(half + my_x0, 2)
        dy = lax.rem(lax.div(inner, 4) + lax.rem(inner, 2) + 2 * far_z + 2 * core, 4)
        dz = lax.rem(lax.rem(part, 2) + 2 * far_z + 2 * core, 4)
        return lax.rem(my_z + dz, 4), lax.rem(my_x + dx, 4), lax.rem(my_y + dy, 4)

    def gather_rows(step, carry):
        z, x, y = target_in(step)
        ell = z * 16 + x * 4 + y
        for tile in range(9):
            sbuf[ell, 8 * tile : 8 * tile + 8, :] = coef_ref[pl.ds(tile * 512 + ell, 8, stride=64), :]
        return carry

    def send_in(step, carry):
        half, part = lax.div(step, 32), lax.div(step, 16)
        to_z, to_x, to_y = target_in(step)
        to_bx, to_by = to_z * 4 + to_x, to_y * 2 + my_x0
        src, dst = sbuf.at[to_z * 16 + to_x * 4 + to_y], xin.at[half, core, my_z, my_y]
        here = jnp.logical_and(to_bx == bx, to_by == by)

        @pl.when(here)
        def _():
            pltpu.make_async_copy(src, dst, in_recv.at[part]).start()

        @pl.when(jnp.logical_not(here))
        def _():
            pltpu.make_async_remote_copy(
                src_ref=src, dst_ref=dst, send_sem=in_send, recv_sem=in_recv.at[part],
                device_id=(to_bx, to_by), device_id_type=MESH,
            ).start()

        return carry

    def send_and_gather(step, carry):
        send_in(step, carry)
        return gather_rows(step + 16, carry)

    for copy in loads[:3]:
        copy.wait()
    lax.fori_loop(0, 16, gather_rows, 0, unroll=4)
    pl.semaphore_wait(barrier, 127)
    lax.fori_loop(0, 48, send_and_gather, 0)
    lax.fori_loop(48, 64, send_in, 0)

    loads[3].wait()
    lane = lax.broadcasted_iota(jnp.int32, (TERMS, 96), 1).astype(jnp.float32)
    row = lax.broadcasted_iota(jnp.int32, (TERMS, 96), 0).astype(jnp.float32)
    q1, q2, t1, t2 = digits(row, 2, 2, CHEB, CHEB)
    row_i, row_j = CHEB * q1 + t1, CHEB * q2 + t2

    def spread(level, a1):
        pick = jnp.where(row_i + (12 * a1).astype(jnp.float32) == lane, 1.0, 0.0)
        return jnp.dot(pick, slow_ref[level], precision=lax.Precision.HIGHEST, preferred_element_type=jnp.float32)

    def column(table, a2):
        picked = jnp.where(row_j + (12 * a2).astype(jnp.float32) == lane, table, 0.0)
        return jnp.broadcast_to(jnp.sum(picked, axis=1, keepdims=True), (TERMS, LANES))

    zero, one = jnp.int32(0), jnp.int32(1)
    vtab[0] = column(spread(0, zero), zero)

    def fill1(a1, carry):
        table = spread(1, a1)
        for a2 in range(2):
            vtab[1 + 2 * a1 + a2] = column(table, a2 * one)
        return carry

    lax.fori_loop(0, 2, fill1, 0)

    def fill2(z, carry):
        table = spread(2, z)
        for a2 in range(2):
            vtab[5 + 2 * z + a2] = column(table, 2 * a2 + core)
        return carry

    lax.fori_loop(0, 4, fill2, 0)
    left_rows = lax.broadcasted_iota(jnp.int32, (TERMS, LANES), 1) < 64

    def fill3(a1, carry):
        table = spread(3, a1)
        for a2 in range(2):
            box = 2 * (2 * a2 + core)
            vtab[13 + 2 * a1 + a2] = jnp.where(left_rows, column(table, box), column(table, box + 1))
        return carry

    lax.fori_loop(0, 8, fill3, 0)

    lanes = lax.broadcasted_iota(jnp.int32, (8, LANES), 1)
    low2 = reverse6(lax.rem(lanes, 64)) * 16
    lane2 = lax.div(lanes, 64) * 8 + low2
    back = 127 - lanes
    back_half = lax.div(lanes, 64) * 64 + 63 - lax.rem(lanes, 64)

    def permute(block, index):
        rows = [
            jnp.take_along_axis(block[8 * i : 8 * i + 8], index, axis=1, mode="promise_in_bounds")
            for i in range(block.shape[0] // 8)
        ]
        return jnp.concatenate(rows, axis=0)

    def magnitude(level, r1, c1, r2, c2):
        width = 2.0 ** (level + 1)
        k = (lax.div(r1, 1 << level).astype(jnp.float32) + 0.5) * width - N / 2
        step = (c1 - 0.5) * width
        k0 = k - step
        k2 = (lax.div(r2, jnp.full(r2.shape, 1 << level, jnp.int32)).astype(jnp.float32) + 0.5) * width - N / 2
        step2 = (c2 - 0.5) * width
        k20 = k2 - step2
        above = step * (k + k0) + step2 * (k2 + k20)
        return above / (jnp.sqrt(k * k + k2 * k2) + jnp.sqrt(k0 * k0 + k20 * k20))

    def interpolate(y_ref, child, table, blocks):
        y_ref[child] = jnp.dot(
            mix_ref[table], operand(jnp.concatenate(blocks, axis=1)), preferred_element_type=jnp.float32
        )

    def tiles(body):
        def tile(i, carry):
            body(i, pl.ds(pl.multiple_of(8 * i, 8), 8), pl.ds(pl.multiple_of(8 * i + TERMS, 8), 8))
            return carry

        lax.fori_loop(0, TERMS // 8, tile, 0, unroll=True)

    def added(total, co, si, y_ref, child, at, at_im, side):
        cols = pl.ds(side * LANES, LANES)
        y_re, y_im = y_ref[child, at, cols], y_ref[child, at_im, cols]
        re, im = co * y_re - si * y_im, co * y_im + si * y_re
        return (re, im) if total is None else (total[0] + re, total[1] + im)

    def exponentials(entry, slots, sizes):
        def tile(i, carry):
            at = pl.ds(pl.multiple_of(8 * i, 8), 8)
            for j in range(4):
                co, si = unit(vtab[slots[j], at, :] * sizes[j])
                e_tab[entry, j, 0, at, :] = co
                e_tab[entry, j, 1, at, :] = si
            return carry

        lax.fori_loop(0, TERMS // 8, tile, 0, unroll=3)

    def combine_cores(y_ref, dst, entry):
        def body(i, at, at_im):
            totals = [None, None]
            for c1 in range(2):
                for c2 in range(2):
                    co, si = e_tab[entry, 2 * c1 + c2, 0, at, :], e_tab[entry, 2 * c1 + c2, 1, at, :]
                    totals[0] = added(totals[0], co, si, y_ref, 2 * c1 + c2, at, at_im, 0)
                    totals[1] = added(totals[1], co, si, y_ref, 2 * c1 + 1 - c2, at, at_im, 1)
            for side in range(2):
                put(dst[side], i, totals[side])

        tiles(body)

    def combine_mirrored(y_ref, dst, entry, index):
        def body(i, at, at_im):
            for side in range(2):
                totals = [None, None]
                for c1 in range(2):
                    co, si = e_tab[entry, 2 * c1 + side, 0, at, :], e_tab[entry, 2 * c1 + side, 1, at, :]
                    for c2 in range(2):
                        totals[c2] = added(totals[c2], co, si, y_ref, 2 * c1 + c2, at, at_im, side)
                put(dst[side], i, [totals[0][part] + permute(totals[1][part], index) for part in range(2)])

        tiles(body)

    def put(dst, i, total):
        rows = pl.ds(pl.multiple_of(8 * lax.rem(i, 9), 8), 8)
        for part in range(2):
            dst[2 * part + lax.div(i, 9), rows, :] = total[part]

    def window(src, q1, q2):
        rows = pl.ds(pl.multiple_of(32 * q2, 8), 40)
        return jnp.concatenate([src[q1, rows, :], src[2 + q1, rows, :]], axis=0)

    pairs = ((0, y_a, acc_a), (1, y_b, acc_b))

    def x_of(slot):
        odd = lax.rem(my_x + core, 2)
        dx = odd * (2 * slot + 1) + (1 - odd) * 2 * lax.rem(slot + core, 2)
        x = lax.rem(my_x - dx + 4, 4)
        return lax.div(x, 2), low1 + 4 * lax.div(x, 2) + 8 * core

    def box_of(box):
        other1 = 1 - lax.rem(box, 2)
        other2 = 1 - lax.rem(lax.rem(box, 2) + lax.div(box, 2), 2)
        return lax.rem(lax.div(my_z, 2) + other1, 2), lax.rem(lax.div(my_y, 2) + other2, 2)

    children = [(c1, c2) for c1 in range(2) for c2 in range(2)]

    def phases0(part, carry):
        z0 = lax.rem(my_z + part, 2)
        r1 = x_of(lax.div(part, 2))[1] + 2 * z0
        for y0 in range(2):
            sizes = [magnitude(0, r1 + c1, c1, lane2 + (c2 + 2 * y0), c2) for c1, c2 in children]
            exponentials(2 * part + y0, (0,) * 4, sizes)
        return carry

    def phases1(step, carry):
        a1, a2 = box_of(step)
        for slot in range(2):
            r1 = x_of(slot)[1]
            sizes = [magnitude(1, r1 + 2 * c1, c1, lane2 + 2 * c2, c2) for c1, c2 in children]
            exponentials(8 + 2 * step + slot, (1 + 2 * a1 + a2,) * 4, sizes)
        return carry

    def phases2(step, carry):
        a1, a2 = box_of(step)
        sizes = [
            magnitude(2, low1 + 4 * c1 + 8 * x0, c1, lane2, 0) for c1 in range(2) for x0 in (core, 1 - core)
        ]
        for z0 in range(2):
            exponentials(16 + 2 * step + z0, (5 + 2 * (2 * a1 + z0) + a2,) * 4, sizes)
        return carry

    def phases3(step, carry):
        a1, a2 = box_of(step)
        sizes = [magnitude(3, low1 + 8 * c1, c1, low2, 0) for c1 in range(2) for side in range(2)]
        for z0 in range(2):
            slot = 13 + 4 * (2 * a1 + z0) + a2
            exponentials(24 + 2 * step + z0, (slot, slot + 2, slot, slot + 2), sizes)
        return carry

    def level0(part, carry):
        pltpu.make_async_copy(xin.at[0, 0], xin.at[0, 0], in_recv.at[part]).wait()
        slot, z0 = lax.div(part, 2), lax.rem(my_z + part, 2)
        for y0, y_ref, _ in pairs:
            for c1, c2 in children:
                z = 2 * c1 + z0
                first = xin[slot, 0, z, 2 * c2 + y0]
                second = permute(xin[slot, 1, z, 2 * c2 + 1 - y0], back)
                interpolate(y_ref, 2 * c1 + c2, 2 * c1 + c2, [first, second])
        for y0, y_ref, _ in pairs:
            combine_cores(y_ref, (s0.at[slot, z0, y0, 0], s0.at[slot, z0, 1 - y0, 1]), 2 * part + y0)
        return carry

    def level1(half, slot):
        x1 = x_of(slot)[0]
        for i, y_ref, _ in pairs:
            a1, a2 = box_of(2 * half + i)
            for c1, c2 in children:
                blocks = [window(s0.at[slot, c1, c2, side], a1, a2) for side in range(2)]
                interpolate(y_ref, 2 * c1 + c2, 4 + 4 * a2 + 2 * c1 + c2, blocks)
        for i, y_ref, _ in pairs:
            box = 2 * half + i
            combine_cores(y_ref, (z1.at[box, x1, 0], z1.at[box, x1, 1]), 8 + 2 * box + slot)
            pltpu.make_async_remote_copy(
                src_ref=z1.at[box, x1, :, :, pl.ds(pl.multiple_of(32 * (1 - core), 8), 40), :],
                dst_ref=zr.at[box, x1],
                send_sem=sib_send.at[box],
                recv_sem=sib_recv.at[box],
                device_id=(bx, my_y * 2 + 1 - core),
                device_id_type=MESH,
            ).start()

    mixing_tables(mix_ref, raw_ref)
    for phases, boxes in ((phases0, 4), (phases1, 4), (phases2, 2), (phases3, 2)):
        lax.fori_loop(0, boxes, phases, 0)

    def first_slot(half, carry):
        level1(half, 0)
        return carry

    lax.fori_loop(0, 2, level0, 0)
    lax.fori_loop(0, 2, first_slot, 0)
    lax.fori_loop(2, 4, level0, 0)

    left = lax.broadcasted_iota(jnp.int32, (PAD, LANES), 1) < 64
    left_half = lax.broadcasted_iota(jnp.int32, (HALF, LANES), 1) < 64

    def level23(half, i):
        z0 = lax.rem(my_z + i, 2)
        jobs = [(2 * half + j, j, y_ref, acc_ref) for j, y_ref, acc_ref in pairs]
        for box, j, y_ref, _ in jobs:
            for c1, c2 in children:
                other = zr.at[box, c1, c2]
                blocks = [
                    window(z1.at[box, c1, c2], z0, core),
                    jnp.concatenate([other[z0], other[2 + z0]], axis=0),
                ]
                interpolate(y_ref, 2 * c1 + c2, 4 + 4 * core + 2 * c1 + c2, blocks)
        for box, j, y_ref, _ in jobs:
            combine_mirrored(y_ref, (s2.at[j, 0], s2.at[j, 1]), 16 + 2 * box + z0, back)
        for box, j, y_ref, _ in jobs:
            for c1 in range(2):
                src = s2.at[j, lax.rem(c1 + core, 2)]
                near, far = [], []
                for x1 in range(2):
                    first = window(src, x1, 0)
                    second = window(src, x1, 1)
                    second = jnp.concatenate([second[4:40], second[36:40], second[44:80], second[76:80]], axis=0)
                    near.append(jnp.where(left, first, pltpu.roll(second, 64, 1)))
                    far.append(jnp.where(left, permute(first, back), permute(second, back_half)))
                interpolate(y_ref, 2 * c1, 4 + 2 * c1, near)
                interpolate(y_ref, 2 * c1 + 1, 4 + 2 * c1 + 1, far)
        for box, j, y_ref, acc_ref in jobs:
            combine_mirrored(y_ref, (acc_ref.at[0], acc_ref.at[1]), 24 + 2 * box + z0, back_half)
            for x1 in range(2):
                for q1 in range(2):
                    for part in range(2):
                        upper = acc_ref[x1, 2 * part + q1, 0:HALF, :]
                        lower = acc_ref[x1, 2 * part + q1, HALF:ROWS, :]
                        rows = pl.ds(HALF * part, HALF)
                        obuf[box, i, x1, q1, 0, rows, :] = jnp.where(left_half, upper, pltpu.roll(lower, 64, 1))
                        obuf[box, i, x1, q1, 1, rows, :] = jnp.where(left_half, pltpu.roll(upper, 64, 1), lower)

    def send_out(half, i, number):
        turn, round_ = lax.rem(number, 2), lax.div(number, 2)
        box = 2 * half + lax.rem(turn + core, 2)
        a1, a2 = box_of(box)
        x = lax.rem(my_x + 1 + 2 * core + round_ + 2 * turn, 4)
        c = lax.rem(round_ + lax.div(round_, 4) + turn, 2)
        to_bx, to_by = (2 * a1 + lax.rem(my_z + i, 2)) * 4 + x, 2 * (2 * a2 + core) + c
        src, dst = obuf.at[box, i, lax.div(x, 2), lax.rem(x, 2), c], orecv.at[chip]
        here = jnp.logical_and(to_bx == bx, to_by == by)

        @pl.when(here)
        def _():
            pltpu.make_async_copy(src, dst, out_recv.at[2 * half + i]).start()

        @pl.when(jnp.logical_not(here))
        def _():
            pltpu.make_async_remote_copy(
                src_ref=src, dst_ref=dst, send_sem=out_send, recv_sem=out_recv.at[2 * half + i],
                device_id=(to_bx, to_by), device_id_type=MESH,
            ).start()

    def two_boxes(half, carry):
        level1(half, 1)
        for box in range(2):
            pltpu.make_async_copy(zr.at[0], zr.at[0], sib_recv.at[2 * half + box]).wait()

        def both_z(i, carry):
            level23(half, i)

            def send_some(number, carry):
                send_out(half, i, number)
                return carry

            lax.fori_loop(0, 16, send_some, 0)
            return carry

        lax.fori_loop(0, 2, both_z, 0)

        @pl.when(half == 0)
        def _():
            for phases in (phases2, phases3):
                lax.fori_loop(2, 4, phases, 0)

        return carry

    lax.fori_loop(0, 2, two_boxes, 0)

    def settle(step, carry):
        pltpu.make_async_copy(zr.at[0], zr.at[0], sib_send.at[step]).wait()
        return carry

    lax.fori_loop(0, 4, settle, 0)
    for keeps, sem in ((my_x0 == core, in_send), (lax.rem(my_y, 2) == core, out_send)):

        @pl.when(keeps)
        def _(sem=sem):
            pltpu.make_async_copy(sbuf.at[pl.ds(0, 63)], sbuf.at[pl.ds(0, 63)], sem).wait()

        @pl.when(jnp.logical_not(keeps))
        def _(sem=sem):
            pltpu.make_async_copy(sbuf, sbuf, sem).wait()

    def arrive(step, carry):
        pltpu.make_async_copy(orecv.at[pl.ds(0, 16)], orecv.at[pl.ds(0, 16)], out_recv.at[step]).wait()

        def scatter_rows(i, carry):
            upper = lax.div(i, 8)
            z = 2 * upper + lax.rem(my_z + step, 2)
            other = lax.rem(lax.div(my_z, 2) + upper + lax.div(step, 2), 2)
            y = 2 * lax.rem(lax.div(my_y, 2) + other, 2) + lax.rem(i, 2)
            x = lax.rem(lax.div(i, 2), 4)
            ell = z * 16 + x * 4 + y
            for tile in range(9):
                out_ref[pl.ds(tile * 512 + ell, 8, stride=64), :] = orecv[ell, 8 * tile : 8 * tile + 8, :]
            return carry

        lax.fori_loop(0, 16, scatter_rows, 0, unroll=4)
        return carry

    lax.fori_loop(0, 4, arrive, 0)


def shards(coefficients, slowness):
    rows = jnp.transpose(coefficients, (0, 1, 3, 2, 4)).reshape(ROWS * 64, LANES)
    operands = (rows, pltpu.with_memory_space_constraint(slowness, pltpu.HBM))
    dense = (ROWS, LANES)
    scratch = [pltpu.VMEM(operands[i].shape, jnp.float32) for i in range(2)]
    scratch += [pltpu.VMEM((12, 2 * TERMS, DEPTH), jnp.bfloat16), pltpu.VMEM((4, 2 * TERMS, DEPTH), jnp.float32)]
    scratch += [
        pltpu.VMEM(shape, jnp.float32)
        for shape in (
            (64,) + dense,
            (2, 2, 4, 4) + dense,
            (2, 2, 2, 2, 4) + dense,
            (4, 2, 2, 4) + dense,
            (4, 2, 2, 4, 40, LANES),
            (2, 2, 4) + dense,
            (4, 2, 2, 2, 2) + dense,
            (64,) + dense,
            (29, TERMS, LANES),
            (32, 4, 2, TERMS, LANES),
            (4, 2 * TERMS, 2 * LANES),
            (4, 2 * TERMS, 2 * LANES),
            (2, 4) + dense,
            (2, 4) + dense,
        )
    ]
    scratch += [
        pltpu.SemaphoreType.DMA((4,)),
        pltpu.SemaphoreType.DMA,
        pltpu.SemaphoreType.DMA((4,)),
        pltpu.SemaphoreType.DMA((4,)),
        pltpu.SemaphoreType.DMA((4,)),
        pltpu.SemaphoreType.DMA,
        pltpu.SemaphoreType.DMA((4,)),
    ]
    out = pl.pallas_call(
        kernel,
        out_shape=jax.ShapeDtypeStruct((ROWS * 64, LANES), jnp.float32),
        in_specs=[pl.BlockSpec(memory_space=pl.ANY), pl.BlockSpec(memory_space=pltpu.HBM)],
        out_specs=pl.BlockSpec(memory_space=pltpu.VMEM),
        scratch_shapes=scratch,
        compiler_params=pltpu.CompilerParams(collective_id=0, has_side_effects=True, vmem_limit_bytes=50 << 20),
    )(*operands)
    return jnp.transpose(out.reshape(2, CHEB, CHEB, 64, LANES), (0, 1, 3, 2, 4))


def solution(mesh):
    placed = (P(None, None, "bx", None, "by"), P())
    return jax.shard_map(
        shards,
        mesh=mesh,
        in_specs=placed,
        out_specs=P(None, None, "bx", None, "by"),
        check_vma=False,
    )
```

```python
import math

import jax
import jax.numpy as jnp
import numpy as np
from jax import lax
from jax.experimental import pallas as pl
from jax.experimental.pallas import tpu as pltpu
from jax.sharding import PartitionSpec as P

N = 2048
CHEB = 6
HALF = CHEB * CHEB
ROWS = 2 * HALF
TERMS = 4 * HALF
PAD = 80
DEPTH = 256
LANES = 128
MESH = pl.DeviceIdType.MESH


def cheb_points():
    return np.cos(np.pi * (2 * np.arange(CHEB) + 1) / (2 * CHEB))


def fit(function, degree):
    count = 200
    s = 0.125 * (1 + np.cos(np.pi * (2 * np.arange(count) + 1) / (2 * count)))
    series = np.polynomial.chebyshev.Chebyshev.fit(s, function(np.sqrt(s)), degree, domain=[0, 0.25])
    return [float(c) for c in series.convert(kind=np.polynomial.Polynomial).coef]


SIN = fit(lambda r: math.sqrt(2) * np.sin(np.pi * r) / r, 3)
COS = fit(lambda r: math.sqrt(2) * np.cos(np.pi * r), 4)
WHOLE = 1.5 * 2.0**23


POINTS = [float(point) for point in cheb_points()]
SCALES = [
    float(1 / np.prod([cheb_points()[s] - cheb_points()[j] for j in range(CHEB) if j != s])) for s in range(CHEB)
]


def horner(coefficients, s):
    value = s * coefficients[-1] + coefficients[-2]
    for coefficient in coefficients[-3::-1]:
        value = value * s + coefficient
    return value


def unit(turns):
    r = turns - ((turns + WHOLE) - WHOLE)
    s = r * r
    half = horner(SIN, s) * r
    return 1.0 - half * half, half * horner(COS, s)


def operand(block):
    if block.shape[0] < PAD:
        block = jnp.concatenate([block, jnp.zeros((PAD - block.shape[0], block.shape[1]), jnp.float32)], axis=0)
    high = block.astype(jnp.bfloat16)
    low = (block - high.astype(jnp.float32)).astype(jnp.bfloat16)
    return jnp.concatenate([high, low, high, jnp.zeros((DEPTH - 3 * PAD, block.shape[1]), jnp.bfloat16)], axis=0)


def choose(index, values):
    result = jnp.full(index.shape, values[0], jnp.float32)
    for number, value in enumerate(values[1:], 1):
        result = jnp.where(index == number, value, result)
    return result


def digits(value, *sizes):
    out = []
    for size in sizes[::-1]:
        rest = jnp.floor((value + 0.5) * (1.0 / size))
        out.append(value - rest * size)
        value = rest
    return out[::-1]


def lagrange(at, source):
    product = choose(source, SCALES)
    for number, point in enumerate(POINTS):
        product = product * jnp.where(source == number, 1.0, at - point)
    return product


def mixing_tables(mix_ref, raw_ref):
    shape = (HALF, DEPTH)
    column = lax.broadcasted_iota(jnp.int32, shape, 1).astype(jnp.float32)
    copy, inside = digits(column, 4, PAD)
    row = lax.broadcasted_iota(jnp.int32, shape, 0).astype(jnp.float32)
    t1, t2 = digits(row, CHEB, CHEB)
    second = inside >= 40
    place = inside - jnp.where(second, 40.0, 0.0)
    used = jnp.logical_and(place < HALF, copy < 3)
    s1, s2 = digits(jnp.minimum(place, HALF - 1.0), CHEB, CHEB)
    at1, at2 = choose(t1, POINTS) * 0.5, choose(t2, POINTS) * 0.5
    weights1 = [jnp.where(used, lagrange(q - 0.5 + at1, s1), 0.0) for q in range(2)]
    weights2 = [lagrange(q - 0.5 + at2, s2) for q in range(2)]
    for q1 in range(2):
        for q2 in range(2):
            weights = weights1[q1] * weights2[q2]
            turns1, turns2 = 0.5 * (q1 + 0.5 + at1), 0.5 * (q2 + 0.5 + at2)
            plus, minus = unit(turns1 + turns2), unit(turns1 - turns2)
            for c1 in range(2):
                for c2 in range(2):
                    co, si = plus if c1 == c2 else minus
                    si = si if c1 else -si
                    real, imag = co * weights, si * weights
                    for part, values in enumerate((jnp.where(second, -imag, real), jnp.where(second, real, imag))):
                        high = values.astype(jnp.bfloat16).astype(jnp.float32)
                        values = jnp.where(copy < 2, high, values - high)
                        base = part * TERMS + q1 * ROWS + q2 * HALF
                        raw_ref[2 * c1 + c2, base : base + HALF, :] = values

    shape = (48, DEPTH)
    copy, inside = digits(lax.broadcasted_iota(jnp.int32, shape, 1).astype(jnp.float32), 4, PAD)

    def variants(i, carry):
        table, rows = lax.div(i, 6), pl.ds(pl.multiple_of(48 * lax.rem(i, 6), 16), 48)
        values = raw_ref[table, rows, :]
        dense = jnp.where(inside < HALF, values, pltpu.roll(values, DEPTH - 4, 1))
        dense = jnp.where(inside < ROWS, dense, 0.0)
        for variant, block in enumerate((dense, values, pltpu.roll(values, 4, 1))):
            mix_ref[4 * variant + table, rows, :] = block.astype(jnp.bfloat16)
        return carry

    lax.fori_loop(0, 24, variants, 0)


def reverse6(value):
    total = 0
    for bit in range(6):
        total = total + lax.rem(lax.div(value, 1 << bit), 2) * (1 << (5 - bit))
    return total


def kernel(
    coef_hbm, slow_hbm, out_ref,
    coef_ref, slow_ref, mix_ref, raw_ref, pieces_ref,
    sbuf, xin, s0, z1, zr, s2, obuf, orecv, vtab, e_tab, y_a, y_b, acc_a, acc_b,
    load, in_send, in_recv, sib_send, sib_recv, out_send, out_recv,
):
    bx, by = lax.axis_index("bx"), lax.axis_index("by")
    my_z, my_x = lax.div(bx, 4), lax.rem(bx, 4)
    my_y, core = lax.div(by, 2), lax.rem(by, 2)
    my_x0 = lax.rem(my_x, 2)
    chip = bx * 4 + my_y
    low1 = reverse6(chip) * 16

    chunks = [coef_ref.at[pl.ds(1536 * i, 1536)] for i in range(3)]
    loads = [pltpu.make_async_copy(coef_hbm.at[pl.ds(1536 * i, 1536)], chunks[i], load.at[i]) for i in range(3)]
    loads.append(pltpu.make_async_copy(slow_hbm, slow_ref, load.at[3]))
    for copy in loads:
        copy.start()

    barrier = pltpu.get_barrier_semaphore()
    across = [lax.rem(by + j, 8) for j in range(8)]

    def greet(i, carry):
        there = lax.rem(bx + i, 16)
        for j in range(8):

            @pl.when(i + j > 0)
            def _(j=j):
                pl.semaphore_signal(barrier, inc=1, device_id=(there, across[j]), device_id_type=MESH)

        return carry

    lax.fori_loop(0, 16, greet, 0)

    y_at = [lax.rem(my_y + 2 * core + v, 4) for v in range(4)]

    def targets_in(part):
        half = lax.div(part, 2)
        odd = lax.rem(my_x + 2 * half + 1, 4)
        even = lax.rem(my_x + 2 * lax.rem(half + my_x0, 2), 4)
        x_at = (odd + core * (even - odd), even + core * (odd - even))
        z_at = [lax.rem(my_z + lax.rem(part, 2) + 2 * far + 2 * core, 4) for far in range(2)]
        for inner in range(16):
            far = inner // 2 % 2
            yield z_at[far], x_at[inner % 2], y_at[(inner // 4 + inner % 2 + 2 * far) % 4]

    def gather_rows(z, x, y):
        ell = z * 16 + x * 4 + y
        for tile in range(9):
            sbuf[ell, 8 * tile : 8 * tile + 8, :] = coef_ref[pl.ds(tile * 512 + ell, 8, stride=64), :]

    def send_part(part, carry):
        half = lax.div(part, 2)
        for z, x, y in targets_in(part):
            to_bx, to_by = z * 4 + x, y * 2 + my_x0
            src, dst = sbuf.at[z * 16 + x * 4 + y], xin.at[half, core, my_z, my_y]
            here = jnp.logical_and(to_bx == bx, to_by == by)

            @pl.when(here)
            def _(src=src, dst=dst):
                pltpu.make_async_copy(src, dst, in_recv.at[part]).start()

            @pl.when(jnp.logical_not(here))
            def _(src=src, dst=dst, to_bx=to_bx, to_by=to_by):
                pltpu.make_async_remote_copy(
                    src_ref=src, dst_ref=dst, send_sem=in_send, recv_sem=in_recv.at[part],
                    device_id=(to_bx, to_by), device_id_type=MESH,
                ).start()

        @pl.when(part < 3)
        def _():
            for target in targets_in(part + 1):
                gather_rows(*target)

        return carry

    for copy in loads[:3]:
        copy.wait()
    for target in targets_in(jnp.int32(0)):
        gather_rows(*target)
    pl.semaphore_wait(barrier, 127)
    lax.fori_loop(0, 4, send_part, 0)

    loads[3].wait()
    for level in range(4):
        table = jnp.concatenate([slow_ref[level], jnp.zeros((96, LANES - 96), jnp.float32)], axis=1)
        for piece in range(3):
            rounded = table.astype(jnp.bfloat16)
            pieces_ref[level, :, piece * LANES : piece * LANES + LANES] = rounded
            table = table - rounded.astype(jnp.float32)
    lane = lax.broadcasted_iota(jnp.int32, (TERMS, LANES), 1).astype(jnp.float32)
    row = lax.broadcasted_iota(jnp.int32, (TERMS, LANES), 0).astype(jnp.float32)
    q1, q2, t1, t2 = digits(row, 2, 2, CHEB, CHEB)
    row_i, row_j = CHEB * q1 + t1, CHEB * q2 + t2
    left_rows = lane < 64

    def spread(level, a1):
        pick = jnp.where(row_i[:, 0:96] + (12 * a1).astype(jnp.float32) == lane[:, 0:96], 1.0, 0.0)
        found = jnp.dot(pick.astype(jnp.bfloat16), pieces_ref[level], preferred_element_type=jnp.float32)
        return found[:, 0:LANES] + found[:, LANES : 2 * LANES] + found[:, 2 * LANES :]

    def column(table, a2):
        picked = jnp.where(row_j + (12 * a2).astype(jnp.float32) == lane, table, 0.0)
        return jnp.broadcast_to(jnp.sum(picked, axis=1, keepdims=True), (TERMS, LANES))

    zero, one = jnp.int32(0), jnp.int32(1)
    vtab[0] = column(spread(0, zero), zero)

    def fill1(a1, carry):
        table = spread(1, a1)
        for a2 in range(2):
            vtab[1 + 2 * a1 + a2] = column(table, a2 * one)
        return carry

    lax.fori_loop(0, 2, fill1, 0)

    def fill23(half):
        def fill(z, carry):
            other = lax.rem(lax.div(z, 2) + lax.div(my_z, 2) + half, 2)
            a2 = lax.rem(lax.div(my_y, 2) + other, 2)
            box = 2 * a2 + core
            vtab[5 + 2 * z + a2] = column(spread(2, z), box)
            for x1 in range(2):
                table = spread(3, 2 * z + x1)
                vtab[13 + 4 * z + 2 * x1 + a2] = jnp.where(left_rows, column(table, 2 * box), column(table, 2 * box + 1))
            return carry

        lax.fori_loop(0, 4, fill, 0)

    fill23(0)

    lanes = lax.broadcasted_iota(jnp.int32, (8, LANES), 1)
    low2 = reverse6(lax.rem(lanes, 64)) * 16
    lane2 = lax.div(lanes, 64) * 8 + low2
    back = 127 - lanes
    back_half = lax.div(lanes, 64) * 64 + 63 - lax.rem(lanes, 64)

    def permute(block, index):
        rows = [
            jnp.take_along_axis(block[8 * i : 8 * i + 8], index, axis=1, mode="promise_in_bounds")
            for i in range(block.shape[0] // 8)
        ]
        return jnp.concatenate(rows, axis=0)

    def magnitude(level, r1, c1, r2, c2):
        width = 2.0 ** (level + 1)
        k = (lax.div(r1, 1 << level).astype(jnp.float32) + 0.5) * width - N / 2
        step = (c1 - 0.5) * width
        k0 = k - step
        k2 = (lax.div(r2, jnp.full(r2.shape, 1 << level, jnp.int32)).astype(jnp.float32) + 0.5) * width - N / 2
        step2 = (c2 - 0.5) * width
        k20 = k2 - step2
        above = step * (k + k0) + step2 * (k2 + k20)
        return above / (jnp.sqrt(k * k + k2 * k2) + jnp.sqrt(k0 * k0 + k20 * k20))

    def interpolate(y_ref, child, table, blocks):
        y_ref[child] = jnp.dot(
            mix_ref[table], operand(jnp.concatenate(blocks, axis=1)), preferred_element_type=jnp.float32
        )

    def tiles(body):
        def tile(i, carry):
            body(i, pl.ds(pl.multiple_of(8 * i, 8), 8), pl.ds(pl.multiple_of(8 * i + TERMS, 8), 8))
            return carry

        lax.fori_loop(0, TERMS // 8, tile, 0, unroll=True)

    def added(total, co, si, y_ref, child, at, at_im, side):
        cols = pl.ds(side * LANES, LANES)
        y_re, y_im = y_ref[child, at, cols], y_ref[child, at_im, cols]
        re, im = co * y_re - si * y_im, co * y_im + si * y_re
        return (re, im) if total is None else (total[0] + re, total[1] + im)

    def exponentials(entry, slots, sizes):
        def tile(i, carry):
            at = pl.ds(pl.multiple_of(8 * i, 8), 8)
            for j in range(4):
                co, si = unit(vtab[slots[j], at, :] * sizes[j])
                e_tab[entry, j, 0, at, :] = co
                e_tab[entry, j, 1, at, :] = si
            return carry

        lax.fori_loop(0, TERMS // 8, tile, 0, unroll=3)

    def combine_cores(y_ref, dst, entry):
        def body(i, at, at_im):
            totals = [None, None]
            for c1 in range(2):
                for c2 in range(2):
                    co, si = e_tab[entry, 2 * c1 + c2, 0, at, :], e_tab[entry, 2 * c1 + c2, 1, at, :]
                    totals[0] = added(totals[0], co, si, y_ref, 2 * c1 + c2, at, at_im, 0)
                    totals[1] = added(totals[1], co, si, y_ref, 2 * c1 + 1 - c2, at, at_im, 1)
            for side in range(2):
                put(dst[side], i, totals[side])

        tiles(body)

    def combine_mirrored(y_ref, dst, entry, index):
        def body(i, at, at_im):
            for side in range(2):
                totals = [None, None]
                for c1 in range(2):
                    co, si = e_tab[entry, 2 * c1 + side, 0, at, :], e_tab[entry, 2 * c1 + side, 1, at, :]
                    for c2 in range(2):
                        totals[c2] = added(totals[c2], co, si, y_ref, 2 * c1 + c2, at, at_im, side)
                put(dst[side], i, [totals[0][part] + permute(totals[1][part], index) for part in range(2)])

        tiles(body)

    def put(dst, i, total):
        rows = pl.ds(pl.multiple_of(8 * lax.rem(i, 9), 8), 8)
        for part in range(2):
            dst[2 * part + lax.div(i, 9), rows, :] = total[part]

    def window(src, q1, q2):
        rows = pl.ds(pl.multiple_of(32 * q2, 8), 40)
        return jnp.concatenate([src[q1, rows, :], src[2 + q1, rows, :]], axis=0)

    pairs = ((0, y_a, acc_a), (1, y_b, acc_b))

    def x_of(slot):
        odd = lax.rem(my_x + core, 2)
        dx = odd * (2 * slot + 1) + (1 - odd) * 2 * lax.rem(slot + core, 2)
        x = lax.rem(my_x - dx + 4, 4)
        return lax.div(x, 2), low1 + 4 * lax.div(x, 2) + 8 * core

    def box_of(box):
        other1 = 1 - lax.rem(box, 2)
        other2 = 1 - lax.rem(lax.rem(box, 2) + lax.div(box, 2), 2)
        return lax.rem(lax.div(my_z, 2) + other1, 2), lax.rem(lax.div(my_y, 2) + other2, 2)

    children = [(c1, c2) for c1 in range(2) for c2 in range(2)]

    def phases0(part, carry):
        z0 = lax.rem(my_z + part, 2)
        r1 = x_of(lax.div(part, 2))[1] + 2 * z0
        for y0 in range(2):
            sizes = [magnitude(0, r1 + c1, c1, lane2 + (c2 + 2 * y0), c2) for c1, c2 in children]
            exponentials(2 * part + y0, (0,) * 4, sizes)
        return carry

    def phases1(step, carry):
        a1, a2 = box_of(step)
        for slot in range(2):
            r1 = x_of(slot)[1]
            sizes = [magnitude(1, r1 + 2 * c1, c1, lane2 + 2 * c2, c2) for c1, c2 in children]
            exponentials(8 + 2 * step + slot, (1 + 2 * a1 + a2,) * 4, sizes)
        return carry

    def phases2(step, carry):
        a1, a2 = box_of(step)
        sizes = [
            magnitude(2, low1 + 4 * c1 + 8 * x0, c1, lane2, 0) for c1 in range(2) for x0 in (core, 1 - core)
        ]
        for z0 in range(2):
            exponentials(16 + 2 * step + z0, (5 + 2 * (2 * a1 + z0) + a2,) * 4, sizes)
        return carry

    def phases3(step, carry):
        a1, a2 = box_of(step)
        sizes = [magnitude(3, low1 + 8 * c1, c1, low2, 0) for c1 in range(2) for side in range(2)]
        for z0 in range(2):
            slot = 13 + 4 * (2 * a1 + z0) + a2
            exponentials(24 + 2 * step + z0, (slot, slot + 2, slot, slot + 2), sizes)
        return carry

    def level0(part, carry):
        pltpu.make_async_copy(xin.at[0, 0], xin.at[0, 0], in_recv.at[part]).wait()
        slot, z0 = lax.div(part, 2), lax.rem(my_z + part, 2)
        for y0, y_ref, _ in pairs:
            for c1, c2 in children:
                z = 2 * c1 + z0
                first = xin[slot, 0, z, 2 * c2 + y0]
                second = permute(xin[slot, 1, z, 2 * c2 + 1 - y0], back)
                interpolate(y_ref, 2 * c1 + c2, 2 * c1 + c2, [first, second])
        for y0, y_ref, _ in pairs:
            combine_cores(y_ref, (s0.at[slot, z0, y0, 0], s0.at[slot, z0, 1 - y0, 1]), 2 * part + y0)
        return carry

    def level1(half, slot):
        x1 = x_of(slot)[0]
        for i, y_ref, _ in pairs:
            a1, a2 = box_of(2 * half + i)
            for c1, c2 in children:
                blocks = [window(s0.at[slot, c1, c2, side], a1, a2) for side in range(2)]
                interpolate(y_ref, 2 * c1 + c2, 4 + 4 * a2 + 2 * c1 + c2, blocks)
        for i, y_ref, _ in pairs:
            box = 2 * half + i
            combine_cores(y_ref, (z1.at[box, x1, 0], z1.at[box, x1, 1]), 8 + 2 * box + slot)
            pltpu.make_async_remote_copy(
                src_ref=z1.at[box, x1, :, :, pl.ds(pl.multiple_of(32 * (1 - core), 8), 40), :],
                dst_ref=zr.at[box, x1],
                send_sem=sib_send.at[box],
                recv_sem=sib_recv.at[box],
                device_id=(bx, my_y * 2 + 1 - core),
                device_id_type=MESH,
            ).start()

    mixing_tables(mix_ref, raw_ref)
    for phases, boxes in ((phases0, 4), (phases1, 4), (phases2, 2), (phases3, 2)):
        lax.fori_loop(0, boxes, phases, 0)

    def first_slot(half, carry):
        level1(half, 0)
        return carry

    lax.fori_loop(0, 2, level0, 0)
    lax.fori_loop(0, 2, first_slot, 0)
    lax.fori_loop(2, 4, level0, 0)

    left = lax.broadcasted_iota(jnp.int32, (PAD, LANES), 1) < 64
    left_half = lax.broadcasted_iota(jnp.int32, (HALF, LANES), 1) < 64

    def level23(half, i):
        z0 = lax.rem(my_z + i, 2)
        jobs = [(2 * half + j, j, y_ref, acc_ref) for j, y_ref, acc_ref in pairs]
        for box, j, y_ref, _ in jobs:
            for c1, c2 in children:
                other = zr.at[box, c1, c2]
                blocks = [
                    window(z1.at[box, c1, c2], z0, core),
                    jnp.concatenate([other[z0], other[2 + z0]], axis=0),
                ]
                interpolate(y_ref, 2 * c1 + c2, 4 + 4 * core + 2 * c1 + c2, blocks)
        for box, j, y_ref, _ in jobs:
            combine_mirrored(y_ref, (s2.at[j, 0], s2.at[j, 1]), 16 + 2 * box + z0, back)
        for box, j, y_ref, _ in jobs:
            for c1 in range(2):
                src = s2.at[j, lax.rem(c1 + core, 2)]
                near, far = [], []
                for x1 in range(2):
                    first = window(src, x1, 0)
                    second = window(src, x1, 1)
                    second = jnp.concatenate([second[4:40], second[36:40], second[44:80], second[76:80]], axis=0)
                    near.append(jnp.where(left, first, pltpu.roll(second, 64, 1)))
                    far.append(jnp.where(left, permute(first, back), permute(second, back_half)))
                interpolate(y_ref, 2 * c1, 4 + 2 * c1, near)
                interpolate(y_ref, 2 * c1 + 1, 4 + 2 * c1 + 1, far)
        for box, j, y_ref, acc_ref in jobs:
            combine_mirrored(y_ref, (acc_ref.at[0], acc_ref.at[1]), 24 + 2 * box + z0, back_half)
            for x1 in range(2):
                for q1 in range(2):
                    for part in range(2):
                        upper = acc_ref[x1, 2 * part + q1, 0:HALF, :]
                        lower = acc_ref[x1, 2 * part + q1, HALF:ROWS, :]
                        rows = pl.ds(HALF * part, HALF)
                        obuf[box, i, 2 * x1 + q1, 0, rows, :] = jnp.where(left_half, upper, pltpu.roll(lower, 64, 1))
                        obuf[box, i, 2 * x1 + q1, 1, rows, :] = jnp.where(left_half, pltpu.roll(upper, 64, 1), lower)

    x_out = [lax.rem(my_x + 1 + 2 * core + k, 4) for k in range(4)]

    def send_out(half, i):
        boxes = [2 * half + core, 2 * half + 1 - core]
        z0 = lax.rem(my_z + i, 2)
        places = [box_of(box) for box in boxes]
        places = [((2 * a1 + z0) * 4, 2 * (2 * a2 + core)) for a1, a2 in places]
        for number in range(16):
            turn, round_ = number % 2, number // 2
            x, c = x_out[(round_ + 2 * turn) % 4], (round_ + round_ // 4 + turn) % 2
            to_bx, to_by = places[turn][0] + x, places[turn][1] + c
            src, dst = obuf.at[boxes[turn], i, x, c], orecv.at[chip]
            here = jnp.logical_and(to_bx == bx, to_by == by)

            @pl.when(here)
            def _(src=src, dst=dst):
                pltpu.make_async_copy(src, dst, out_recv.at[2 * half + i]).start()

            @pl.when(jnp.logical_not(here))
            def _(src=src, dst=dst, to_bx=to_bx, to_by=to_by):
                pltpu.make_async_remote_copy(
                    src_ref=src, dst_ref=dst, send_sem=out_send, recv_sem=out_recv.at[2 * half + i],
                    device_id=(to_bx, to_by), device_id_type=MESH,
                ).start()

    def two_boxes(half, carry):
        level1(half, 1)
        for box in range(2):
            pltpu.make_async_copy(zr.at[0], zr.at[0], sib_recv.at[2 * half + box]).wait()

        def both_z(i, carry):
            level23(half, i)
            send_out(half, i)
            return carry

        lax.fori_loop(0, 2, both_z, 0)

        @pl.when(half == 0)
        def _():
            fill23(1)
            for phases in (phases2, phases3):
                lax.fori_loop(2, 4, phases, 0)

        return carry

    lax.fori_loop(0, 2, two_boxes, 0)

    def settle(step, carry):
        pltpu.make_async_copy(zr.at[0], zr.at[0], sib_send.at[step]).wait()
        return carry

    lax.fori_loop(0, 4, settle, 0)
    for keeps, sem in ((my_x0 == core, in_send), (lax.rem(my_y, 2) == core, out_send)):

        @pl.when(keeps)
        def _(sem=sem):
            pltpu.make_async_copy(sbuf.at[pl.ds(0, 63)], sbuf.at[pl.ds(0, 63)], sem).wait()

        @pl.when(jnp.logical_not(keeps))
        def _(sem=sem):
            pltpu.make_async_copy(sbuf, sbuf, sem).wait()

    def arrive(step, carry):
        pltpu.make_async_copy(orecv.at[pl.ds(0, 16)], orecv.at[pl.ds(0, 16)], out_recv.at[step]).wait()

        def scatter_rows(i, carry):
            upper = lax.div(i, 8)
            z = 2 * upper + lax.rem(my_z + step, 2)
            other = lax.rem(lax.div(my_z, 2) + upper + lax.div(step, 2), 2)
            y = 2 * lax.rem(lax.div(my_y, 2) + other, 2) + lax.rem(i, 2)
            x = lax.rem(lax.div(i, 2), 4)
            ell = z * 16 + x * 4 + y
            for tile in range(9):
                out_ref[pl.ds(tile * 512 + ell, 8, stride=64), :] = orecv[ell, 8 * tile : 8 * tile + 8, :]
            return carry

        lax.fori_loop(0, 16, scatter_rows, 0, unroll=4)
        return carry

    lax.fori_loop(0, 4, arrive, 0)


def shards(coefficients, slowness):
    rows = jnp.transpose(coefficients, (0, 1, 3, 2, 4)).reshape(ROWS * 64, LANES)
    operands = (rows, pltpu.with_memory_space_constraint(slowness, pltpu.HBM))
    dense = (ROWS, LANES)
    scratch = [pltpu.VMEM(operands[i].shape, jnp.float32) for i in range(2)]
    scratch += [pltpu.VMEM((12, 2 * TERMS, DEPTH), jnp.bfloat16), pltpu.VMEM((4, 2 * TERMS, DEPTH), jnp.float32)]
    scratch += [pltpu.VMEM((4, 96, 3 * LANES), jnp.bfloat16)]
    scratch += [
        pltpu.VMEM(shape, jnp.float32)
        for shape in (
            (64,) + dense,
            (2, 2, 4, 4) + dense,
            (2, 2, 2, 2, 4) + dense,
            (4, 2, 2, 4) + dense,
            (4, 2, 2, 4, 40, LANES),
            (2, 2, 4) + dense,
            (4, 2, 4, 2) + dense,
            (64,) + dense,
            (29, TERMS, LANES),
            (32, 4, 2, TERMS, LANES),
            (4, 2 * TERMS, 2 * LANES),
            (4, 2 * TERMS, 2 * LANES),
            (2, 4) + dense,
            (2, 4) + dense,
        )
    ]
    scratch += [
        pltpu.SemaphoreType.DMA((4,)),
        pltpu.SemaphoreType.DMA,
        pltpu.SemaphoreType.DMA((4,)),
        pltpu.SemaphoreType.DMA((4,)),
        pltpu.SemaphoreType.DMA((4,)),
        pltpu.SemaphoreType.DMA,
        pltpu.SemaphoreType.DMA((4,)),
    ]
    out = pl.pallas_call(
        kernel,
        out_shape=jax.ShapeDtypeStruct((ROWS * 64, LANES), jnp.float32),
        in_specs=[pl.BlockSpec(memory_space=pl.ANY), pl.BlockSpec(memory_space=pltpu.HBM)],
        out_specs=pl.BlockSpec(memory_space=pltpu.VMEM),
        scratch_shapes=scratch,
        compiler_params=pltpu.CompilerParams(collective_id=0, has_side_effects=True, vmem_limit_bytes=50 << 20),
    )(*operands)
    return jnp.transpose(out.reshape(2, CHEB, CHEB, 64, LANES), (0, 1, 3, 2, 4))


def solution(mesh):
    placed = (P(None, None, "bx", None, "by"), P())
    return jax.shard_map(
        shards,
        mesh=mesh,
        in_specs=placed,
        out_specs=P(None, None, "bx", None, "by"),
        check_vma=False,
    )
```

```python
import math

import jax
import jax.numpy as jnp
import numpy as np
from jax import lax
from jax.experimental import pallas as pl
from jax.experimental.pallas import tpu as pltpu
from jax.sharding import PartitionSpec as P

N = 2048
CHEB = 6
HALF = CHEB * CHEB
ROWS = 2 * HALF
TERMS = 4 * HALF
PAD = 80
DEPTH = 256
LANES = 128
MESH = pl.DeviceIdType.MESH


def cheb_points():
    return np.cos(np.pi * (2 * np.arange(CHEB) + 1) / (2 * CHEB))


def fit(function, degree):
    count = 200
    s = 0.125 * (1 + np.cos(np.pi * (2 * np.arange(count) + 1) / (2 * count)))
    series = np.polynomial.chebyshev.Chebyshev.fit(s, function(np.sqrt(s)), degree, domain=[0, 0.25])
    return [float(c) for c in series.convert(kind=np.polynomial.Polynomial).coef]


SIN = fit(lambda r: math.sqrt(2) * np.sin(np.pi * r) / r, 3)
COS = fit(lambda r: math.sqrt(2) * np.cos(np.pi * r), 4)
WHOLE = 1.5 * 2.0**23


RESULT_ORDER = (
    (
        (0, 0, 1), (1, 2, 0), (0, 1, 0), (1, 3, 1),
        (0, 2, 1), (1, 0, 0), (0, 3, 0), (1, 1, 1),
        (0, 2, 0), (1, 0, 1), (0, 3, 1), (1, 1, 0),
        (0, 0, 0), (1, 2, 1), (0, 1, 1), (1, 3, 0),
    ),
    (
        (1, 3, 0), (0, 1, 1), (0, 2, 0), (1, 0, 1),
        (0, 0, 0), (1, 2, 1), (0, 3, 1), (1, 1, 0),
        (0, 2, 1), (1, 0, 0), (0, 1, 0), (1, 3, 1),
        (0, 0, 1), (1, 2, 0), (0, 3, 0), (1, 1, 1),
    ),
)
POINTS = [float(point) for point in cheb_points()]
SCALES = [
    float(1 / np.prod([cheb_points()[s] - cheb_points()[j] for j in range(CHEB) if j != s])) for s in range(CHEB)
]


def horner(coefficients, s):
    value = s * coefficients[-1] + coefficients[-2]
    for coefficient in coefficients[-3::-1]:
        value = value * s + coefficient
    return value


def unit(turns):
    r = turns - ((turns + WHOLE) - WHOLE)
    s = r * r
    half = horner(SIN, s) * r
    return 1.0 - half * half, half * horner(COS, s)


def operand(block):
    if block.shape[0] < PAD:
        block = jnp.concatenate([block, jnp.zeros((PAD - block.shape[0], block.shape[1]), jnp.float32)], axis=0)
    high = block.astype(jnp.bfloat16)
    low = (block - high.astype(jnp.float32)).astype(jnp.bfloat16)
    return jnp.concatenate([high, low, high, jnp.zeros((DEPTH - 3 * PAD, block.shape[1]), jnp.bfloat16)], axis=0)


def choose(index, values):
    result = jnp.full(index.shape, values[0], jnp.float32)
    for number, value in enumerate(values[1:], 1):
        result = jnp.where(index == number, value, result)
    return result


def digits(value, *sizes):
    out = []
    for size in sizes[::-1]:
        rest = jnp.floor((value + 0.5) * (1.0 / size))
        out.append(value - rest * size)
        value = rest
    return out[::-1]


def lagrange(at, source):
    product = choose(source, SCALES)
    for number, point in enumerate(POINTS):
        product = product * jnp.where(source == number, 1.0, at - point)
    return product


def mixing_tables(mix_ref, raw_ref):
    shape = (HALF, DEPTH)
    column = lax.broadcasted_iota(jnp.int32, shape, 1).astype(jnp.float32)
    copy, inside = digits(column, 4, PAD)
    row = lax.broadcasted_iota(jnp.int32, shape, 0).astype(jnp.float32)
    t1, t2 = digits(row, CHEB, CHEB)
    second = inside >= 40
    place = inside - jnp.where(second, 40.0, 0.0)
    used = jnp.logical_and(place < HALF, copy < 3)
    s1, s2 = digits(jnp.minimum(place, HALF - 1.0), CHEB, CHEB)
    at1, at2 = choose(t1, POINTS) * 0.5, choose(t2, POINTS) * 0.5
    weights1 = [jnp.where(used, lagrange(q - 0.5 + at1, s1), 0.0) for q in range(2)]
    weights2 = [lagrange(q - 0.5 + at2, s2) for q in range(2)]
    for q1 in range(2):
        for q2 in range(2):
            weights = weights1[q1] * weights2[q2]
            turns1, turns2 = 0.5 * (q1 + 0.5 + at1), 0.5 * (q2 + 0.5 + at2)
            plus, minus = unit(turns1 + turns2), unit(turns1 - turns2)
            for c1 in range(2):
                for c2 in range(2):
                    co, si = plus if c1 == c2 else minus
                    si = si if c1 else -si
                    real, imag = co * weights, si * weights
                    for part, values in enumerate((jnp.where(second, -imag, real), jnp.where(second, real, imag))):
                        high = values.astype(jnp.bfloat16).astype(jnp.float32)
                        values = jnp.where(copy < 2, high, values - high)
                        base = part * TERMS + q1 * ROWS + q2 * HALF
                        raw_ref[2 * c1 + c2, base : base + HALF, :] = values

    shape = (48, DEPTH)
    copy, inside = digits(lax.broadcasted_iota(jnp.int32, shape, 1).astype(jnp.float32), 4, PAD)

    def variants(i, carry):
        table, rows = lax.div(i, 6), pl.ds(pl.multiple_of(48 * lax.rem(i, 6), 16), 48)
        values = raw_ref[table, rows, :]
        dense = jnp.where(inside < HALF, values, pltpu.roll(values, DEPTH - 4, 1))
        dense = jnp.where(inside < ROWS, dense, 0.0)
        for variant, block in enumerate((dense, values, pltpu.roll(values, 4, 1))):
            mix_ref[4 * variant + table, rows, :] = block.astype(jnp.bfloat16)
        return carry

    lax.fori_loop(0, 24, variants, 0)


def reverse6(value):
    total = 0
    for bit in range(6):
        total = total + lax.rem(lax.div(value, 1 << bit), 2) * (1 << (5 - bit))
    return total


def kernel(
    coef_hbm, slow_hbm, out_ref,
    coef_ref, slow_ref, mix_ref, raw_ref, pieces_ref,
    sbuf, xin, s0, z1, zr, s2, obuf, orecv, vtab, e_tab, y_a, y_b, acc_a, acc_b,
    load, in_send, in_recv, sib_send, sib_recv, out_send, out_recv,
):
    bx, by = lax.axis_index("bx"), lax.axis_index("by")
    my_z, my_x = lax.div(bx, 4), lax.rem(bx, 4)
    my_y, core = lax.div(by, 2), lax.rem(by, 2)
    my_x0 = lax.rem(my_x, 2)
    chip = bx * 4 + my_y
    low1 = reverse6(chip) * 16

    chunks = [coef_ref.at[pl.ds(1536 * i, 1536)] for i in range(3)]
    loads = [pltpu.make_async_copy(coef_hbm.at[pl.ds(1536 * i, 1536)], chunks[i], load.at[i]) for i in range(3)]
    loads.append(pltpu.make_async_copy(slow_hbm, slow_ref, load.at[3]))
    for copy in loads:
        copy.start()

    barrier = pltpu.get_barrier_semaphore()
    across = [lax.rem(by + j, 8) for j in range(8)]

    def greet(i, carry):
        there = lax.rem(bx + i, 16)
        for j in range(8):

            @pl.when(i + j > 0)
            def _(j=j):
                pl.semaphore_signal(barrier, inc=1, device_id=(there, across[j]), device_id_type=MESH)

        return carry

    lax.fori_loop(0, 16, greet, 0)

    y_at = [lax.rem(my_y + 2 * core + v, 4) for v in range(4)]

    def targets_in(part):
        half = lax.div(part, 2)
        odd = lax.rem(my_x + 2 * half + 1, 4)
        even = lax.rem(my_x + 2 * lax.rem(half + my_x0, 2), 4)
        x_at = (odd + core * (even - odd), even + core * (odd - even))
        z_at = [lax.rem(my_z + lax.rem(part, 2) + 2 * far + 2 * core, 4) for far in range(2)]
        for inner in range(16):
            far = inner // 2 % 2
            yield z_at[far], x_at[inner % 2], y_at[(inner // 4 + inner % 2 + 2 * far) % 4]

    def gather_rows(z, x, y):
        ell = z * 16 + x * 4 + y
        for tile in range(9):
            sbuf[ell, 8 * tile : 8 * tile + 8, :] = coef_ref[pl.ds(tile * 512 + ell, 8, stride=64), :]

    def send_part(part, carry):
        half = lax.div(part, 2)
        for z, x, y in targets_in(part):
            to_bx, to_by = z * 4 + x, y * 2 + my_x0
            src, dst = sbuf.at[z * 16 + x * 4 + y], xin.at[half, core, my_z, my_y]
            here = jnp.logical_and(to_bx == bx, to_by == by)

            @pl.when(here)
            def _(src=src, dst=dst):
                pltpu.make_async_copy(src, dst, in_recv.at[part]).start()

            @pl.when(jnp.logical_not(here))
            def _(src=src, dst=dst, to_bx=to_bx, to_by=to_by):
                pltpu.make_async_remote_copy(
                    src_ref=src, dst_ref=dst, send_sem=in_send, recv_sem=in_recv.at[part],
                    device_id=(to_bx, to_by), device_id_type=MESH,
                ).start()

        @pl.when(part < 3)
        def _():
            for target in targets_in(part + 1):
                gather_rows(*target)

        return carry

    for copy in loads[:3]:
        copy.wait()
    for target in targets_in(jnp.int32(0)):
        gather_rows(*target)
    pl.semaphore_wait(barrier, 127)
    lax.fori_loop(0, 4, send_part, 0)

    loads[3].wait()
    for level in range(4):
        table = jnp.concatenate([slow_ref[level], jnp.zeros((96, LANES - 96), jnp.float32)], axis=1)
        for piece in range(3):
            rounded = table.astype(jnp.bfloat16)
            pieces_ref[level, :, piece * LANES : piece * LANES + LANES] = rounded
            table = table - rounded.astype(jnp.float32)
    lane = lax.broadcasted_iota(jnp.int32, (TERMS, LANES), 1).astype(jnp.float32)
    row = lax.broadcasted_iota(jnp.int32, (TERMS, LANES), 0).astype(jnp.float32)
    q1, q2, t1, t2 = digits(row, 2, 2, CHEB, CHEB)
    row_i, row_j = CHEB * q1 + t1, CHEB * q2 + t2
    left_rows = lane < 64

    def spread(level, a1):
        pick = jnp.where(row_i[:, 0:96] + (12 * a1).astype(jnp.float32) == lane[:, 0:96], 1.0, 0.0)
        found = jnp.dot(pick.astype(jnp.bfloat16), pieces_ref[level], preferred_element_type=jnp.float32)
        return found[:, 0:LANES] + found[:, LANES : 2 * LANES] + found[:, 2 * LANES :]

    def column(table, a2):
        picked = jnp.where(row_j + (12 * a2).astype(jnp.float32) == lane, table, 0.0)
        return jnp.broadcast_to(jnp.sum(picked, axis=1, keepdims=True), (TERMS, LANES))

    zero, one = jnp.int32(0), jnp.int32(1)
    vtab[0] = column(spread(0, zero), zero)

    def fill1(a1, carry):
        table = spread(1, a1)
        for a2 in range(2):
            vtab[1 + 2 * a1 + a2] = column(table, a2 * one)
        return carry

    lax.fori_loop(0, 2, fill1, 0)

    def fill23(half):
        def fill(z, carry):
            other = lax.rem(lax.div(z, 2) + lax.div(my_z, 2) + half, 2)
            a2 = lax.rem(lax.div(my_y, 2) + other, 2)
            box = 2 * a2 + core
            vtab[5 + 2 * z + a2] = column(spread(2, z), box)
            for x1 in range(2):
                table = spread(3, 2 * z + x1)
                vtab[13 + 4 * z + 2 * x1 + a2] = jnp.where(left_rows, column(table, 2 * box), column(table, 2 * box + 1))
            return carry

        lax.fori_loop(0, 4, fill, 0)

    fill23(0)

    lanes = lax.broadcasted_iota(jnp.int32, (8, LANES), 1)
    low2 = reverse6(lax.rem(lanes, 64)) * 16
    lane2 = lax.div(lanes, 64) * 8 + low2
    back = 127 - lanes
    back_half = lax.div(lanes, 64) * 64 + 63 - lax.rem(lanes, 64)

    def permute(block, index):
        rows = [
            jnp.take_along_axis(block[8 * i : 8 * i + 8], index, axis=1, mode="promise_in_bounds")
            for i in range(block.shape[0] // 8)
        ]
        return jnp.concatenate(rows, axis=0)

    def magnitude(level, r1, c1, r2, c2):
        width = 2.0 ** (level + 1)
        k = (lax.div(r1, 1 << level).astype(jnp.float32) + 0.5) * width - N / 2
        step = (c1 - 0.5) * width
        k0 = k - step
        k2 = (lax.div(r2, jnp.full(r2.shape, 1 << level, jnp.int32)).astype(jnp.float32) + 0.5) * width - N / 2
        step2 = (c2 - 0.5) * width
        k20 = k2 - step2
        above = step * (k + k0) + step2 * (k2 + k20)
        return above / (jnp.sqrt(k * k + k2 * k2) + jnp.sqrt(k0 * k0 + k20 * k20))

    def interpolate(y_ref, child, table, blocks):
        y_ref[child] = jnp.dot(
            mix_ref[table], operand(jnp.concatenate(blocks, axis=1)), preferred_element_type=jnp.float32
        )

    def tiles(body):
        def tile(i, carry):
            body(i, pl.ds(pl.multiple_of(8 * i, 8), 8), pl.ds(pl.multiple_of(8 * i + TERMS, 8), 8))
            return carry

        lax.fori_loop(0, TERMS // 8, tile, 0, unroll=True)

    def added(total, co, si, y_ref, child, at, at_im, side):
        cols = pl.ds(side * LANES, LANES)
        y_re, y_im = y_ref[child, at, cols], y_ref[child, at_im, cols]
        re, im = co * y_re - si * y_im, co * y_im + si * y_re
        return (re, im) if total is None else (total[0] + re, total[1] + im)

    def exponentials(entry, slots, sizes):
        def tile(i, carry):
            at = pl.ds(pl.multiple_of(8 * i, 8), 8)
            for j in range(4):
                co, si = unit(vtab[slots[j], at, :] * sizes[j])
                e_tab[entry, j, 0, at, :] = co
                e_tab[entry, j, 1, at, :] = si
            return carry

        lax.fori_loop(0, TERMS // 8, tile, 0, unroll=3)

    def combine_cores(y_ref, dst, entry):
        def body(i, at, at_im):
            totals = [None, None]
            for c1 in range(2):
                for c2 in range(2):
                    co, si = e_tab[entry, 2 * c1 + c2, 0, at, :], e_tab[entry, 2 * c1 + c2, 1, at, :]
                    totals[0] = added(totals[0], co, si, y_ref, 2 * c1 + c2, at, at_im, 0)
                    totals[1] = added(totals[1], co, si, y_ref, 2 * c1 + 1 - c2, at, at_im, 1)
            for side in range(2):
                put(dst[side], i, totals[side])

        tiles(body)

    def combine_mirrored(y_ref, dst, entry, index):
        def body(i, at, at_im):
            for side in range(2):
                totals = [None, None]
                for c1 in range(2):
                    co, si = e_tab[entry, 2 * c1 + side, 0, at, :], e_tab[entry, 2 * c1 + side, 1, at, :]
                    for c2 in range(2):
                        totals[c2] = added(totals[c2], co, si, y_ref, 2 * c1 + c2, at, at_im, side)
                put(dst[side], i, [totals[0][part] + permute(totals[1][part], index) for part in range(2)])

        tiles(body)

    def put(dst, i, total):
        rows = pl.ds(pl.multiple_of(8 * lax.rem(i, 9), 8), 8)
        for part in range(2):
            dst[2 * part + lax.div(i, 9), rows, :] = total[part]

    def window(src, q1, q2):
        rows = pl.ds(pl.multiple_of(32 * q2, 8), 40)
        return jnp.concatenate([src[q1, rows, :], src[2 + q1, rows, :]], axis=0)

    pairs = ((0, y_a, acc_a), (1, y_b, acc_b))

    def x_of(slot):
        odd = lax.rem(my_x + core, 2)
        dx = odd * (2 * slot + 1) + (1 - odd) * 2 * lax.rem(slot + core, 2)
        x = lax.rem(my_x - dx + 4, 4)
        return lax.div(x, 2), low1 + 4 * lax.div(x, 2) + 8 * core

    def box_of(box):
        other1 = 1 - lax.rem(box, 2)
        other2 = 1 - lax.rem(lax.rem(box, 2) + lax.div(box, 2), 2)
        return lax.rem(lax.div(my_z, 2) + other1, 2), lax.rem(lax.div(my_y, 2) + other2, 2)

    children = [(c1, c2) for c1 in range(2) for c2 in range(2)]

    def phases0(part, carry):
        z0 = lax.rem(my_z + part, 2)
        r1 = x_of(lax.div(part, 2))[1] + 2 * z0
        for y0 in range(2):
            sizes = [magnitude(0, r1 + c1, c1, lane2 + (c2 + 2 * y0), c2) for c1, c2 in children]
            exponentials(2 * part + y0, (0,) * 4, sizes)
        return carry

    def phases1(step, carry):
        a1, a2 = box_of(step)
        for slot in range(2):
            r1 = x_of(slot)[1]
            sizes = [magnitude(1, r1 + 2 * c1, c1, lane2 + 2 * c2, c2) for c1, c2 in children]
            exponentials(8 + 2 * step + slot, (1 + 2 * a1 + a2,) * 4, sizes)
        return carry

    def phases2(step, carry):
        a1, a2 = box_of(step)
        sizes = [
            magnitude(2, low1 + 4 * c1 + 8 * x0, c1, lane2, 0) for c1 in range(2) for x0 in (core, 1 - core)
        ]
        for z0 in range(2):
            exponentials(16 + 2 * step + z0, (5 + 2 * (2 * a1 + z0) + a2,) * 4, sizes)
        return carry

    def phases3(step, carry):
        a1, a2 = box_of(step)
        sizes = [magnitude(3, low1 + 8 * c1, c1, low2, 0) for c1 in range(2) for side in range(2)]
        for z0 in range(2):
            slot = 13 + 4 * (2 * a1 + z0) + a2
            exponentials(24 + 2 * step + z0, (slot, slot + 2, slot, slot + 2), sizes)
        return carry

    def level0(part, carry):
        pltpu.make_async_copy(xin.at[0, 0], xin.at[0, 0], in_recv.at[part]).wait()
        slot, z0 = lax.div(part, 2), lax.rem(my_z + part, 2)
        for y0, y_ref, _ in pairs:
            for c1, c2 in children:
                z = 2 * c1 + z0
                first = xin[slot, 0, z, 2 * c2 + y0]
                second = permute(xin[slot, 1, z, 2 * c2 + 1 - y0], back)
                interpolate(y_ref, 2 * c1 + c2, 2 * c1 + c2, [first, second])
        for y0, y_ref, _ in pairs:
            combine_cores(y_ref, (s0.at[slot, z0, y0, 0], s0.at[slot, z0, 1 - y0, 1]), 2 * part + y0)
        return carry

    def level1(half, slot):
        x1 = x_of(slot)[0]
        for i, y_ref, _ in pairs:
            a1, a2 = box_of(2 * half + i)
            for c1, c2 in children:
                blocks = [window(s0.at[slot, c1, c2, side], a1, a2) for side in range(2)]
                interpolate(y_ref, 2 * c1 + c2, 4 + 4 * a2 + 2 * c1 + c2, blocks)
        for i, y_ref, _ in pairs:
            box = 2 * half + i
            combine_cores(y_ref, (z1.at[box, x1, 0], z1.at[box, x1, 1]), 8 + 2 * box + slot)
            pltpu.make_async_remote_copy(
                src_ref=z1.at[box, x1, :, :, pl.ds(pl.multiple_of(32 * (1 - core), 8), 40), :],
                dst_ref=zr.at[box, x1],
                send_sem=sib_send.at[box],
                recv_sem=sib_recv.at[box],
                device_id=(bx, my_y * 2 + 1 - core),
                device_id_type=MESH,
            ).start()

    mixing_tables(mix_ref, raw_ref)
    for phases, boxes in ((phases0, 4), (phases1, 4), (phases2, 2), (phases3, 2)):
        lax.fori_loop(0, boxes, phases, 0)

    def first_slot(half, carry):
        level1(half, 0)
        return carry

    lax.fori_loop(0, 2, level0, 0)
    lax.fori_loop(0, 2, first_slot, 0)
    lax.fori_loop(2, 4, level0, 0)

    left = lax.broadcasted_iota(jnp.int32, (PAD, LANES), 1) < 64
    left_half = lax.broadcasted_iota(jnp.int32, (HALF, LANES), 1) < 64

    def level23(half, i):
        z0 = lax.rem(my_z + i, 2)
        jobs = [(2 * half + j, j, y_ref, acc_ref) for j, y_ref, acc_ref in pairs]
        for box, j, y_ref, _ in jobs:
            for c1, c2 in children:
                other = zr.at[box, c1, c2]
                blocks = [
                    window(z1.at[box, c1, c2], z0, core),
                    jnp.concatenate([other[z0], other[2 + z0]], axis=0),
                ]
                interpolate(y_ref, 2 * c1 + c2, 4 + 4 * core + 2 * c1 + c2, blocks)
        for box, j, y_ref, _ in jobs:
            combine_mirrored(y_ref, (s2.at[j, 0], s2.at[j, 1]), 16 + 2 * box + z0, back)
        for box, j, y_ref, _ in jobs:
            for c1 in range(2):
                src = s2.at[j, lax.rem(c1 + core, 2)]
                near, far = [], []
                for x1 in range(2):
                    first = window(src, x1, 0)
                    second = window(src, x1, 1)
                    second = jnp.concatenate([second[4:40], second[36:40], second[44:80], second[76:80]], axis=0)
                    near.append(jnp.where(left, first, pltpu.roll(second, 64, 1)))
                    far.append(jnp.where(left, permute(first, back), permute(second, back_half)))
                interpolate(y_ref, 2 * c1, 4 + 2 * c1, near)
                interpolate(y_ref, 2 * c1 + 1, 4 + 2 * c1 + 1, far)
        for box, j, y_ref, acc_ref in jobs:
            combine_mirrored(y_ref, (acc_ref.at[0], acc_ref.at[1]), 24 + 2 * box + z0, back_half)
            for x1 in range(2):
                for q1 in range(2):
                    for part in range(2):
                        upper = acc_ref[x1, 2 * part + q1, 0:HALF, :]
                        lower = acc_ref[x1, 2 * part + q1, HALF:ROWS, :]
                        rows = pl.ds(HALF * part, HALF)
                        obuf[box, i, 2 * x1 + q1, 0, rows, :] = jnp.where(left_half, upper, pltpu.roll(lower, 64, 1))
                        obuf[box, i, 2 * x1 + q1, 1, rows, :] = jnp.where(left_half, pltpu.roll(upper, 64, 1), lower)

    x_out = [lax.rem(my_x + k, 4) for k in range(4)]
    role = lax.rem(core + my_y, 2)

    def by_role(first, second):
        return first if first is second else first + role * (second - first)

    def send_out(half, i):
        boxes = [2 * half + side for side in range(2)]
        z0 = lax.rem(my_z + i, 2)
        places = [box_of(box) for box in boxes]
        places = [((2 * a1 + z0) * 4, 2 * (2 * a2 + core)) for a1, a2 in places]
        for (side0, x0, c0), (side1, x1, c1) in zip(*RESULT_ORDER):
            box = by_role(boxes[side0], boxes[side1])
            to_z, to_y = [by_role(*ends) for ends in zip(places[side0], places[side1])]
            x, c = by_role(x_out[x0], x_out[x1]), c0 if c0 == c1 else by_role(c0, c1)
            to_bx, to_by = to_z + x, to_y + c
            src, dst = obuf.at[box, i, x, c], orecv.at[chip]
            here = jnp.logical_and(to_bx == bx, to_by == by)

            @pl.when(here)
            def _(src=src, dst=dst):
                pltpu.make_async_copy(src, dst, out_recv.at[2 * half + i]).start()

            @pl.when(jnp.logical_not(here))
            def _(src=src, dst=dst, to_bx=to_bx, to_by=to_by):
                pltpu.make_async_remote_copy(
                    src_ref=src, dst_ref=dst, send_sem=out_send, recv_sem=out_recv.at[2 * half + i],
                    device_id=(to_bx, to_by), device_id_type=MESH,
                ).start()

    def two_boxes(half, carry):
        level1(half, 1)
        for box in range(2):
            pltpu.make_async_copy(zr.at[0], zr.at[0], sib_recv.at[2 * half + box]).wait()

        def both_z(i, carry):
            level23(half, i)
            send_out(half, i)
            return carry

        lax.fori_loop(0, 2, both_z, 0)

        @pl.when(half == 0)
        def _():
            fill23(1)
            for phases in (phases2, phases3):
                lax.fori_loop(2, 4, phases, 0)

        return carry

    lax.fori_loop(0, 2, two_boxes, 0)

    def settle(step, carry):
        pltpu.make_async_copy(zr.at[0], zr.at[0], sib_send.at[step]).wait()
        return carry

    lax.fori_loop(0, 4, settle, 0)
    for keeps, sem in ((my_x0 == core, in_send), (lax.rem(my_y, 2) == core, out_send)):

        @pl.when(keeps)
        def _(sem=sem):
            pltpu.make_async_copy(sbuf.at[pl.ds(0, 63)], sbuf.at[pl.ds(0, 63)], sem).wait()

        @pl.when(jnp.logical_not(keeps))
        def _(sem=sem):
            pltpu.make_async_copy(sbuf, sbuf, sem).wait()

    def arrive(step, carry):
        pltpu.make_async_copy(orecv.at[pl.ds(0, 16)], orecv.at[pl.ds(0, 16)], out_recv.at[step]).wait()

        def scatter_rows(i, carry):
            upper = lax.div(i, 8)
            z = 2 * upper + lax.rem(my_z + step, 2)
            other = lax.rem(lax.div(my_z, 2) + upper + lax.div(step, 2), 2)
            y = 2 * lax.rem(lax.div(my_y, 2) + other, 2) + lax.rem(i, 2)
            x = lax.rem(lax.div(i, 2), 4)
            ell = z * 16 + x * 4 + y
            for tile in range(9):
                out_ref[pl.ds(tile * 512 + ell, 8, stride=64), :] = orecv[ell, 8 * tile : 8 * tile + 8, :]
            return carry

        lax.fori_loop(0, 16, scatter_rows, 0, unroll=4)
        return carry

    lax.fori_loop(0, 4, arrive, 0)


def shards(coefficients, slowness):
    rows = jnp.transpose(coefficients, (0, 1, 3, 2, 4)).reshape(ROWS * 64, LANES)
    operands = (rows, pltpu.with_memory_space_constraint(slowness, pltpu.HBM))
    dense = (ROWS, LANES)
    scratch = [pltpu.VMEM(operands[i].shape, jnp.float32) for i in range(2)]
    scratch += [pltpu.VMEM((12, 2 * TERMS, DEPTH), jnp.bfloat16), pltpu.VMEM((4, 2 * TERMS, DEPTH), jnp.float32)]
    scratch += [pltpu.VMEM((4, 96, 3 * LANES), jnp.bfloat16)]
    scratch += [
        pltpu.VMEM(shape, jnp.float32)
        for shape in (
            (64,) + dense,
            (2, 2, 4, 4) + dense,
            (2, 2, 2, 2, 4) + dense,
            (4, 2, 2, 4) + dense,
            (4, 2, 2, 4, 40, LANES),
            (2, 2, 4) + dense,
            (4, 2, 4, 2) + dense,
            (64,) + dense,
            (29, TERMS, LANES),
            (32, 4, 2, TERMS, LANES),
            (4, 2 * TERMS, 2 * LANES),
            (4, 2 * TERMS, 2 * LANES),
            (2, 4) + dense,
            (2, 4) + dense,
        )
    ]
    scratch += [
        pltpu.SemaphoreType.DMA((4,)),
        pltpu.SemaphoreType.DMA,
        pltpu.SemaphoreType.DMA((4,)),
        pltpu.SemaphoreType.DMA((4,)),
        pltpu.SemaphoreType.DMA((4,)),
        pltpu.SemaphoreType.DMA,
        pltpu.SemaphoreType.DMA((4,)),
    ]
    out = pl.pallas_call(
        kernel,
        out_shape=jax.ShapeDtypeStruct((ROWS * 64, LANES), jnp.float32),
        in_specs=[pl.BlockSpec(memory_space=pl.ANY), pl.BlockSpec(memory_space=pltpu.HBM)],
        out_specs=pl.BlockSpec(memory_space=pltpu.VMEM),
        scratch_shapes=scratch,
        compiler_params=pltpu.CompilerParams(collective_id=0, has_side_effects=True, vmem_limit_bytes=50 << 20),
    )(*operands)
    return jnp.transpose(out.reshape(2, CHEB, CHEB, 64, LANES), (0, 1, 3, 2, 4))


def solution(mesh):
    placed = (P(None, None, "bx", None, "by"), P())
    return jax.shard_map(
        shards,
        mesh=mesh,
        in_specs=placed,
        out_specs=P(None, None, "bx", None, "by"),
        check_vma=False,
    )
```

```python
import math

import jax
import jax.numpy as jnp
import numpy as np
from jax import lax
from jax.experimental import pallas as pl
from jax.experimental.pallas import tpu as pltpu
from jax.sharding import PartitionSpec as P

N = 2048
CHEB = 6
HALF = CHEB * CHEB
ROWS = 2 * HALF
TERMS = 4 * HALF
PAD = 80
DEPTH = 256
LANES = 128
MESH = pl.DeviceIdType.MESH
PIECES = (pl.ds(0, 40), pl.ds(40, 32))


def cheb_points():
    return np.cos(np.pi * (2 * np.arange(CHEB) + 1) / (2 * CHEB))


def fit(function, degree):
    count = 200
    s = 0.125 * (1 + np.cos(np.pi * (2 * np.arange(count) + 1) / (2 * count)))
    series = np.polynomial.chebyshev.Chebyshev.fit(s, function(np.sqrt(s)), degree, domain=[0, 0.25])
    return [float(c) for c in series.convert(kind=np.polynomial.Polynomial).coef]


SIN = fit(lambda r: math.sqrt(2) * np.sin(np.pi * r) / r, 3)
COS = fit(lambda r: math.sqrt(2) * np.cos(np.pi * r), 4)
WHOLE = 1.5 * 2.0**23


POINTS = [float(point) for point in cheb_points()]
SCALES = [
    float(1 / np.prod([cheb_points()[s] - cheb_points()[j] for j in range(CHEB) if j != s])) for s in range(CHEB)
]


def horner(coefficients, s):
    value = s * coefficients[-1] + coefficients[-2]
    for coefficient in coefficients[-3::-1]:
        value = value * s + coefficient
    return value


def unit(turns):
    r = turns - ((turns + WHOLE) - WHOLE)
    s = r * r
    half = horner(SIN, s) * r
    return 1.0 - half * half, half * horner(COS, s)


def operand(block):
    if block.shape[0] < PAD:
        block = jnp.concatenate([block, jnp.zeros((PAD - block.shape[0], block.shape[1]), jnp.float32)], axis=0)
    high = block.astype(jnp.bfloat16)
    low = (block - high.astype(jnp.float32)).astype(jnp.bfloat16)
    return jnp.concatenate([high, low, high, jnp.zeros((DEPTH - 3 * PAD, block.shape[1]), jnp.bfloat16)], axis=0)


def choose(index, values):
    result = jnp.full(index.shape, values[0], jnp.float32)
    for number, value in enumerate(values[1:], 1):
        result = jnp.where(index == number, value, result)
    return result


def digits(value, *sizes):
    out = []
    for size in sizes[::-1]:
        rest = jnp.floor((value + 0.5) * (1.0 / size))
        out.append(value - rest * size)
        value = rest
    return out[::-1]


def lagrange(at, source):
    product = choose(source, SCALES)
    for number, point in enumerate(POINTS):
        product = product * jnp.where(source == number, 1.0, at - point)
    return product


def mixing_tables(mix_ref, raw_ref):
    shape = (HALF, DEPTH)
    column = lax.broadcasted_iota(jnp.int32, shape, 1).astype(jnp.float32)
    copy, inside = digits(column, 4, PAD)
    row = lax.broadcasted_iota(jnp.int32, shape, 0).astype(jnp.float32)
    t1, t2 = digits(row, CHEB, CHEB)
    second = inside >= 40
    place = inside - jnp.where(second, 40.0, 0.0)
    used = jnp.logical_and(place < HALF, copy < 3)
    s1, s2 = digits(jnp.minimum(place, HALF - 1.0), CHEB, CHEB)
    at1, at2 = choose(t1, POINTS) * 0.5, choose(t2, POINTS) * 0.5
    weights1 = [jnp.where(used, lagrange(q - 0.5 + at1, s1), 0.0) for q in range(2)]
    weights2 = [lagrange(q - 0.5 + at2, s2) for q in range(2)]
    for q1 in range(2):
        for q2 in range(2):
            weights = weights1[q1] * weights2[q2]
            turns1, turns2 = 0.5 * (q1 + 0.5 + at1), 0.5 * (q2 + 0.5 + at2)
            plus, minus = unit(turns1 + turns2), unit(turns1 - turns2)
            for c1 in range(2):
                for c2 in range(2):
                    co, si = plus if c1 == c2 else minus
                    si = si if c1 else -si
                    real, imag = co * weights, si * weights
                    for part, values in enumerate((jnp.where(second, -imag, real), jnp.where(second, real, imag))):
                        high = values.astype(jnp.bfloat16).astype(jnp.float32)
                        values = jnp.where(copy < 2, high, values - high)
                        base = part * TERMS + q1 * ROWS + q2 * HALF
                        raw_ref[2 * c1 + c2, base : base + HALF, :] = values

    shape = (48, DEPTH)
    copy, inside = digits(lax.broadcasted_iota(jnp.int32, shape, 1).astype(jnp.float32), 4, PAD)

    def variants(i, carry):
        table, rows = lax.div(i, 6), pl.ds(pl.multiple_of(48 * lax.rem(i, 6), 16), 48)
        values = raw_ref[table, rows, :]
        dense = jnp.where(inside < HALF, values, pltpu.roll(values, DEPTH - 4, 1))
        dense = jnp.where(inside < ROWS, dense, 0.0)
        for variant, block in enumerate((dense, values, pltpu.roll(values, 4, 1))):
            mix_ref[4 * variant + table, rows, :] = block.astype(jnp.bfloat16)
        return carry

    lax.fori_loop(0, 24, variants, 0)


def reverse6(value):
    total = 0
    for bit in range(6):
        total = total + lax.rem(lax.div(value, 1 << bit), 2) * (1 << (5 - bit))
    return total


def kernel(
    coef_hbm, slow_hbm, out_ref,
    coef_ref, slow_ref, mix_ref, raw_ref, pieces_ref,
    sbuf, xin, s0, z1, zr, s2, obuf, orecv, vtab, e_tab, y_a, y_b, acc_a, acc_b,
    load, in_send, in_recv, sib_send, sib_recv, out_send, out_recv,
):
    bx, by = lax.axis_index("bx"), lax.axis_index("by")
    my_z, my_x = lax.div(bx, 4), lax.rem(bx, 4)
    my_y, core = lax.div(by, 2), lax.rem(by, 2)
    my_x0 = lax.rem(my_x, 2)
    chip = bx * 4 + my_y
    low1 = reverse6(chip) * 16

    chunks = [coef_ref.at[pl.ds(1536 * i, 1536)] for i in range(3)]
    loads = [pltpu.make_async_copy(coef_hbm.at[pl.ds(1536 * i, 1536)], chunks[i], load.at[i]) for i in range(3)]
    loads.append(pltpu.make_async_copy(slow_hbm, slow_ref, load.at[3]))
    for copy in loads:
        copy.start()

    barrier = pltpu.get_barrier_semaphore()
    across = [lax.rem(by + j, 8) for j in range(8)]

    def greet(i, carry):
        there = lax.rem(bx + i, 16)
        for j in range(8):

            @pl.when(i + j > 0)
            def _(j=j):
                pl.semaphore_signal(barrier, inc=1, device_id=(there, across[j]), device_id_type=MESH)

        return carry

    lax.fori_loop(0, 16, greet, 0)

    y_at = [lax.rem(my_y + 2 * core + v, 4) for v in range(4)]

    def targets_in(part):
        half = lax.div(part, 2)
        odd = lax.rem(my_x + 2 * half + 1, 4)
        even = lax.rem(my_x + 2 * lax.rem(half + my_x0, 2), 4)
        x_at = (odd + core * (even - odd), even + core * (odd - even))
        z_at = [lax.rem(my_z + lax.rem(part, 2) + 2 * far + 2 * core, 4) for far in range(2)]
        for inner in range(16):
            far = inner // 2 % 2
            yield z_at[far], x_at[inner % 2], y_at[(inner // 4 + inner % 2 + 2 * far) % 4]

    def gather_rows(z, x, y):
        ell = z * 16 + x * 4 + y
        for tile in range(9):
            sbuf[ell, 8 * tile : 8 * tile + 8, :] = coef_ref[pl.ds(tile * 512 + ell, 8, stride=64), :]

    def send_part(part, carry):
        half = lax.div(part, 2)
        for z, x, y in targets_in(part):
            to_bx, to_by = z * 4 + x, y * 2 + my_x0
            src, dst = sbuf.at[z * 16 + x * 4 + y], xin.at[half, core, my_z, my_y]
            here = jnp.logical_and(to_bx == bx, to_by == by)

            @pl.when(here)
            def _(src=src, dst=dst):
                pltpu.make_async_copy(src, dst, in_recv.at[part]).start()

            @pl.when(jnp.logical_not(here))
            def _(src=src, dst=dst, to_bx=to_bx, to_by=to_by):
                for rows in PIECES:
                    pltpu.make_async_remote_copy(
                        src_ref=src.at[rows], dst_ref=dst.at[rows], send_sem=in_send, recv_sem=in_recv.at[part],
                        device_id=(to_bx, to_by), device_id_type=MESH,
                    ).start()

        @pl.when(part < 3)
        def _():
            for target in targets_in(part + 1):
                gather_rows(*target)

        return carry

    for copy in loads[:3]:
        copy.wait()
    for target in targets_in(jnp.int32(0)):
        gather_rows(*target)
    pl.semaphore_wait(barrier, 127)
    lax.fori_loop(0, 4, send_part, 0)

    loads[3].wait()
    for level in range(4):
        table = jnp.concatenate([slow_ref[level], jnp.zeros((96, LANES - 96), jnp.float32)], axis=1)
        for piece in range(3):
            rounded = table.astype(jnp.bfloat16)
            pieces_ref[level, :, piece * LANES : piece * LANES + LANES] = rounded
            table = table - rounded.astype(jnp.float32)
    lane = lax.broadcasted_iota(jnp.int32, (TERMS, LANES), 1).astype(jnp.float32)
    row = lax.broadcasted_iota(jnp.int32, (TERMS, LANES), 0).astype(jnp.float32)
    q1, q2, t1, t2 = digits(row, 2, 2, CHEB, CHEB)
    row_i, row_j = CHEB * q1 + t1, CHEB * q2 + t2
    left_rows = lane < 64

    def spread(level, a1):
        pick = jnp.where(row_i[:, 0:96] + (12 * a1).astype(jnp.float32) == lane[:, 0:96], 1.0, 0.0)
        found = jnp.dot(pick.astype(jnp.bfloat16), pieces_ref[level], preferred_element_type=jnp.float32)
        return found[:, 0:LANES] + found[:, LANES : 2 * LANES] + found[:, 2 * LANES :]

    def column(table, a2):
        picked = jnp.where(row_j + (12 * a2).astype(jnp.float32) == lane, table, 0.0)
        return jnp.broadcast_to(jnp.sum(picked, axis=1, keepdims=True), (TERMS, LANES))

    zero, one = jnp.int32(0), jnp.int32(1)
    vtab[0] = column(spread(0, zero), zero)

    def fill1(a1, carry):
        table = spread(1, a1)
        for a2 in range(2):
            vtab[1 + 2 * a1 + a2] = column(table, a2 * one)
        return carry

    lax.fori_loop(0, 2, fill1, 0)

    def fill23(half):
        def fill(z, carry):
            other = lax.rem(lax.div(z, 2) + lax.div(my_z, 2) + half, 2)
            a2 = lax.rem(lax.div(my_y, 2) + other, 2)
            box = 2 * a2 + core
            vtab[5 + 2 * z + a2] = column(spread(2, z), box)
            for x1 in range(2):
                table = spread(3, 2 * z + x1)
                vtab[13 + 4 * z + 2 * x1 + a2] = jnp.where(left_rows, column(table, 2 * box), column(table, 2 * box + 1))
            return carry

        lax.fori_loop(0, 4, fill, 0)

    fill23(0)

    lanes = lax.broadcasted_iota(jnp.int32, (8, LANES), 1)
    low2 = reverse6(lax.rem(lanes, 64)) * 16
    lane2 = lax.div(lanes, 64) * 8 + low2
    back = 127 - lanes
    back_half = lax.div(lanes, 64) * 64 + 63 - lax.rem(lanes, 64)

    def permute(block, index):
        rows = [
            jnp.take_along_axis(block[8 * i : 8 * i + 8], index, axis=1, mode="promise_in_bounds")
            for i in range(block.shape[0] // 8)
        ]
        return jnp.concatenate(rows, axis=0)

    def magnitude(level, r1, c1, r2, c2):
        width = 2.0 ** (level + 1)
        k = (lax.div(r1, 1 << level).astype(jnp.float32) + 0.5) * width - N / 2
        step = (c1 - 0.5) * width
        k0 = k - step
        k2 = (lax.div(r2, jnp.full(r2.shape, 1 << level, jnp.int32)).astype(jnp.float32) + 0.5) * width - N / 2
        step2 = (c2 - 0.5) * width
        k20 = k2 - step2
        above = step * (k + k0) + step2 * (k2 + k20)
        return above / (jnp.sqrt(k * k + k2 * k2) + jnp.sqrt(k0 * k0 + k20 * k20))

    def interpolate(y_ref, child, table, blocks):
        y_ref[child] = jnp.dot(
            mix_ref[table], operand(jnp.concatenate(blocks, axis=1)), preferred_element_type=jnp.float32
        )

    def tiles(body):
        def tile(i, carry):
            body(i, pl.ds(pl.multiple_of(8 * i, 8), 8), pl.ds(pl.multiple_of(8 * i + TERMS, 8), 8))
            return carry

        lax.fori_loop(0, TERMS // 8, tile, 0, unroll=True)

    def added(total, co, si, y_ref, child, at, at_im, side):
        cols = pl.ds(side * LANES, LANES)
        y_re, y_im = y_ref[child, at, cols], y_ref[child, at_im, cols]
        re, im = co * y_re - si * y_im, co * y_im + si * y_re
        return (re, im) if total is None else (total[0] + re, total[1] + im)

    def exponentials(entry, slots, sizes):
        def tile(i, carry):
            at = pl.ds(pl.multiple_of(8 * i, 8), 8)
            for j in range(4):
                co, si = unit(vtab[slots[j], at, :] * sizes[j])
                e_tab[entry, j, 0, at, :] = co
                e_tab[entry, j, 1, at, :] = si
            return carry

        lax.fori_loop(0, TERMS // 8, tile, 0, unroll=3)

    def combine_cores(y_ref, dst, entry):
        def body(i, at, at_im):
            totals = [None, None]
            for c1 in range(2):
                for c2 in range(2):
                    co, si = e_tab[entry, 2 * c1 + c2, 0, at, :], e_tab[entry, 2 * c1 + c2, 1, at, :]
                    totals[0] = added(totals[0], co, si, y_ref, 2 * c1 + c2, at, at_im, 0)
                    totals[1] = added(totals[1], co, si, y_ref, 2 * c1 + 1 - c2, at, at_im, 1)
            for side in range(2):
                put(dst[side], i, totals[side])

        tiles(body)

    def combine_mirrored(y_ref, dst, entry, index):
        def body(i, at, at_im):
            for side in range(2):
                totals = [None, None]
                for c1 in range(2):
                    co, si = e_tab[entry, 2 * c1 + side, 0, at, :], e_tab[entry, 2 * c1 + side, 1, at, :]
                    for c2 in range(2):
                        totals[c2] = added(totals[c2], co, si, y_ref, 2 * c1 + c2, at, at_im, side)
                put(dst[side], i, [totals[0][part] + permute(totals[1][part], index) for part in range(2)])

        tiles(body)

    def put(dst, i, total):
        rows = pl.ds(pl.multiple_of(8 * lax.rem(i, 9), 8), 8)
        for part in range(2):
            dst[2 * part + lax.div(i, 9), rows, :] = total[part]

    def window(src, q1, q2):
        rows = pl.ds(pl.multiple_of(32 * q2, 8), 40)
        return jnp.concatenate([src[q1, rows, :], src[2 + q1, rows, :]], axis=0)

    pairs = ((0, y_a, acc_a), (1, y_b, acc_b))

    def x_of(slot):
        odd = lax.rem(my_x + core, 2)
        dx = odd * (2 * slot + 1) + (1 - odd) * 2 * lax.rem(slot + core, 2)
        x = lax.rem(my_x - dx + 4, 4)
        return lax.div(x, 2), low1 + 4 * lax.div(x, 2) + 8 * core

    def box_of(box):
        other1 = 1 - lax.rem(box, 2)
        other2 = 1 - lax.rem(lax.rem(box, 2) + lax.div(box, 2), 2)
        return lax.rem(lax.div(my_z, 2) + other1, 2), lax.rem(lax.div(my_y, 2) + other2, 2)

    children = [(c1, c2) for c1 in range(2) for c2 in range(2)]

    def phases0(part, carry):
        z0 = lax.rem(my_z + part, 2)
        r1 = x_of(lax.div(part, 2))[1] + 2 * z0
        for y0 in range(2):
            sizes = [magnitude(0, r1 + c1, c1, lane2 + (c2 + 2 * y0), c2) for c1, c2 in children]
            exponentials(2 * part + y0, (0,) * 4, sizes)
        return carry

    def phases1(step, carry):
        a1, a2 = box_of(step)
        for slot in range(2):
            r1 = x_of(slot)[1]
            sizes = [magnitude(1, r1 + 2 * c1, c1, lane2 + 2 * c2, c2) for c1, c2 in children]
            exponentials(8 + 2 * step + slot, (1 + 2 * a1 + a2,) * 4, sizes)
        return carry

    def phases2(step, carry):
        a1, a2 = box_of(step)
        sizes = [
            magnitude(2, low1 + 4 * c1 + 8 * x0, c1, lane2, 0) for c1 in range(2) for x0 in (core, 1 - core)
        ]
        for z0 in range(2):
            exponentials(16 + 2 * step + z0, (5 + 2 * (2 * a1 + z0) + a2,) * 4, sizes)
        return carry

    def phases3(step, carry):
        a1, a2 = box_of(step)
        sizes = [magnitude(3, low1 + 8 * c1, c1, low2, 0) for c1 in range(2) for side in range(2)]
        for z0 in range(2):
            slot = 13 + 4 * (2 * a1 + z0) + a2
            exponentials(24 + 2 * step + z0, (slot, slot + 2, slot, slot + 2), sizes)
        return carry

    def level0(part, carry):
        pltpu.make_async_copy(xin.at[0, 0], xin.at[0, 0], in_recv.at[part]).wait()
        slot, z0 = lax.div(part, 2), lax.rem(my_z + part, 2)
        for y0, y_ref, _ in pairs:
            for c1, c2 in children:
                z = 2 * c1 + z0
                first = xin[slot, 0, z, 2 * c2 + y0]
                second = permute(xin[slot, 1, z, 2 * c2 + 1 - y0], back)
                interpolate(y_ref, 2 * c1 + c2, 2 * c1 + c2, [first, second])
        for y0, y_ref, _ in pairs:
            combine_cores(y_ref, (s0.at[slot, z0, y0, 0], s0.at[slot, z0, 1 - y0, 1]), 2 * part + y0)
        return carry

    def level1(half, slot):
        x1 = x_of(slot)[0]
        for i, y_ref, _ in pairs:
            a1, a2 = box_of(2 * half + i)
            for c1, c2 in children:
                blocks = [window(s0.at[slot, c1, c2, side], a1, a2) for side in range(2)]
                interpolate(y_ref, 2 * c1 + c2, 4 + 4 * a2 + 2 * c1 + c2, blocks)
        for i, y_ref, _ in pairs:
            box = 2 * half + i
            combine_cores(y_ref, (z1.at[box, x1, 0], z1.at[box, x1, 1]), 8 + 2 * box + slot)
            pltpu.make_async_remote_copy(
                src_ref=z1.at[box, x1, :, :, pl.ds(pl.multiple_of(32 * (1 - core), 8), 40), :],
                dst_ref=zr.at[box, x1],
                send_sem=sib_send.at[box],
                recv_sem=sib_recv.at[box],
                device_id=(bx, my_y * 2 + 1 - core),
                device_id_type=MESH,
            ).start()

    mixing_tables(mix_ref, raw_ref)
    for phases, boxes in ((phases0, 4), (phases1, 4), (phases2, 2), (phases3, 2)):
        lax.fori_loop(0, boxes, phases, 0)

    def first_slot(half, carry):
        level1(half, 0)
        return carry

    lax.fori_loop(0, 2, level0, 0)
    lax.fori_loop(0, 2, first_slot, 0)
    lax.fori_loop(2, 4, level0, 0)

    left = lax.broadcasted_iota(jnp.int32, (PAD, LANES), 1) < 64
    left_half = lax.broadcasted_iota(jnp.int32, (HALF, LANES), 1) < 64

    def level23(half, i):
        z0 = lax.rem(my_z + i, 2)
        jobs = [(2 * half + j, j, y_ref, acc_ref) for j, y_ref, acc_ref in pairs]
        for box, j, y_ref, _ in jobs:
            for c1, c2 in children:
                other = zr.at[box, c1, c2]
                blocks = [
                    window(z1.at[box, c1, c2], z0, core),
                    jnp.concatenate([other[z0], other[2 + z0]], axis=0),
                ]
                interpolate(y_ref, 2 * c1 + c2, 4 + 4 * core + 2 * c1 + c2, blocks)
        for box, j, y_ref, _ in jobs:
            combine_mirrored(y_ref, (s2.at[j, 0], s2.at[j, 1]), 16 + 2 * box + z0, back)
        for box, j, y_ref, _ in jobs:
            for c1 in range(2):
                src = s2.at[j, lax.rem(c1 + core, 2)]
                near, far = [], []
                for x1 in range(2):
                    first = window(src, x1, 0)
                    second = window(src, x1, 1)
                    second = jnp.concatenate([second[4:40], second[36:40], second[44:80], second[76:80]], axis=0)
                    near.append(jnp.where(left, first, pltpu.roll(second, 64, 1)))
                    far.append(jnp.where(left, permute(first, back), permute(second, back_half)))
                interpolate(y_ref, 2 * c1, 4 + 2 * c1, near)
                interpolate(y_ref, 2 * c1 + 1, 4 + 2 * c1 + 1, far)
        for box, j, y_ref, acc_ref in jobs:
            combine_mirrored(y_ref, (acc_ref.at[0], acc_ref.at[1]), 24 + 2 * box + z0, back_half)
            for x1 in range(2):
                for q1 in range(2):
                    for part in range(2):
                        upper = acc_ref[x1, 2 * part + q1, 0:HALF, :]
                        lower = acc_ref[x1, 2 * part + q1, HALF:ROWS, :]
                        rows = pl.ds(HALF * part, HALF)
                        obuf[box, i, 2 * x1 + q1, 0, rows, :] = jnp.where(left_half, upper, pltpu.roll(lower, 64, 1))
                        obuf[box, i, 2 * x1 + q1, 1, rows, :] = jnp.where(left_half, pltpu.roll(upper, 64, 1), lower)

    x_out = [lax.rem(my_x + 1 + 2 * core + k, 4) for k in range(4)]

    def send_out(half, i):
        boxes = [2 * half + core, 2 * half + 1 - core]
        z0 = lax.rem(my_z + i, 2)
        places = [box_of(box) for box in boxes]
        places = [((2 * a1 + z0) * 4, 2 * (2 * a2 + core)) for a1, a2 in places]
        for number in range(16):
            turn, round_ = number % 2, number // 2
            x, c = x_out[(round_ + 2 * turn) % 4], (round_ + round_ // 4 + turn) % 2
            to_bx, to_by = places[turn][0] + x, places[turn][1] + c
            src, dst = obuf.at[boxes[turn], i, x, c], orecv.at[chip]
            here = jnp.logical_and(to_bx == bx, to_by == by)

            @pl.when(here)
            def _(src=src, dst=dst):
                pltpu.make_async_copy(src, dst, out_recv.at[2 * half + i]).start()

            @pl.when(jnp.logical_not(here))
            def _(src=src, dst=dst, to_bx=to_bx, to_by=to_by):
                for rows in PIECES:
                    pltpu.make_async_remote_copy(
                        src_ref=src.at[rows], dst_ref=dst.at[rows], send_sem=out_send, recv_sem=out_recv.at[2 * half + i],
                        device_id=(to_bx, to_by), device_id_type=MESH,
                    ).start()

    def two_boxes(half, carry):
        level1(half, 1)
        for box in range(2):
            pltpu.make_async_copy(zr.at[0], zr.at[0], sib_recv.at[2 * half + box]).wait()

        def both_z(i, carry):
            level23(half, i)
            send_out(half, i)
            return carry

        lax.fori_loop(0, 2, both_z, 0)

        @pl.when(half == 0)
        def _():
            fill23(1)
            for phases in (phases2, phases3):
                lax.fori_loop(2, 4, phases, 0)

        return carry

    lax.fori_loop(0, 2, two_boxes, 0)

    def settle(step, carry):
        pltpu.make_async_copy(zr.at[0], zr.at[0], sib_send.at[step]).wait()
        return carry

    lax.fori_loop(0, 4, settle, 0)
    for keeps, sem in ((my_x0 == core, in_send), (lax.rem(my_y, 2) == core, out_send)):

        @pl.when(keeps)
        def _(sem=sem):
            pltpu.make_async_copy(sbuf.at[pl.ds(0, 63)], sbuf.at[pl.ds(0, 63)], sem).wait()

        @pl.when(jnp.logical_not(keeps))
        def _(sem=sem):
            pltpu.make_async_copy(sbuf, sbuf, sem).wait()

    def arrive(step, carry):
        pltpu.make_async_copy(orecv.at[pl.ds(0, 16)], orecv.at[pl.ds(0, 16)], out_recv.at[step]).wait()

        def scatter_rows(i, carry):
            upper = lax.div(i, 8)
            z = 2 * upper + lax.rem(my_z + step, 2)
            other = lax.rem(lax.div(my_z, 2) + upper + lax.div(step, 2), 2)
            y = 2 * lax.rem(lax.div(my_y, 2) + other, 2) + lax.rem(i, 2)
            x = lax.rem(lax.div(i, 2), 4)
            ell = z * 16 + x * 4 + y
            for tile in range(9):
                out_ref[pl.ds(tile * 512 + ell, 8, stride=64), :] = orecv[ell, 8 * tile : 8 * tile + 8, :]
            return carry

        lax.fori_loop(0, 16, scatter_rows, 0, unroll=4)
        return carry

    lax.fori_loop(0, 4, arrive, 0)


def shards(coefficients, slowness):
    rows = jnp.transpose(coefficients, (0, 1, 3, 2, 4)).reshape(ROWS * 64, LANES)
    operands = (rows, pltpu.with_memory_space_constraint(slowness, pltpu.HBM))
    dense = (ROWS, LANES)
    scratch = [pltpu.VMEM(operands[i].shape, jnp.float32) for i in range(2)]
    scratch += [pltpu.VMEM((12, 2 * TERMS, DEPTH), jnp.bfloat16), pltpu.VMEM((4, 2 * TERMS, DEPTH), jnp.float32)]
    scratch += [pltpu.VMEM((4, 96, 3 * LANES), jnp.bfloat16)]
    scratch += [
        pltpu.VMEM(shape, jnp.float32)
        for shape in (
            (64,) + dense,
            (2, 2, 4, 4) + dense,
            (2, 2, 2, 2, 4) + dense,
            (4, 2, 2, 4) + dense,
            (4, 2, 2, 4, 40, LANES),
            (2, 2, 4) + dense,
            (4, 2, 4, 2) + dense,
            (64,) + dense,
            (29, TERMS, LANES),
            (32, 4, 2, TERMS, LANES),
            (4, 2 * TERMS, 2 * LANES),
            (4, 2 * TERMS, 2 * LANES),
            (2, 4) + dense,
            (2, 4) + dense,
        )
    ]
    scratch += [
        pltpu.SemaphoreType.DMA((4,)),
        pltpu.SemaphoreType.DMA,
        pltpu.SemaphoreType.DMA((4,)),
        pltpu.SemaphoreType.DMA((4,)),
        pltpu.SemaphoreType.DMA((4,)),
        pltpu.SemaphoreType.DMA,
        pltpu.SemaphoreType.DMA((4,)),
    ]
    out = pl.pallas_call(
        kernel,
        out_shape=jax.ShapeDtypeStruct((ROWS * 64, LANES), jnp.float32),
        in_specs=[pl.BlockSpec(memory_space=pl.ANY), pl.BlockSpec(memory_space=pltpu.HBM)],
        out_specs=pl.BlockSpec(memory_space=pltpu.VMEM),
        scratch_shapes=scratch,
        compiler_params=pltpu.CompilerParams(collective_id=0, has_side_effects=True, vmem_limit_bytes=50 << 20),
    )(*operands)
    return jnp.transpose(out.reshape(2, CHEB, CHEB, 64, LANES), (0, 1, 3, 2, 4))


def solution(mesh):
    placed = (P(None, None, "bx", None, "by"), P())
    return jax.shard_map(
        shards,
        mesh=mesh,
        in_specs=placed,
        out_specs=P(None, None, "bx", None, "by"),
        check_vma=False,
    )
```
